32 devices in a mesh: tile: 16 (over z, y, core), head: 2 (over x).
Axes of the slice: x: 2, y: 2, z: 4, core: 2. Of those that a mesh axis runs over, the one named last changes fastest.
Arguments:
- vision_rows: bfloat16 [512, 8, 768], P(('tile', 'head')), may hold values from -6 to 6
- positions: int32 [3, 512], P(None, ('tile', 'head')), may hold values from 0 to 63
- destination: int32 [512, 1], replicated, may hold values from 0 to 15; in each aligned block of 16 rows (0 to 15, 16 to 31, ...) at most 2 rows name the same one
- out_grad: bfloat16 [1024, 8, 512], P(('tile', 'head')), may hold values from -6 to 6
Outputs:
- row_grads: bfloat16 [512, 8, 768], P(('tile', 'head'))
The draws below stay inside these ranges and needn't reach their ends.
Inputs may be any that keep to these rules, and one draw needn't show every extreme that they name: `destination`: among the 16 tokens of one device (aligned blocks of rows) no tile is named more than 2 times, and some block names a tile exactly 2 times.
All inputs are finite; a program needn't handle non-finite values.
Results may differ from the reference program's by a relative error of at most 0.01.
Values may be sent and summed in bfloat16 or wider, within the bound.
No kernel may reach another device: no remote copies, remote signals or barrier semaphores. Data moves between devices by JAX's collectives and lax.ppermute only.
A program may use at most 64 MiB of HBM per device.

```python
import math
import jax
import jax.numpy as jnp
import numpy as np
from jax import lax

KV = 8
HD = 128
C = 2
QPK = 4
G = 768
VIS_DEV = 16
VIS_ROWS = 512
SLOT_DEV = 32
SEQ = 64
SLOTS = 1024
N_TILE = 16
N_HEAD = 2


def draw_vision_rows(key, part):
    key = jax.random.fold_in(key, 11)
    keys = jax.random.split(key, 1)
    shape = (VIS_ROWS, KV, G)
    return jnp.clip(jax.random.normal(keys[0], shape, jnp.float32), -6.0, 6.0).astype(jnp.bfloat16)


def with_ends(values, key, smallest, high):
    index_at = [jax.random.randint(jax.random.fold_in(key, axis), (), 0, length) for axis, length in enumerate(values.shape)]
    main_axis = values.shape.index(max(values.shape))
    next_to = index_at[:main_axis] + [(index_at[main_axis] + 1) % values.shape[main_axis]] + index_at[main_axis + 1:]
    return values.at[tuple(index_at)].set(smallest).at[tuple(next_to)].set(high)


def shard_levels(stream_key, shape, cuts, least, high):
    def one(position, parts):
        draws = jax.random.uniform(jax.random.fold_in(jax.random.fold_in(stream_key, 6), position), (parts,), jnp.float32, least / len(cuts), high / len(cuts))
        return jnp.repeat(jnp.exp(draws), shape[position] // parts).reshape((-1,) + (1,) * (len(shape) - position - 1))

    gain = one(*cuts[0])
    for cut in cuts[1:]:
        gain = gain * one(*cut)
    return gain


def assign_block(key, own, number, rows, number_of, top, reach, slope):
    order = jax.random.permutation(key, number_of)
    packed, ordinary = shares(number_of, rows * top, reach, slope, True), shares(number_of, rows * top, reach, slope, False)
    places = jnp.arange(number_of)

    def named(tallies, turn):
        used = int((tallies > 0).sum())
        fixed = max(1, used // 4)
        shifted = fixed + (places - fixed + turn * (used - fixed)) % max(1, number_of - fixed)
        return jnp.zeros((number_of,), jnp.int32).at[order[jnp.where(places < fixed, places, shifted)]].set(jnp.asarray(tallies, jnp.int32))

    tallies = jnp.where(number % 4 == 0, named(packed, number // 4), named(ordinary, number - number // 4 - 1))
    mixed = jax.random.permutation(jax.random.fold_in(own, 3), number_of)
    donor, sink = mixed[0:number_of // 2 * 2:2], mixed[1:number_of // 2 * 2:2]
    room = jnp.minimum(tallies[donor] - 1, reach - tallies[sink]) // 2
    room = jnp.where((donor == order[0]) | (sink == order[0]) | (tallies[sink] == 0), 0, jnp.maximum(room, 0))
    shifted = jax.random.randint(jax.random.fold_in(own, 4), (number_of // 2,), 0, 1 << 20) % (room + 1)
    tallies = tallies.at[donor].add(-shifted).at[sink].add(shifted)
    labels = jnp.searchsorted(jnp.cumsum(tallies), jnp.arange(rows * top), side="right").astype(jnp.int32)
    listing = labels.reshape(top, rows).T
    listing = listing[jax.random.permutation(jax.random.fold_in(own, 1), rows)]
    turn = jax.random.randint(jax.random.fold_in(own, 2), (rows, 1), 0, top)
    return jnp.take_along_axis(listing, (jnp.arange(top)[None, :] + turn) % top, axis=1)


def shares(count, total, bound, slope, full):
    portions = [(1 << 20) // math.isqrt(standing ** slope) + 1 for standing in range(1, count + 1)]
    largest = bound if full else min(bound, max(-(-total // count), total * portions[0] // sum(portions)))
    least = 1 if total - largest >= count - 1 else 0
    given, spare = [largest] + [least] * (count - 1), total - largest - least * (count - 1)
    while spare > 0:
        candidates = [i for i in range(1, count) if given[i] < largest] or [i for i in range(1, count) if given[i] < bound]
        mass, left = sum([portions[i] for i in candidates]), spare
        for i in candidates:
            more = min(bound - given[i], max(1, left * portions[i] // mass), spare)
            given[i] = given[i] + more
            spare = spare - more
    return np.array(given)


def scatter_about(key, extent, width, most, pieces=(), kind=jnp.bfloat16):
    array = jax.random.normal(key, extent, jnp.float32) * width
    if len(pieces) > 0:
        array = shard_levels(key, extent, pieces, -0.22, 0.18) * array
    return jnp.clip(array, min=-most, max=most).astype(kind)


def setup_inputs(seed: int = 0) -> dict:
    key_list = jax.random.split(jax.random.key(seed), 5)
    vision_rows = draw_vision_rows(jax.random.fold_in(key_list[4], 71), 0)
    positions = with_ends(jax.random.randint(key_list[1], (3, VIS_ROWS), 0, 64), jax.random.fold_in(key_list[1], 1), 0, 63).astype(jnp.int32)
    destination_keys = jax.random.split(jax.random.fold_in(key_list[2], 1), VIS_ROWS // VIS_DEV)
    destination_turns = jax.random.permutation(jax.random.fold_in(key_list[2], 3), VIS_ROWS // VIS_DEV)
    destination = jax.vmap(lambda own, number: assign_block(jax.random.fold_in(key_list[2], 2), own, number, VIS_DEV, N_TILE, 1, C, 2))(destination_keys, destination_turns).reshape((VIS_ROWS, 1))
    out_grad = scatter_about(key_list[3], (SLOTS, KV, QPK * HD), 1.0, 6.0, ((0, 32),))
    return {"vision_rows": vision_rows, "positions": positions, "destination": destination, "out_grad": out_grad}


def rope_parts(positions):
    half = HD // 2
    slots = jnp.arange(half, dtype=jnp.int32)
    first = half // 4
    second = (half - first) // 2
    section = jnp.where(slots < first, 0, jnp.where(slots < first + second, 1, 2))
    picks = (section[:, None] == jnp.arange(3, dtype=jnp.int32)[None, :]).astype(jnp.float32)
    chosen = jnp.dot(picks, positions.astype(jnp.float32), precision=lax.Precision.HIGHEST)
    freq = jnp.exp(-(2.0 * slots.astype(jnp.float32) / HD) * jnp.log(jnp.float32(1.0e6)))
    angle = jnp.transpose(chosen) * freq[None, :]
    return jnp.cos(angle), jnp.sin(angle)


def rotate(x, cosv, sinv):
    half = x.shape[-1] // 2
    first, second = x[..., :half], x[..., half:]
    return jnp.concatenate([first * cosv - second * sinv, second * cosv + first * sinv], -1)


def unrotate(x, cosv, sinv):
    half = x.shape[-1] // 2
    first, second = x[..., :half], x[..., half:]
    return jnp.concatenate([first * cosv + second * sinv, second * cosv - first * sinv], -1)


def turn_rows(rows, cosv, sinv, turner):
    count = rows.shape[0]
    query = rows[:, :, :QPK * HD].reshape(count, KV, QPK, HD)
    query = turner(query, cosv[:, None, None, :], sinv[:, None, None, :]).reshape(count, KV, QPK * HD)
    key = turner(rows[:, :, QPK * HD:(QPK + 1) * HD], cosv[:, None, :], sinv[:, None, :])
    return jnp.concatenate([query, key, rows[:, :, (QPK + 1) * HD:]], 2)


def settle(value):
    return lax.optimization_barrier(value.astype(jnp.bfloat16)).astype(jnp.float32)


def attend_group(rows, cot, valid):
    scale = HD ** -0.5
    query = rows[:, :QPK * HD].reshape(SEQ, QPK, HD).astype(jnp.float32)
    key = rows[:, QPK * HD:(QPK + 1) * HD].astype(jnp.float32)
    value = rows[:, (QPK + 1) * HD:].astype(jnp.float32)
    cot = jnp.where(valid[:, None], cot, jnp.zeros((), cot.dtype)).reshape(SEQ, QPK, HD).astype(jnp.float32)
    score = jnp.einsum("iqd,jd->qij", query, key) * scale
    place = jnp.arange(SEQ, dtype=jnp.int32)
    allowed = (place[None, :] <= place[:, None]) & valid[None, :]
    score = jnp.where(allowed[None], score, -1.0e30)
    top = jnp.max(score, axis=-1, keepdims=True)
    weight = jnp.exp(score - top)
    probs = settle(weight / jnp.sum(weight, axis=-1, keepdims=True))
    output = settle(jnp.einsum("qij,jd->iqd", probs, value))
    dvalue = jnp.einsum("qij,iqd->jd", probs, cot).astype(jnp.bfloat16)
    dprob = jnp.einsum("iqd,jd->qij", cot, value)
    delta = jnp.transpose(jnp.sum(cot * output, axis=-1))
    dscore = settle(probs * (dprob - delta[:, :, None]))
    dquery = (jnp.einsum("qij,jd->iqd", dscore, key) * scale).astype(jnp.bfloat16).reshape(SEQ, QPK * HD)
    dkey = (jnp.einsum("qij,iqd->jd", dscore, query) * scale).astype(jnp.bfloat16)
    return jnp.concatenate([dquery, dkey, dvalue], 1)


def reference(vision_rows, positions, destination, out_grad):
    cosv, sinv = rope_parts(positions)
    rotated = turn_rows(vision_rows.astype(jnp.float32), cosv, sinv, rotate).astype(jnp.bfloat16)
    devices = N_TILE * N_HEAD
    dest = destination[:, 0].reshape(devices, VIS_DEV)
    order = jnp.arange(VIS_DEV, dtype=jnp.int32)
    same = (dest[:, :, None] == dest[:, None, :]) & (order[None, None, :] < order[None, :, None])
    rank = jnp.sum(same.astype(jnp.int32), axis=2)
    device = jnp.arange(devices, dtype=jnp.int32)[:, None]
    place = dest * SEQ + (device % N_HEAD) * SLOT_DEV + (device // N_HEAD) * C + rank
    slot_row = jnp.full((N_TILE * SEQ,), VIS_ROWS, jnp.int32).at[place.reshape(-1)].set(jnp.arange(VIS_ROWS, dtype=jnp.int32))

    def one_sequence(carry, index):
        ids = lax.dynamic_slice_in_dim(slot_row, index * SEQ, SEQ, 0)
        valid = ids < VIS_ROWS
        rows = jnp.where(valid[:, None, None], rotated[jnp.minimum(ids, VIS_ROWS - 1)], jnp.zeros((), jnp.bfloat16))
        cot = lax.dynamic_slice_in_dim(out_grad, index * SEQ, SEQ, 0)

        def per_group(pair):
            return attend_group(pair[0], pair[1], valid)

        grads = lax.map(per_group, (jnp.swapaxes(rows, 0, 1), jnp.swapaxes(cot, 0, 1)))
        carry = carry.at[ids].set(jnp.swapaxes(grads, 0, 1), mode="drop")
        return carry, None

    start = jnp.zeros((VIS_ROWS, KV, G), jnp.bfloat16)
    gathered, _ = lax.scan(one_sequence, start, jnp.arange(N_TILE, dtype=jnp.int32))
    return turn_rows(gathered.astype(jnp.float32), cosv, sinv, unrotate).astype(jnp.bfloat16)
```

```python
import functools
import math

import jax
import jax.numpy as jnp
from jax import lax
from jax.experimental import pallas as pl
from jax.experimental.pallas import tpu as pltpu
from jax.sharding import PartitionSpec as P

KV = 8
HD = 128
C = 2
QPK = 4
LANES = 128
F32 = jnp.float32
BF16 = jnp.bfloat16
NEG = -1e30
VMEM = pl.BlockSpec(memory_space=pltpu.VMEM)


def nt(a, b):
    return lax.dot_general(a, b, (((1,), (1,)), ((), ())), preferred_element_type=F32)


def iota(shape, dim):
    return lax.broadcasted_iota(jnp.int32, shape, dim)


def rope_tables(pos_ref):
    tokens = pos_ref.shape[1]
    half = HD // 2
    slots = iota((tokens, HD), 1) % half
    first = half // 4
    second = (half - first) // 2
    eye = (iota((tokens, tokens), 0) == iota((tokens, tokens), 1)).astype(BF16)
    column = [
        nt(eye, jnp.broadcast_to(pos_ref[s : s + 1, :].astype(F32).astype(BF16), (HD, tokens)))
        for s in range(3)
    ]
    chosen = jnp.where(
        slots < first, column[0], jnp.where(slots < first + second, column[1], column[2])
    )
    freq = jnp.exp(-(2.0 * slots.astype(F32) / HD) * math.log(1000000.0))
    angle = chosen * freq
    sign = jnp.where(iota((tokens, HD), 1) < half, -1.0, 1.0)
    return jnp.cos(angle), jnp.sin(angle) * sign


def per_group(table):
    tokens = table.shape[0]
    return jnp.broadcast_to(table[:, None, :], (tokens, KV, HD)).reshape(tokens * KV, HD)


def own_row(dest_ref, tokens):
    start = (lax.axis_index("tile") * lax.axis_size("head") + lax.axis_index("head")) * tokens
    row = dest_ref[pl.ds(start // LANES, 1), :].astype(F32).astype(BF16)
    return row, start % LANES


def own_targets(dest_ref, tokens, rows):
    row, off = own_row(dest_ref, tokens)
    count = tokens * KV
    wide = (iota((count, LANES), 1) == off + iota((count, LANES), 0) // KV).astype(BF16)
    narrow = (iota((tokens, LANES), 1) == off + iota((tokens, LANES), 0)).astype(BF16)
    along = nt(jnp.broadcast_to(row, (8, LANES)), wide)[:1]
    down = nt(narrow, jnp.broadcast_to(row, (rows, LANES)))
    return along, down


def slot_keys(dest_ref, tokens):
    count = tokens * KV
    along, down = own_targets(dest_ref, tokens, count)
    lane = iota((tokens, count), 1)
    earlier = (down == along) & (iota((tokens, count), 0) < lane // KV)
    rank = jnp.sum(earlier.astype(F32), axis=0, keepdims=True)
    return ((along * C + rank) * KV).astype(jnp.int32) + iota((1, count), 1) % KV


def row_keys(shape, dim, tiles, local):
    at = iota(shape, dim)
    slots = tiles * C
    return ((at // local) % slots) * KV + (at // (slots * local)) * local + at % local


def pack_kernel(vis_ref, pos_ref, dest_ref, out_ref, *, tiles, local):
    count, width = vis_ref.shape
    tokens = count // KV
    total = out_ref.shape[0]
    cosv, sinv = rope_tables(pos_ref)
    cosv, sinv = per_group(cosv), per_group(sinv)
    place = (row_keys((total, count), 0, tiles, local) == slot_keys(dest_ref, tokens)).astype(BF16)
    for at in range(0, width, HD):
        x = vis_ref[:, at : at + HD]
        if at < (QPK + 1) * HD:
            x = x.astype(F32)
            x = (x * cosv + pltpu.roll(x, HD // 2, 1) * sinv).astype(BF16)
        out_ref[:, at : at + HD] = jnp.dot(place, x, preferred_element_type=F32).astype(BF16)


def side_kernel(
    pos_ref, dest_ref, after_ref, cos_ref, sin_ref, gather_ref, bias_ref, valid_ref, *, tiles, heads, local
):
    del after_ref
    tokens = pos_ref.shape[1]
    count = tokens * KV
    total = heads * tiles * C * local
    cosv, sinv = rope_tables(pos_ref)
    cos_ref[...] = per_group(cosv)
    sin_ref[...] = per_group(sinv)
    place = row_keys((total, count), 0, tiles, local) == slot_keys(dest_ref, tokens)
    gather_ref[...] = jnp.transpose(place.astype(F32)).astype(BF16)
    mine = lax.axis_index("tile")
    at = iota((total, LANES), 0)
    slots = tiles * C
    device = ((at // (C * local)) % tiles) * heads + at // (slots * local)

    def tally(block, sums):
        hit = (dest_ref[pl.ds(block, 1), :] == mine).astype(F32).astype(BF16)
        source = (block * LANES + iota((total, LANES), 1)) // tokens
        return sums + nt((source == device).astype(F32).astype(BF16), jnp.broadcast_to(hit, (LANES, LANES)))

    counts = lax.fori_loop(0, dest_ref.shape[0], tally, jnp.zeros((total, LANES), F32))
    valid = counts > ((at // local) % C).astype(F32)
    valid_ref[...] = valid.astype(F32)
    key_ok = jnp.where(valid, 0.0, NEG)
    key = iota((total, LANES), 0)
    for first in range(0, total, LANES):
        query = first + iota((total, LANES), 1)
        seen = (key // local <= query // local) & (key % local == query % local)
        bias_ref[:, first : first + LANES] = jnp.where(seen, key_ok, NEG)


def split_kernel(cot_ref, own_ref, other_ref, *, local):
    head = lax.axis_index("head")
    total, count = own_ref.shape[0], cot_ref.shape[0]
    row, lane = iota((total, count), 0), iota((total, count), 1)
    base = (row // local) * KV + row % local
    cot = cot_ref[...]
    for ref, group in ((own_ref, head), (other_ref, 1 - head)):
        pick = (lane == base + group * local).astype(BF16)
        ref[...] = jnp.dot(pick, cot, preferred_element_type=F32).astype(BF16)


def attend_kernel(rows_ref, bias_ref, valid_ref, *refs, pair):
    cot_refs, (out_ref, cot_at, dkey_at, dvalue_at) = refs[: 1 + pair], refs[1 + pair :]
    total = rows_ref.shape[0]
    block = min(256, total)
    qcols = QPK * HD
    scale = HD ** (-0.5)
    if pair:
        half = total // 2
        head = lax.axis_index("head")
        cot_at[pl.ds(pl.multiple_of(head * half, half), half), :] = cot_refs[0][...]
        cot_at[pl.ds(pl.multiple_of((1 - head) * half, half), half), :] = cot_refs[1][...]
    else:
        cot_at[...] = cot_refs[0][...]
    key = rows_ref[:, qcols : qcols + HD]
    value = rows_ref[:, qcols + HD :]

    def step(at):
        rows = pl.ds(at, block)
        ok = valid_ref[rows, :] > 0.0
        dkey = jnp.zeros((total, HD), F32)
        dvalue = jnp.zeros((total, HD), F32)
        for q in range(QPK):
            cols = slice(q * HD, (q + 1) * HD)
            query = rows_ref[rows, cols]
            cot = jnp.where(ok, cot_at[rows, cols].astype(F32), 0.0).astype(BF16)
            score = nt(key, query) * scale + bias_ref[:, pl.ds(at, block)]
            weight = jnp.exp(score - jnp.max(score, axis=0, keepdims=True))
            probs = (weight * (1.0 / jnp.sum(weight, axis=0, keepdims=True))).astype(BF16)
            dprob = nt(value, cot)
            wide = probs.astype(F32)
            delta = jnp.sum(wide * dprob, axis=0, keepdims=True)
            dscore = (wide * (dprob - delta)).astype(BF16)
            dvalue += jnp.dot(probs, cot, preferred_element_type=F32)
            dkey += jnp.dot(dscore, query, preferred_element_type=F32)
            dquery = lax.dot_general(
                dscore, key, (((0,), (0,)), ((), ())), preferred_element_type=F32
            )
            out_ref[rows, cols] = (dquery * scale).astype(BF16)
        return dkey, dvalue

    if total == block:
        dkey, dvalue = step(0)
    else:
        dkey_at[...] = jnp.zeros((total, HD), F32)
        dvalue_at[...] = jnp.zeros((total, HD), F32)

        @pl.loop(0, total // block)
        def _(index):
            dkey, dvalue = step(pl.multiple_of(index * block, block))
            dkey_at[...] += dkey
            dvalue_at[...] += dvalue

        dkey, dvalue = dkey_at[...], dvalue_at[...]
    out_ref[:, qcols : qcols + HD] = (dkey * scale).astype(BF16)
    out_ref[:, qcols + HD :] = dvalue.astype(BF16)


def gather_kernel(rows_ref, gather_ref, cos_ref, sin_ref, out_ref):
    width = rows_ref.shape[1]
    pick = gather_ref[...]
    for at in range(0, width, HD):
        x = jnp.dot(pick, rows_ref[:, at : at + HD], preferred_element_type=F32)
        if at < (QPK + 1) * HD:
            x = x * cos_ref[...] - pltpu.roll(x, HD // 2, 1) * sin_ref[...]
        out_ref[:, at : at + HD] = x.astype(BF16)


def call(kernel, outs, *args, scratch=()):
    shapes = [jax.ShapeDtypeStruct(s, d) for s, d in outs]
    single = len(shapes) == 1
    return pl.pallas_call(
        kernel,
        out_shape=shapes[0] if single else shapes,
        in_specs=[VMEM] * len(args),
        out_specs=VMEM if single else [VMEM] * len(shapes),
        scratch_shapes=list(scratch),
        compiler_params=pltpu.CompilerParams(vmem_limit_bytes=48 * 2**20),
    )(*args)


def body(vision_rows, positions, destination, out_grad):
    tiles = lax.axis_size("tile")
    heads = lax.axis_size("head")
    tokens, groups, width = vision_rows.shape
    local = groups // heads
    count = tokens * groups
    total = heads * tiles * C * local
    qcols = QPK * HD
    targets = destination.reshape(-1, LANES)
    outgoing = call(
        functools.partial(pack_kernel, tiles=tiles, local=local),
        [((total, width), BF16)],
        vision_rows.reshape(count, width),
        positions,
        targets,
    )

    def swap(rows):
        parts = rows.reshape(heads * tiles, C * local, width)
        parts = lax.all_to_all(parts, ("head", "tile"), split_axis=0, concat_axis=0, tiled=True)
        return parts.reshape(total, width)

    incoming = swap(outgoing)
    if heads == 2:
        slots = out_grad.shape[0]
        own, other = call(
            functools.partial(split_kernel, local=local),
            [((slots * local, qcols), BF16)] * 2,
            out_grad.reshape(slots * groups, qcols),
        )
        cots = [own, lax.ppermute(other, "head", [(0, 1), (1, 0)])]
    else:
        moved = lax.all_to_all(out_grad, "head", split_axis=1, concat_axis=0, tiled=True)
        cots = [moved.reshape(total, qcols)]
    cosv, sinv, gather, bias, valid = call(
        functools.partial(side_kernel, tiles=tiles, heads=heads, local=local),
        [
            ((count, HD), F32),
            ((count, HD), F32),
            ((count, total), BF16),
            ((total, total), F32),
            ((total, LANES), F32),
        ],
        positions,
        targets,
        outgoing[:16, :LANES],
    )
    grads = call(
        functools.partial(attend_kernel, pair=heads == 2),
        [((total, width), BF16)],
        incoming,
        bias,
        valid,
        *cots,
        scratch=(
            pltpu.VMEM((total, qcols), BF16),
            pltpu.VMEM((total, HD), F32),
            pltpu.VMEM((total, HD), F32),
        ),
    )
    result = call(gather_kernel, [((count, width), BF16)], swap(grads), gather, cosv, sinv)
    return result.reshape(tokens, groups, width)


def solution(mesh):
    return jax.shard_map(
        body,
        mesh=mesh,
        in_specs=(
            P(("tile", "head"), None, None),
            P(None, ("tile", "head")),
            P(),
            P(("tile", "head"), None, None),
        ),
        out_specs=P(("tile", "head"), None, None),
        check_vma=False,
    )
```

```python
import functools
import math

import jax
import jax.numpy as jnp
from jax import lax
from jax.experimental import pallas as pl
from jax.experimental.pallas import tpu as pltpu
from jax.sharding import PartitionSpec as P

KV = 8
HD = 128
C = 2
QPK = 4
LANES = 128
BLOCK = 64
F32 = jnp.float32
BF16 = jnp.bfloat16
NEG = -1e30
VMEM = pl.BlockSpec(memory_space=pltpu.VMEM)


def nt(a, b):
    return lax.dot_general(a, b, (((1,), (1,)), ((), ())), preferred_element_type=F32)


def iota(shape, dim):
    return lax.broadcasted_iota(jnp.int32, shape, dim)


def rope_tables(pos_ref):
    tokens = pos_ref.shape[1]
    half = HD // 2
    slots = iota((tokens, HD), 1) % half
    first = half // 4
    second = (half - first) // 2
    eye = (iota((tokens, tokens), 0) == iota((tokens, tokens), 1)).astype(BF16)
    column = [
        nt(eye, jnp.broadcast_to(pos_ref[s : s + 1, :].astype(F32).astype(BF16), (HD, tokens)))
        for s in range(3)
    ]
    chosen = jnp.where(
        slots < first, column[0], jnp.where(slots < first + second, column[1], column[2])
    )
    freq = jnp.exp(-(2.0 * slots.astype(F32) / HD) * math.log(1000000.0))
    angle = chosen * freq
    sign = jnp.where(iota((tokens, HD), 1) < half, -1.0, 1.0)
    return jnp.cos(angle), jnp.sin(angle) * sign


def per_group(table):
    tokens = table.shape[0]
    return jnp.broadcast_to(table[:, None, :], (tokens, KV, HD)).reshape(tokens * KV, HD)


def own_row(dest_ref, tokens):
    start = (lax.axis_index("tile") * lax.axis_size("head") + lax.axis_index("head")) * tokens
    row = dest_ref[pl.ds(start // LANES, 1), :].astype(F32).astype(BF16)
    return row, start % LANES


def own_targets(dest_ref, tokens, rows):
    row, off = own_row(dest_ref, tokens)
    count = tokens * KV
    wide = (iota((count, LANES), 1) == off + iota((count, LANES), 0) // KV).astype(BF16)
    narrow = (iota((tokens, LANES), 1) == off + iota((tokens, LANES), 0)).astype(BF16)
    along = nt(jnp.broadcast_to(row, (8, LANES)), wide)[:1]
    down = nt(narrow, jnp.broadcast_to(row, (rows, LANES)))
    return along, down


def slot_keys(dest_ref, tokens):
    count = tokens * KV
    along, down = own_targets(dest_ref, tokens, count)
    lane = iota((tokens, count), 1)
    earlier = (down == along) & (iota((tokens, count), 0) < lane // KV)
    rank = jnp.sum(earlier.astype(F32), axis=0, keepdims=True)
    return ((along * C + rank) * KV).astype(jnp.int32) + iota((1, count), 1) % KV


def row_keys(shape, dim, tiles, local):
    at = iota(shape, dim)
    slots = tiles * C
    return ((at // local) % slots) * KV + (at // (slots * local)) * local + at % local


def pack_kernel(vis_hbm, pos_hbm, dest_hbm, out_ref, vis_ref, pos_ref, dest_ref, sems, *, tiles, local):
    pairs = ((dest_hbm, dest_ref), (pos_hbm, pos_ref), (vis_hbm, vis_ref))
    loads = [pltpu.make_async_copy(a, b, sems.at[n]) for n, (a, b) in enumerate(pairs)]
    for load in loads:
        load.start()
    count, width = vis_ref.shape
    tokens = count // KV
    total = out_ref.shape[0]
    keys = row_keys((total, count), 0, tiles, local)
    loads[0].wait()
    place = (keys == slot_keys(dest_ref, tokens)).astype(BF16)
    loads[1].wait()
    cosv, sinv = rope_tables(pos_ref)
    cosv, sinv = per_group(cosv), per_group(sinv)
    loads[2].wait()
    for at in range(0, width, HD):
        x = vis_ref[:, at : at + HD]
        if at < (QPK + 1) * HD:
            x = x.astype(F32)
            x = (x * cosv + pltpu.roll(x, HD // 2, 1) * sinv).astype(BF16)
        out_ref[:, at : at + HD] = jnp.dot(place, x, preferred_element_type=F32).astype(BF16)


def side_kernel(
    pos_ref, dest_ref, after_ref, cos_ref, sin_ref, gather_ref, valid_ref, *order_refs, tiles, heads, local
):
    del after_ref
    tokens = pos_ref.shape[1]
    count = tokens * KV
    seq = heads * tiles * C
    total = seq * local
    cosv, sinv = rope_tables(pos_ref)
    cos_ref[...] = per_group(cosv)
    sin_ref[...] = per_group(sinv)
    place = row_keys((total, count), 0, tiles, local) == slot_keys(dest_ref, tokens)
    gather_ref[...] = jnp.transpose(place.astype(F32)).astype(BF16)
    mine = lax.axis_index("tile")
    slot = iota((seq, LANES), 0)
    device = ((slot // C) % tiles) * heads + slot // (tiles * C)

    def tally(block, sums):
        hit = (dest_ref[pl.ds(block, 1), :] == mine).astype(F32).astype(BF16)
        source = (block * LANES + iota((seq, LANES), 1)) // tokens
        return sums + nt((source == device).astype(F32).astype(BF16), jnp.broadcast_to(hit, (LANES, LANES)))

    counts = lax.fori_loop(0, dest_ref.shape[0], tally, jnp.zeros((seq, LANES), F32))
    valid_ref[...] = (counts > (slot % C).astype(F32)).astype(F32)
    if order_refs:
        by_group, by_slot = iota((total, total), 0), iota((total, total), 1)
        order_refs[0][...] = (by_group % seq * local + by_group // seq == by_slot).astype(BF16)
        by_slot, by_group = by_group, by_slot
        order_refs[1][...] = (by_group % seq * local + by_group // seq == by_slot).astype(BF16)


def split_kernel(cot_ref, own_ref, other_ref, *, local):
    head = lax.axis_index("head")
    total, count = own_ref.shape[0], cot_ref.shape[0]
    slots = total // local
    row, lane = iota((total, count), 0), iota((total, count), 1)
    base = (row % slots) * KV + row // slots
    cot = cot_ref[...]
    for ref, group in ((own_ref, head), (other_ref, 1 - head)):
        pick = (lane == base + group * local).astype(BF16)
        ref[...] = jnp.dot(pick, cot, preferred_element_type=F32).astype(BF16)


def join_kernel(valid_ref, *refs, local):
    cot_refs, (out_ref, whole) = refs[:-2], refs[-2:]
    seq = valid_ref.shape[0]
    block = min(BLOCK, seq)
    if len(cot_refs) == 2:
        half = seq // 2
        head = lax.axis_index("head")
        for ref, place in zip(cot_refs, (head, 1 - head)):
            for g in range(local):
                at = pl.multiple_of(g * seq + place * half, half)
                whole[pl.ds(at, half), :] = ref[g * half : (g + 1) * half, :]
    else:
        whole[...] = cot_refs[0][...]
    for first in range(0, seq, block):
        ok = valid_ref[first : first + block, :] > 0.0
        for g in range(local):
            for q in range(QPK):
                part = whole[g * seq + first : g * seq + first + block, q * HD : (q + 1) * HD]
                at = (g * seq + first) * QPK + q * block
                out_ref[at : at + block, :] = jnp.where(ok, part.astype(F32), 0.0).astype(BF16)


def attend_kernel(rows_ref, valid_ref, cot_ref, *refs, local):
    order_refs, (out_ref, rows_at, grads_at, dkey_at, dvalue_at) = refs[:-5], refs[-5:]
    total, width = rows_ref.shape
    seq = total // local
    block = min(BLOCK, seq)
    wide = QPK * block
    qcols = QPK * HD
    scale = HD ** (-0.5)
    if order_refs:
        for at in range(0, width, 2 * HD):
            cols = slice(at, at + 2 * HD)
            rows_at[:, cols] = jnp.dot(
                order_refs[0][...], rows_ref[:, cols], preferred_element_type=F32
            ).astype(BF16)
    else:
        rows_at, grads_at = rows_ref, out_ref
    key_ok = jnp.where(valid_ref[:, :1] > 0.0, 0.0, NEG)

    def step(group, first, bias):
        rows = pl.ds(group * seq + first, block)
        every = slice(group * seq, (group + 1) * seq)
        key = rows_at[every, qcols : qcols + HD]
        value = rows_at[every, qcols + HD :]
        query = jnp.concatenate([rows_at[rows, q * HD : (q + 1) * HD] for q in range(QPK)], 0)
        cot = cot_ref[pl.ds((group * seq + first) * QPK, wide), :]
        score = nt(key, query) * scale + bias
        weight = jnp.exp(score - jnp.max(score, axis=0, keepdims=True))
        probs = (weight * (1.0 / jnp.sum(weight, axis=0, keepdims=True))).astype(BF16)
        dprob = nt(value, cot)
        broad = probs.astype(F32)
        delta = jnp.sum(broad * dprob, axis=0, keepdims=True)
        dscore = (broad * (dprob - delta)).astype(BF16)
        dvalue = jnp.dot(probs, cot, preferred_element_type=F32)
        dkey = jnp.dot(dscore, query, preferred_element_type=F32)
        dquery = lax.dot_general(dscore, key, (((0,), (0,)), ((), ())), preferred_element_type=F32)
        dquery = (dquery * scale).astype(BF16)
        for q in range(QPK):
            grads_at[rows, q * HD : (q + 1) * HD] = dquery[q * block : (q + 1) * block]
        return dkey, dvalue

    def mask(first):
        seen = iota((seq, wide), 0) <= first + iota((seq, wide), 1) % block
        return jnp.where(seen, key_ok, NEG)

    bias = mask(0) if seq == block else None
    for group in range(local):
        every = slice(group * seq, (group + 1) * seq)
        if seq == block:
            dkey, dvalue = step(group, 0, bias)
        else:
            dkey_at[...] = jnp.zeros((seq, HD), F32)
            dvalue_at[...] = jnp.zeros((seq, HD), F32)

            @pl.loop(0, seq // block)
            def _(index):
                first = pl.multiple_of(index * block, block)
                dkey, dvalue = step(group, first, mask(first))
                dkey_at[...] += dkey
                dvalue_at[...] += dvalue

            dkey, dvalue = dkey_at[...], dvalue_at[...]
        grads_at[every, qcols : qcols + HD] = (dkey * scale).astype(BF16)
        grads_at[every, qcols + HD :] = dvalue.astype(BF16)
    if order_refs:
        for at in range(0, width, 2 * HD):
            cols = slice(at, at + 2 * HD)
            out_ref[:, cols] = jnp.dot(
                order_refs[1][...], grads_at[:, cols], preferred_element_type=F32
            ).astype(BF16)


def gather_kernel(rows_ref, gather_ref, cos_ref, sin_ref, out_ref):
    width = rows_ref.shape[1]
    pick = gather_ref[...]
    for at in range(0, width, HD):
        x = jnp.dot(pick, rows_ref[:, at : at + HD], preferred_element_type=F32)
        if at < (QPK + 1) * HD:
            x = x * cos_ref[...] - pltpu.roll(x, HD // 2, 1) * sin_ref[...]
        out_ref[:, at : at + HD] = x.astype(BF16)


def call(kernel, outs, *args, scratch=(), specs=None):
    shapes = [jax.ShapeDtypeStruct(s, d) for s, d in outs]
    single = len(shapes) == 1
    return pl.pallas_call(
        kernel,
        out_shape=shapes[0] if single else shapes,
        in_specs=specs or [VMEM] * len(args),
        out_specs=VMEM if single else [VMEM] * len(shapes),
        scratch_shapes=list(scratch),
        compiler_params=pltpu.CompilerParams(vmem_limit_bytes=48 * 2**20),
    )(*args)


def body(vision_rows, positions, destination, out_grad):
    tiles = lax.axis_size("tile")
    heads = lax.axis_size("head")
    tokens, groups, width = vision_rows.shape
    local = groups // heads
    count = tokens * groups
    seq = heads * tiles * C
    total = seq * local
    qcols = QPK * HD
    targets = destination.reshape(-1, LANES)
    rows = vision_rows.reshape(count, width)
    outgoing = call(
        functools.partial(pack_kernel, tiles=tiles, local=local),
        [((total, width), BF16)],
        *(pltpu.with_memory_space_constraint(x, pltpu.HBM) for x in (rows, positions, targets)),
        specs=[pl.BlockSpec(memory_space=pltpu.HBM)] * 3,
        scratch=(
            pltpu.VMEM(rows.shape, BF16),
            pltpu.VMEM(positions.shape, jnp.int32),
            pltpu.VMEM(targets.shape, jnp.int32),
            pltpu.SemaphoreType.DMA((3,)),
        ),
    )

    def swap(rows):
        parts = rows.reshape(heads * tiles, C * local, width)
        parts = lax.all_to_all(parts, ("head", "tile"), split_axis=0, concat_axis=0, tiled=True)
        return parts.reshape(total, width)

    incoming = swap(outgoing)
    if heads == 2:
        slots = out_grad.shape[0]
        own, other = call(
            functools.partial(split_kernel, local=local),
            [((slots * local, qcols), BF16)] * 2,
            out_grad.reshape(slots * groups, qcols),
        )
        cots = [own, lax.ppermute(other, "head", [(0, 1), (1, 0)])]
    else:
        moved = lax.all_to_all(out_grad, "head", split_axis=1, concat_axis=0, tiled=True)
        cots = [jnp.swapaxes(moved, 0, 1).reshape(total, qcols)]
    cosv, sinv, gather, valid, *orders = call(
        functools.partial(side_kernel, tiles=tiles, heads=heads, local=local),
        [
            ((count, HD), F32),
            ((count, HD), F32),
            ((count, total), BF16),
            ((seq, LANES), F32),
        ]
        + [((total, total), BF16)] * (2 if local > 1 else 0),
        positions,
        targets,
        outgoing[:16, :LANES],
    )
    cot = call(
        functools.partial(join_kernel, local=local),
        [((total * QPK, HD), BF16)],
        valid,
        *cots,
        scratch=(pltpu.VMEM((total, qcols), BF16),),
    )
    grads = call(
        functools.partial(attend_kernel, local=local),
        [((total, width), BF16)],
        incoming,
        valid,
        cot,
        *orders,
        scratch=(
            pltpu.VMEM((total, width), BF16),
            pltpu.VMEM((total, width), BF16),
            pltpu.VMEM((seq, HD), F32),
            pltpu.VMEM((seq, HD), F32),
        ),
    )
    result = call(gather_kernel, [((count, width), BF16)], swap(grads), gather, cosv, sinv)
    return result.reshape(tokens, groups, width)


def solution(mesh):
    return jax.shard_map(
        body,
        mesh=mesh,
        in_specs=(
            P(("tile", "head"), None, None),
            P(None, ("tile", "head")),
            P(),
            P(("tile", "head"), None, None),
        ),
        out_specs=P(("tile", "head"), None, None),
        check_vma=False,
    )
```

```python
import functools
import math

import jax
import jax.numpy as jnp
from jax import lax
from jax.experimental import pallas as pl
from jax.experimental.pallas import tpu as pltpu
from jax.sharding import PartitionSpec as P

KV = 8
HD = 128
C = 2
QPK = 4
LANES = 128
BLOCK = 64
PIECES = 2
F32 = jnp.float32
BF16 = jnp.bfloat16
NEG = -1e30
VMEM = pl.BlockSpec(memory_space=pltpu.VMEM)
HBM = pl.BlockSpec(memory_space=pltpu.HBM)


def nt(a, b):
    return lax.dot_general(a, b, (((1,), (1,)), ((), ())), preferred_element_type=F32)


def iota(shape, dim):
    return lax.broadcasted_iota(jnp.int32, shape, dim)


def rope_tables(pos_ref):
    tokens = pos_ref.shape[1]
    half = HD // 2
    slots = iota((tokens, HD), 1) % half
    first = half // 4
    second = (half - first) // 2
    eye = (iota((tokens, tokens), 0) == iota((tokens, tokens), 1)).astype(BF16)
    column = [
        nt(eye, jnp.broadcast_to(pos_ref[s : s + 1, :].astype(F32).astype(BF16), (HD, tokens)))
        for s in range(3)
    ]
    chosen = jnp.where(
        slots < first, column[0], jnp.where(slots < first + second, column[1], column[2])
    )
    freq = jnp.exp(-(2.0 * slots.astype(F32) / HD) * math.log(1000000.0))
    angle = chosen * freq
    sign = jnp.where(iota((tokens, HD), 1) < half, -1.0, 1.0)
    return jnp.cos(angle), jnp.sin(angle) * sign


def per_group(table):
    tokens = table.shape[0]
    return jnp.broadcast_to(table[:, None, :], (tokens, KV, HD)).reshape(tokens * KV, HD)


def token_slots(dest_ref, tokens, tile):
    start = (tile * lax.axis_size("head") + lax.axis_index("head")) * tokens
    count = tokens * KV
    off = start % LANES
    row = dest_ref[pl.ds(start // LANES, 1), :].astype(F32).astype(BF16)
    wide = (iota((count, LANES), 1) == off + iota((count, LANES), 0) // KV).astype(BF16)
    narrow = (iota((tokens, LANES), 1) == off + iota((tokens, LANES), 0)).astype(BF16)
    along = nt(jnp.broadcast_to(row, (8, LANES)), wide)[:1]
    down = nt(narrow, jnp.broadcast_to(row, (count, LANES)))
    lane = iota((tokens, count), 1)
    earlier = (down == along) & (iota((tokens, count), 0) < lane // KV)
    rank = jnp.sum(earlier.astype(F32), axis=0, keepdims=True)
    return (along * C + rank).astype(jnp.int32)


def row_parts(at, tiles, local, sides):
    group, at = at % local, at // local
    rank, at = at % C, at // C
    side, at = at % sides, at // sides
    units = tiles // sides
    order = unit_order(units, sides)
    place, head = at % units, at // units
    unit = place
    if order != list(range(units)):
        unit = sum(jnp.where(place == n, order[n], 0) for n in range(units))
    return head, unit, side, rank, group


def unit_order(units, sides):
    if sides == 2 and units == 8:
        return [z * 2 + y for y in (0, 1) for z in (2, 1, 0, 3)]
    return list(range(units))


def placement(dest_ref, tokens, tiles, local, sides, total):
    count = tokens * KV
    tile = lax.axis_index("tile")
    side = tile % sides
    head, unit, at_side, rank, group = row_parts(iota((total, LANES), 0), tiles, local, sides)
    target = unit * sides + side
    rows = (((target * C + rank) * sides + at_side) * KV + head * local + group)[:, :1]
    parts = []
    for other in range(sides):
        from_side = side + other - 2 * side * other
        slots = token_slots(dest_ref, tokens, tile - side + from_side)
        lanes = (slots * sides + from_side) * KV + iota((1, count), 1) % KV
        parts.append((rows == lanes).astype(F32))
    return parts[0] if sides == 1 else jnp.concatenate(parts, 1)


def ready_kernel(
    vis_hbm, pos_hbm, dest_hbm, rows_ref, place_ref, vis_ref, pos_ref, dest_ref, sems, *, tiles, local, sides
):
    pairs = ((dest_hbm, dest_ref), (pos_hbm, pos_ref), (vis_hbm, vis_ref))
    loads = [pltpu.make_async_copy(a, b, sems.at[n]) for n, (a, b) in enumerate(pairs)]
    for load in loads:
        load.start()
    tokens = pos_ref.shape[1]
    loads[0].wait()
    place_ref[...] = placement(dest_ref, tokens, tiles, local, sides, place_ref.shape[0]).astype(BF16)
    loads[1].wait()
    cosv, sinv = rope_tables(pos_ref)
    loads[2].wait()
    turn(vis_ref, rows_ref, per_group(cosv), per_group(sinv))


def turn(from_ref, to_ref, cosv, sinv):
    for at in range(0, from_ref.shape[1], HD):
        x = from_ref[:, at : at + HD]
        if at < (QPK + 1) * HD:
            x = x.astype(F32)
            x = (x * cosv + pltpu.roll(x, HD // 2, 1) * sinv).astype(BF16)
        to_ref[:, at : at + HD] = x


def pack_kernel(rows_ref, place_ref, *refs):
    others, (out_hbm, both_ref, out_ref, out_sems) = refs[:-4], refs[-4:]
    count = rows_ref.shape[0]
    if others:
        vis_ref, pos_ref = others
        both_ref[:count, :] = rows_ref[...]
        cosv, sinv = rope_tables(pos_ref)
        turn(vis_ref, both_ref.at[count:, :], per_group(cosv), per_group(sinv))
    else:
        both_ref = rows_ref
    stores = Stores(out_ref, out_hbm, out_sems)
    for at in stores.pieces():
        out_ref[at, :] = jnp.dot(place_ref[at, :], both_ref[...], preferred_element_type=F32).astype(BF16)
        stores.start(at)
    stores.wait()


class Stores:
    def __init__(self, source, target, sems):
        self.source, self.target, self.sems, self.copies = source, target, sems, []

    def pieces(self):
        size = self.source.shape[0] // PIECES
        return [slice(n * size, (n + 1) * size) for n in range(PIECES)]

    def start(self, at):
        sem = self.sems.at[len(self.copies)]
        copy = pltpu.make_async_copy(self.source.at[at, :], self.target.at[at, :], sem)
        copy.start()
        self.copies.append(copy)

    def wait(self):
        for copy in self.copies:
            copy.wait()


def side_kernel(
    pos_ref, dest_ref, after_ref, cos_ref, sin_ref, gather_ref, valid_ref, *order_refs, tiles, heads, local, sides
):
    del after_ref
    tokens = pos_ref.shape[1]
    seq = heads * tiles * C
    total = seq * local
    cosv, sinv = rope_tables(pos_ref)
    cos_ref[...] = per_group(cosv)
    sin_ref[...] = per_group(sinv)
    place = placement(dest_ref, tokens, tiles, local, sides, total)
    gather_ref[...] = jnp.transpose(place).astype(BF16)
    mine = lax.axis_index("tile")
    slot = iota((seq, LANES), 0)
    device = ((slot // C) % tiles) * heads + slot // (tiles * C)

    def tally(block, sums):
        hit = (dest_ref[pl.ds(block, 1), :] == mine).astype(F32).astype(BF16)
        source = (block * LANES + iota((seq, LANES), 1)) // tokens
        return sums + nt((source == device).astype(F32).astype(BF16), jnp.broadcast_to(hit, (LANES, LANES)))

    counts = lax.fori_loop(0, dest_ref.shape[0], tally, jnp.zeros((seq, LANES), F32))
    valid_ref[...] = (counts > (slot % C).astype(F32)).astype(F32)
    if order_refs:
        for ref, dim in zip(order_refs, (1, 0)):
            at = iota((total, total), dim)
            head, unit, side, rank, group = row_parts(at, tiles, local, sides)
            by_group = group * seq + (head * tiles + unit * sides + side) * C + rank
            ref[...] = (by_group == iota((total, total), 1 - dim)).astype(BF16)


def split_kernel(cot_ref, own_ref, other_ref, *, local):
    head = lax.axis_index("head")
    total, count = own_ref.shape[0], cot_ref.shape[0]
    slots = total // local
    row, lane = iota((total, count), 0), iota((total, count), 1)
    base = (row % slots) * KV + row // slots
    cot = cot_ref[...]
    for ref, group in ((own_ref, head), (other_ref, 1 - head)):
        pick = (lane == base + group * local).astype(BF16)
        ref[...] = jnp.dot(pick, cot, preferred_element_type=F32).astype(BF16)


def join_kernel(valid_ref, *refs, local):
    cot_refs, (out_ref, whole) = refs[:-2], refs[-2:]
    seq = valid_ref.shape[0]
    block = min(BLOCK, seq)
    if len(cot_refs) == 2:
        half = seq // 2
        head = lax.axis_index("head")
        for ref, place in zip(cot_refs, (head, 1 - head)):
            for g in range(local):
                at = pl.multiple_of(g * seq + place * half, half)
                whole[pl.ds(at, half), :] = ref[g * half : (g + 1) * half, :]
    else:
        whole[...] = cot_refs[0][...]
    for first in range(0, seq, block):
        ok = valid_ref[first : first + block, :] > 0.0
        for g in range(local):
            for q in range(QPK):
                part = whole[g * seq + first : g * seq + first + block, q * HD : (q + 1) * HD]
                at = (g * seq + first) * QPK + q * block
                out_ref[at : at + block, :] = jnp.where(ok, part.astype(F32), 0.0).astype(BF16)


def attend_kernel(rows_ref, valid_ref, cot_ref, *refs, local):
    order_refs, (out_ref, rows_at, grads_at, sums_at) = refs[:-4], refs[-4:]
    total, width = rows_ref.shape
    seq = total // local
    block = min(BLOCK, seq)
    wide = QPK * block
    qcols = QPK * HD
    scale = HD ** (-0.5)
    if order_refs:
        for at in range(0, width, 2 * HD):
            cols = slice(at, at + 2 * HD)
            rows_at[:, cols] = jnp.dot(
                order_refs[0][...], rows_ref[:, cols], preferred_element_type=F32
            ).astype(BF16)
    else:
        rows_at, grads_at = rows_ref, out_ref
    key_ok = jnp.where(valid_ref[:, :1] > 0.0, 0.0, NEG)

    every = [slice(group * seq, (group + 1) * seq) for group in range(local)]

    def step(first):
        seen = iota((seq, wide), 0) <= first + iota((seq, wide), 1) % block
        bias = jnp.where(seen, key_ok, NEG)
        rows = [pl.ds(group * seq + first, block) for group in range(local)]
        keys = [rows_at[at, qcols : qcols + HD] for at in every]
        values = [rows_at[at, qcols + HD :] for at in every]
        queries = [
            jnp.concatenate([rows_at[at, q * HD : (q + 1) * HD] for q in range(QPK)], 0) for at in rows
        ]
        cots = [cot_ref[pl.ds((group * seq + first) * QPK, wide), :] for group in range(local)]
        scores = [nt(key, query) * scale + bias for key, query in zip(keys, queries)]
        dprobs = [nt(value, cot) for value, cot in zip(values, cots)]
        weights = [jnp.exp(x - jnp.max(x, axis=0, keepdims=True)) for x in scores]
        probs = [
            (x * (1.0 / jnp.sum(x, axis=0, keepdims=True))).astype(BF16) for x in weights
        ]
        broad = [x.astype(F32) for x in probs]
        deltas = [jnp.sum(x * y, axis=0, keepdims=True) for x, y in zip(broad, dprobs)]
        dscores = [(x * (y - z)).astype(BF16) for x, y, z in zip(broad, dprobs, deltas)]
        for at, dscore, key in zip(rows, dscores, keys):
            dquery = lax.dot_general(
                dscore, key, (((0,), (0,)), ((), ())), preferred_element_type=F32
            )
            dquery = (dquery * scale).astype(BF16)
            for q in range(QPK):
                grads_at[at, q * HD : (q + 1) * HD] = dquery[q * block : (q + 1) * block]
        dkeys = [jnp.dot(x, y, preferred_element_type=F32) for x, y in zip(dscores, queries)]
        dvalues = [jnp.dot(x, y, preferred_element_type=F32) for x, y in zip(probs, cots)]
        return dkeys, dvalues

    if seq == block:
        dkeys, dvalues = step(0)
    else:
        sums_at[...] = jnp.zeros(sums_at.shape, F32)

        @pl.loop(0, seq // block)
        def _(index):
            dkeys, dvalues = step(pl.multiple_of(index * block, block))
            for group, at in enumerate(every):
                sums_at[at, :HD] += dkeys[group]
                sums_at[at, HD:] += dvalues[group]

        dkeys, dvalues = [sums_at[at, :HD] for at in every], [sums_at[at, HD:] for at in every]
    for at, dkey, dvalue in zip(every, dkeys, dvalues):
        grads_at[at, qcols : qcols + HD] = (dkey * scale).astype(BF16)
        grads_at[at, qcols + HD :] = dvalue.astype(BF16)
    if order_refs:
        for at in range(0, width, 2 * HD):
            cols = slice(at, at + 2 * HD)
            out_ref[:, cols] = jnp.dot(
                order_refs[1][...], grads_at[:, cols], preferred_element_type=F32
            ).astype(BF16)


def gather_kernel(rows_ref, gather_ref, out_ref, *, part):
    count = out_ref.shape[0]
    pick = gather_ref[part * count : (part + 1) * count, :]
    out_ref[...] = jnp.dot(pick, rows_ref[...], preferred_element_type=F32).astype(BF16)


def finish_kernel(cos_ref, sin_ref, *refs):
    parts, (out_hbm, out_ref, out_sems) = refs[:-3], refs[-3:]
    stores = Stores(out_ref, out_hbm, out_sems)
    for at in stores.pieces():
        cosv, sinv = cos_ref[at, :], sin_ref[at, :]
        for first in range(0, out_ref.shape[1], HD):
            cols = slice(first, first + HD)
            x = sum(ref[at, cols].astype(F32) for ref in parts)
            if first < (QPK + 1) * HD:
                x = x * cosv - pltpu.roll(x, HD // 2, 1) * sinv
            out_ref[at, cols] = x.astype(BF16)
        stores.start(at)
    stores.wait()


def call(kernel, outs, *args, scratch=(), specs=None, out_spec=VMEM):
    shapes = [jax.ShapeDtypeStruct(s, d) for s, d in outs]
    single = len(shapes) == 1
    return pl.pallas_call(
        kernel,
        out_shape=shapes[0] if single else shapes,
        in_specs=specs or [VMEM] * len(args),
        out_specs=out_spec if single else [out_spec] * len(shapes),
        scratch_shapes=list(scratch),
        compiler_params=pltpu.CompilerParams(vmem_limit_bytes=48 * 2**20),
    )(*args)


def body(vision_rows, positions, destination, out_grad):
    tiles = lax.axis_size("tile")
    heads = lax.axis_size("head")
    tokens, groups, width = vision_rows.shape
    local = groups // heads
    count = tokens * groups
    seq = heads * tiles * C
    total = seq * local
    qcols = QPK * HD
    sides = 2 if heads == 2 and tiles % 2 == 0 else 1
    targets = destination.reshape(-1, LANES)
    rows = vision_rows.reshape(count, width)
    kernel = functools.partial

    def to_pair(x):
        return lax.ppermute(x, "tile", [(t, t ^ 1) for t in range(tiles)])

    others = [to_pair(rows), to_pair(positions)] if sides == 2 else []
    turned, place = call(
        kernel(ready_kernel, tiles=tiles, local=local, sides=sides),
        [((count, width), BF16), ((total, sides * count), BF16)],
        *(pltpu.with_memory_space_constraint(x, pltpu.HBM) for x in (rows, positions, targets)),
        specs=[HBM] * 3,
        scratch=(
            pltpu.VMEM(rows.shape, BF16),
            pltpu.VMEM(positions.shape, jnp.int32),
            pltpu.VMEM(targets.shape, jnp.int32),
            pltpu.SemaphoreType.DMA((3,)),
        ),
    )
    outgoing = call(
        pack_kernel,
        [((total, width), BF16)],
        turned,
        place,
        *others,
        out_spec=HBM,
        scratch=(
            pltpu.VMEM((sides * count, width), BF16),
            pltpu.VMEM((total, width), BF16),
            pltpu.SemaphoreType.DMA((PIECES,)),
        ),
    )

    def swap(rows):
        units = tiles // sides
        parts = rows.reshape(heads * units, -1, width)
        if sides == 1:
            axes, groups = ("head", "tile"), None
        else:
            axes, order = ("tile", "head"), unit_order(units, sides)
            groups = [
                [(unit * sides + side) * heads + head for head in range(heads) for unit in order]
                for side in range(sides)
            ]
        parts = lax.all_to_all(
            parts, axes, split_axis=0, concat_axis=0, tiled=True, axis_index_groups=groups
        )
        return parts.reshape(total, width)

    incoming = swap(outgoing)
    if heads == 2:
        slots = out_grad.shape[0]
        own, other = call(
            kernel(split_kernel, local=local),
            [((slots * local, qcols), BF16)] * 2,
            out_grad.reshape(slots * groups, qcols),
        )
        cots = [own, lax.ppermute(other, "head", [(0, 1), (1, 0)])]
    else:
        moved = lax.all_to_all(out_grad, "head", split_axis=1, concat_axis=0, tiled=True)
        cots = [jnp.swapaxes(moved, 0, 1).reshape(total, qcols)]
    cosv, sinv, gather, valid, *orders = call(
        kernel(side_kernel, tiles=tiles, heads=heads, local=local, sides=sides),
        [
            ((count, HD), F32),
            ((count, HD), F32),
            ((sides * count, total), BF16),
            ((seq, LANES), F32),
        ]
        + [((total, total), BF16)] * (2 if local * sides > 1 else 0),
        positions,
        targets,
        outgoing[:16, :LANES],
    )
    cot = call(
        kernel(join_kernel, local=local),
        [((total * QPK, HD), BF16)],
        valid,
        *cots,
        scratch=(pltpu.VMEM((total, qcols), BF16),),
    )
    grads = call(
        kernel(attend_kernel, local=local),
        [((total, width), BF16)],
        incoming,
        valid,
        cot,
        *orders,
        scratch=(
            pltpu.VMEM((total, width), BF16),
            pltpu.VMEM((total, width), BF16),
            pltpu.VMEM((total, 2 * HD) if seq > BLOCK else (8, 2 * HD), F32),
        ),
    )
    back = swap(grads)

    def gathered(part):
        return call(kernel(gather_kernel, part=part), [((count, width), BF16)], back, gather)

    parts = [to_pair(gathered(1))] if sides == 2 else []
    parts.append(gathered(0))
    result = call(
        finish_kernel,
        [((count, width), BF16)],
        cosv,
        sinv,
        *parts,
        out_spec=HBM,
        scratch=(pltpu.VMEM((count, width), BF16), pltpu.SemaphoreType.DMA((PIECES,))),
    )
    return result.reshape(tokens, groups, width)


def solution(mesh):
    return jax.shard_map(
        body,
        mesh=mesh,
        in_specs=(
            P(("tile", "head"), None, None),
            P(None, ("tile", "head")),
            P(),
            P(("tile", "head"), None, None),
        ),
        out_specs=P(("tile", "head"), None, None),
        check_vma=False,
    )
```

```python
import functools
import math

import jax
import jax.numpy as jnp
from jax import lax
from jax.experimental import pallas as pl
from jax.experimental.pallas import tpu as pltpu
from jax.sharding import PartitionSpec as P

KV = 8
HD = 128
C = 2
QPK = 4
LANES = 128
BLOCK = 64
PIECES = 2
F32 = jnp.float32
BF16 = jnp.bfloat16
NEG = -1e30
VMEM = pl.BlockSpec(memory_space=pltpu.VMEM)
HBM = pl.BlockSpec(memory_space=pltpu.HBM)


def nt(a, b):
    return lax.dot_general(a, b, (((1,), (1,)), ((), ())), preferred_element_type=F32)


def iota(shape, dim):
    return lax.broadcasted_iota(jnp.int32, shape, dim)


def rope_tables(pos_ref):
    tokens = pos_ref.shape[1]
    half = HD // 2
    slots = iota((tokens, HD), 1) % half
    first = half // 4
    second = (half - first) // 2
    eye = (iota((tokens, tokens), 0) == iota((tokens, tokens), 1)).astype(BF16)
    column = [
        nt(eye, jnp.broadcast_to(pos_ref[s : s + 1, :].astype(F32).astype(BF16), (HD, tokens)))
        for s in range(3)
    ]
    chosen = jnp.where(
        slots < first, column[0], jnp.where(slots < first + second, column[1], column[2])
    )
    freq = jnp.exp(-(2.0 * slots.astype(F32) / HD) * math.log(1000000.0))
    angle = chosen * freq
    sign = jnp.where(iota((tokens, HD), 1) < half, -1.0, 1.0)
    return jnp.cos(angle), jnp.sin(angle) * sign


def per_group(table):
    tokens = table.shape[0]
    return jnp.broadcast_to(table[:, None, :], (tokens, KV, HD)).reshape(tokens * KV, HD)


def token_slots(dest_ref, tokens, tile):
    start = (tile * lax.axis_size("head") + lax.axis_index("head")) * tokens
    count = tokens * KV
    off = start % LANES
    row = dest_ref[pl.ds(start // LANES, 1), :].astype(F32).astype(BF16)
    wide = (iota((count, LANES), 1) == off + iota((count, LANES), 0) // KV).astype(BF16)
    narrow = (iota((tokens, LANES), 1) == off + iota((tokens, LANES), 0)).astype(BF16)
    along = nt(jnp.broadcast_to(row, (8, LANES)), wide)[:1]
    down = nt(narrow, jnp.broadcast_to(row, (count, LANES)))
    lane = iota((tokens, count), 1)
    earlier = (down == along) & (iota((tokens, count), 0) < lane // KV)
    rank = jnp.sum(earlier.astype(F32), axis=0, keepdims=True)
    return (along * C + rank).astype(jnp.int32)


def row_parts(at, tiles, local, sides):
    group, at = at % local, at // local
    rank, at = at % C, at // C
    side, at = at % sides, at // sides
    units = tiles // sides
    order = unit_order(units, sides)
    place, head = at % units, at // units
    unit = place
    if order != list(range(units)):
        unit = sum(jnp.where(place == n, order[n], 0) for n in range(units))
    return head, unit, side, rank, group


def unit_order(units, sides):
    if sides == 2 and units == 8:
        return [z * 2 + y for y in (0, 1) for z in (2, 1, 0, 3)]
    return list(range(units))


def placement(dest_ref, tokens, tiles, local, sides, total):
    count = tokens * KV
    tile = lax.axis_index("tile")
    side = tile % sides
    head, unit, at_side, rank, group = row_parts(iota((total, LANES), 0), tiles, local, sides)
    target = unit * sides + side
    rows = (((target * C + rank) * sides + at_side) * KV + head * local + group)[:, :1]
    parts = []
    for other in range(sides):
        from_side = side + other - 2 * side * other
        slots = token_slots(dest_ref, tokens, tile - side + from_side)
        lanes = (slots * sides + from_side) * KV + iota((1, count), 1) % KV
        parts.append((rows == lanes).astype(F32))
    return parts[0] if sides == 1 else jnp.concatenate(parts, 1)


def ready_kernel(
    vis_hbm, pos_hbm, dest_hbm, rows_ref, place_ref, vis_ref, pos_ref, dest_ref, sems, *, tiles, local, sides
):
    pairs = ((dest_hbm, dest_ref), (pos_hbm, pos_ref), (vis_hbm, vis_ref))
    loads = [pltpu.make_async_copy(a, b, sems.at[n]) for n, (a, b) in enumerate(pairs)]
    for load in loads:
        load.start()
    tokens = pos_ref.shape[1]
    loads[0].wait()
    place_ref[...] = placement(dest_ref, tokens, tiles, local, sides, place_ref.shape[0]).astype(BF16)
    loads[1].wait()
    cosv, sinv = rope_tables(pos_ref)
    loads[2].wait()
    turn(vis_ref, rows_ref, per_group(cosv), per_group(sinv))


def turn(from_ref, to_ref, cosv, sinv):
    for at in range(0, from_ref.shape[1], HD):
        x = from_ref[:, at : at + HD]
        if at < (QPK + 1) * HD:
            x = x.astype(F32)
            x = (x * cosv + pltpu.roll(x, HD // 2, 1) * sinv).astype(BF16)
        to_ref[:, at : at + HD] = x


def pack_kernel(rows_ref, place_ref, after_ref, *refs):
    del after_ref
    others, (out_hbm, both_ref, out_ref, out_sems) = refs[:-4], refs[-4:]
    count = rows_ref.shape[0]
    if others:
        vis_ref, pos_ref = others
        both_ref[:count, :] = rows_ref[...]
        cosv, sinv = rope_tables(pos_ref)
        turn(vis_ref, both_ref.at[count:, :], per_group(cosv), per_group(sinv))
    else:
        both_ref = rows_ref
    stores = Stores(out_ref, out_hbm, out_sems)
    for at in stores.pieces():
        out_ref[at, :] = jnp.dot(place_ref[at, :], both_ref[...], preferred_element_type=F32).astype(BF16)
        stores.start(at)
    stores.wait()


class Stores:
    def __init__(self, source, target, sems):
        self.source, self.target, self.sems, self.copies = source, target, sems, []

    def pieces(self):
        size = self.source.shape[0] // PIECES
        return [slice(n * size, (n + 1) * size) for n in range(PIECES)]

    def start(self, at):
        sem = self.sems.at[len(self.copies)]
        copy = pltpu.make_async_copy(self.source.at[at, :], self.target.at[at, :], sem)
        copy.start()
        self.copies.append(copy)

    def wait(self):
        for copy in self.copies:
            copy.wait()


def fill_tables(pos_ref, dest_ref, table_refs, tiles, heads, local, sides):
    cos_ref, sin_ref, gather_ref, valid_ref, *order_refs = table_refs
    tokens = pos_ref.shape[1]
    seq = heads * tiles * C
    total = seq * local
    cosv, sinv = rope_tables(pos_ref)
    cos_ref[...] = per_group(cosv)
    sin_ref[...] = per_group(sinv)
    place = placement(dest_ref, tokens, tiles, local, sides, total)
    gather_ref[...] = jnp.transpose(place).astype(BF16)
    mine = lax.axis_index("tile")
    slot = iota((seq, LANES), 0)
    device = ((slot // C) % tiles) * heads + slot // (tiles * C)

    def tally(block, sums):
        hit = (dest_ref[pl.ds(block, 1), :] == mine).astype(F32).astype(BF16)
        source = (block * LANES + iota((seq, LANES), 1)) // tokens
        return sums + nt((source == device).astype(F32).astype(BF16), jnp.broadcast_to(hit, (LANES, LANES)))

    counts = lax.fori_loop(0, dest_ref.shape[0], tally, jnp.zeros((seq, LANES), F32))
    valid_ref[...] = (counts > (slot % C).astype(F32)).astype(F32)
    if order_refs:
        for ref, dim in zip(order_refs, (1, 0)):
            at = iota((total, total), dim)
            head, unit, side, rank, group = row_parts(at, tiles, local, sides)
            by_group = group * seq + (head * tiles + unit * sides + side) * C + rank
            ref[...] = (by_group == iota((total, total), 1 - dim)).astype(BF16)


def split_cots(cot_ref, own_ref, other_ref, local):
    head = lax.axis_index("head")
    total, count = own_ref.shape[0], cot_ref.shape[0]
    slots = total // local
    row, lane = iota((total, count), 0), iota((total, count), 1)
    base = (row % slots) * KV + row // slots
    cot = cot_ref[...]
    for ref, group in ((own_ref, head), (other_ref, 1 - head)):
        pick = (lane == base + group * local).astype(BF16)
        ref[...] = jnp.dot(pick, cot, preferred_element_type=F32).astype(BF16)


def is_late(sides):
    return lax.axis_index("tile") % sides == 0


def early_kernel(cot_hbm, pos_hbm, dest_hbm, *refs, tiles, heads, local, sides):
    *out_refs, cot_ref, pos_ref, dest_ref, sems = refs

    @pl.when(is_late(sides))
    def _():
        pairs = ((dest_hbm, dest_ref), (pos_hbm, pos_ref), (cot_hbm, cot_ref))
        loads = [pltpu.make_async_copy(a, b, sems.at[n]) for n, (a, b) in enumerate(pairs)]
        for load in loads:
            load.start()
        for load in loads:
            load.wait()
        split_cots(cot_ref, *out_refs[:2], local)
        fill_tables(pos_ref, dest_ref, out_refs[2:], tiles, heads, local, sides)


def table_kernel(pos_ref, dest_ref, after_ref, *refs, tiles, heads, local, sides):
    del after_ref
    if sides == 1:
        fill_tables(pos_ref, dest_ref, refs, tiles, heads, local, sides)
        return
    early_refs, out_refs = refs[: len(refs) // 2], refs[len(refs) // 2 :]

    @pl.when(is_late(sides))
    def _():
        for from_ref, to_ref in zip(early_refs, out_refs):
            to_ref[...] = from_ref[...]

    @pl.when(jnp.logical_not(is_late(sides)))
    def _():
        fill_tables(pos_ref, dest_ref, out_refs, tiles, heads, local, sides)


def split_kernel(cot_ref, own_early, other_early, own_ref, other_ref, *, local, sides):
    @pl.when(is_late(sides))
    def _():
        own_ref[...] = own_early[...]
        other_ref[...] = other_early[...]

    @pl.when(jnp.logical_not(is_late(sides)))
    def _():
        split_cots(cot_ref, own_ref, other_ref, local)


def join_kernel(valid_ref, *refs, local):
    cot_refs, (out_ref, whole) = refs[:-2], refs[-2:]
    seq = valid_ref.shape[0]
    block = min(BLOCK, seq)
    if len(cot_refs) == 2:
        half = seq // 2
        head = lax.axis_index("head")
        for ref, place in zip(cot_refs, (head, 1 - head)):
            for g in range(local):
                at = pl.multiple_of(g * seq + place * half, half)
                whole[pl.ds(at, half), :] = ref[g * half : (g + 1) * half, :]
    else:
        whole[...] = cot_refs[0][...]
    for first in range(0, seq, block):
        ok = valid_ref[first : first + block, :] > 0.0
        for g in range(local):
            for q in range(QPK):
                part = whole[g * seq + first : g * seq + first + block, q * HD : (q + 1) * HD]
                at = (g * seq + first) * QPK + q * block
                out_ref[at : at + block, :] = jnp.where(ok, part.astype(F32), 0.0).astype(BF16)


def attend_kernel(rows_ref, valid_ref, cot_ref, *refs, local):
    order_refs, (out_ref, rows_at, grads_at, sums_at) = refs[:-4], refs[-4:]
    total, width = rows_ref.shape
    seq = total // local
    block = min(BLOCK, seq)
    wide = QPK * block
    qcols = QPK * HD
    scale = HD ** (-0.5)
    if order_refs:
        for at in range(0, width, 2 * HD):
            cols = slice(at, at + 2 * HD)
            rows_at[:, cols] = jnp.dot(
                order_refs[0][...], rows_ref[:, cols], preferred_element_type=F32
            ).astype(BF16)
    else:
        rows_at, grads_at = rows_ref, out_ref
    key_ok = jnp.where(valid_ref[:, :1] > 0.0, 0.0, NEG)

    every = [slice(group * seq, (group + 1) * seq) for group in range(local)]

    def step(first):
        seen = iota((seq, wide), 0) <= first + iota((seq, wide), 1) % block
        bias = jnp.where(seen, key_ok, NEG)
        rows = [pl.ds(group * seq + first, block) for group in range(local)]
        keys = [rows_at[at, qcols : qcols + HD] for at in every]
        values = [rows_at[at, qcols + HD :] for at in every]
        queries = [
            jnp.concatenate([rows_at[at, q * HD : (q + 1) * HD] for q in range(QPK)], 0) for at in rows
        ]
        cots = [cot_ref[pl.ds((group * seq + first) * QPK, wide), :] for group in range(local)]
        scores = [nt(key, query) * scale + bias for key, query in zip(keys, queries)]
        dprobs = [nt(value, cot) for value, cot in zip(values, cots)]
        weights = [jnp.exp(x - jnp.max(x, axis=0, keepdims=True)) for x in scores]
        probs = [
            (x * (1.0 / jnp.sum(x, axis=0, keepdims=True))).astype(BF16) for x in weights
        ]
        broad = [x.astype(F32) for x in probs]
        deltas = [jnp.sum(x * y, axis=0, keepdims=True) for x, y in zip(broad, dprobs)]
        dscores = [(x * (y - z)).astype(BF16) for x, y, z in zip(broad, dprobs, deltas)]
        for at, dscore, key in zip(rows, dscores, keys):
            dquery = lax.dot_general(
                dscore, key, (((0,), (0,)), ((), ())), preferred_element_type=F32
            )
            dquery = (dquery * scale).astype(BF16)
            for q in range(QPK):
                grads_at[at, q * HD : (q + 1) * HD] = dquery[q * block : (q + 1) * block]
        dkeys = [jnp.dot(x, y, preferred_element_type=F32) for x, y in zip(dscores, queries)]
        dvalues = [jnp.dot(x, y, preferred_element_type=F32) for x, y in zip(probs, cots)]
        return dkeys, dvalues

    if seq == block:
        dkeys, dvalues = step(0)
    else:
        sums_at[...] = jnp.zeros(sums_at.shape, F32)

        @pl.loop(0, seq // block)
        def _(index):
            dkeys, dvalues = step(pl.multiple_of(index * block, block))
            for group, at in enumerate(every):
                sums_at[at, :HD] += dkeys[group]
                sums_at[at, HD:] += dvalues[group]

        dkeys, dvalues = [sums_at[at, :HD] for at in every], [sums_at[at, HD:] for at in every]
    for at, dkey, dvalue in zip(every, dkeys, dvalues):
        grads_at[at, qcols : qcols + HD] = (dkey * scale).astype(BF16)
        grads_at[at, qcols + HD :] = dvalue.astype(BF16)
    if order_refs:
        for at in range(0, width, 2 * HD):
            cols = slice(at, at + 2 * HD)
            out_ref[:, cols] = jnp.dot(
                order_refs[1][...], grads_at[:, cols], preferred_element_type=F32
            ).astype(BF16)


def gather_kernel(rows_ref, gather_ref, out_ref, *, part):
    count = out_ref.shape[0]
    pick = gather_ref[part * count : (part + 1) * count, :]
    out_ref[...] = jnp.dot(pick, rows_ref[...], preferred_element_type=F32).astype(BF16)


def finish_kernel(cos_ref, sin_ref, *refs):
    parts, (out_hbm, out_ref, out_sems) = refs[:-3], refs[-3:]
    stores = Stores(out_ref, out_hbm, out_sems)
    for at in stores.pieces():
        cosv, sinv = cos_ref[at, :], sin_ref[at, :]
        for first in range(0, out_ref.shape[1], HD):
            cols = slice(first, first + HD)
            x = sum(ref[at, cols].astype(F32) for ref in parts)
            if first < (QPK + 1) * HD:
                x = x * cosv - pltpu.roll(x, HD // 2, 1) * sinv
            out_ref[at, cols] = x.astype(BF16)
        stores.start(at)
    stores.wait()


def call(kernel, outs, *args, scratch=(), specs=None, out_spec=VMEM):
    shapes = [jax.ShapeDtypeStruct(s, d) for s, d in outs]
    single = len(shapes) == 1
    return pl.pallas_call(
        kernel,
        out_shape=shapes[0] if single else shapes,
        in_specs=specs or [VMEM] * len(args),
        out_specs=out_spec if single else [out_spec] * len(shapes),
        scratch_shapes=list(scratch),
        compiler_params=pltpu.CompilerParams(vmem_limit_bytes=48 * 2**20),
    )(*args)


def body(vision_rows, positions, destination, out_grad):
    tiles = lax.axis_size("tile")
    heads = lax.axis_size("head")
    tokens, groups, width = vision_rows.shape
    local = groups // heads
    count = tokens * groups
    seq = heads * tiles * C
    total = seq * local
    qcols = QPK * HD
    sides = 2 if heads == 2 and tiles % 2 == 0 else 1
    targets = destination.reshape(-1, LANES)
    rows = vision_rows.reshape(count, width)
    kernel = functools.partial

    def to_pair(x):
        return lax.ppermute(x, "tile", [(t, t ^ 1) for t in range(tiles)])

    others = [to_pair(rows), to_pair(positions)] if sides == 2 else []
    turned, place = call(
        kernel(ready_kernel, tiles=tiles, local=local, sides=sides),
        [((count, width), BF16), ((total, sides * count), BF16)],
        *(pltpu.with_memory_space_constraint(x, pltpu.HBM) for x in (rows, positions, targets)),
        specs=[HBM] * 3,
        scratch=(
            pltpu.VMEM(rows.shape, BF16),
            pltpu.VMEM(positions.shape, jnp.int32),
            pltpu.VMEM(targets.shape, jnp.int32),
            pltpu.SemaphoreType.DMA((3,)),
        ),
    )
    slots = out_grad.shape[0]
    cot_rows = out_grad.reshape(slots * groups, qcols)
    split_outs = [((slots * local, qcols), BF16)] * 2
    table_outs = [
        ((count, HD), F32),
        ((count, HD), F32),
        ((sides * count, total), BF16),
        ((seq, LANES), F32),
    ] + [((total, total), BF16)] * (2 if local * sides > 1 else 0)
    early = []
    if sides == 2:
        early = call(
            kernel(early_kernel, tiles=tiles, heads=heads, local=local, sides=sides),
            split_outs + table_outs,
            *(pltpu.with_memory_space_constraint(x, pltpu.HBM) for x in (cot_rows, positions, targets)),
            specs=[HBM] * 3,
            scratch=(
                pltpu.VMEM(cot_rows.shape, BF16),
                pltpu.VMEM(positions.shape, jnp.int32),
                pltpu.VMEM(targets.shape, jnp.int32),
                pltpu.SemaphoreType.DMA((3,)),
            ),
        )
    outgoing = call(
        pack_kernel,
        [((total, width), BF16)],
        turned,
        place,
        early[0][:16, :LANES] if early else place[:16, :LANES],
        *others,
        out_spec=HBM,
        scratch=(
            pltpu.VMEM((sides * count, width), BF16),
            pltpu.VMEM((total, width), BF16),
            pltpu.SemaphoreType.DMA((PIECES,)),
        ),
    )

    def swap(rows):
        units = tiles // sides
        parts = rows.reshape(heads * units, -1, width)
        if sides == 1:
            axes, groups = ("head", "tile"), None
        else:
            axes, order = ("tile", "head"), unit_order(units, sides)
            groups = [
                [(unit * sides + side) * heads + head for head in range(heads) for unit in order]
                for side in range(sides)
            ]
        parts = lax.all_to_all(
            parts, axes, split_axis=0, concat_axis=0, tiled=True, axis_index_groups=groups
        )
        return parts.reshape(total, width)

    incoming = swap(outgoing)
    if sides == 2:
        own, other = call(kernel(split_kernel, local=local, sides=sides), split_outs, cot_rows, *early[:2])
        cots = [own, lax.ppermute(other, "head", [(0, 1), (1, 0)])]
    else:
        moved = lax.all_to_all(out_grad, "head", split_axis=1, concat_axis=0, tiled=True)
        cots = [jnp.swapaxes(moved, 0, 1).reshape(total, qcols)]
    cosv, sinv, gather, valid, *orders = call(
        kernel(table_kernel, tiles=tiles, heads=heads, local=local, sides=sides),
        table_outs,
        positions,
        targets,
        outgoing[:16, :LANES],
        *early[2:],
    )
    cot = call(
        kernel(join_kernel, local=local),
        [((total * QPK, HD), BF16)],
        valid,
        *cots,
        scratch=(pltpu.VMEM((total, qcols), BF16),),
    )
    grads = call(
        kernel(attend_kernel, local=local),
        [((total, width), BF16)],
        incoming,
        valid,
        cot,
        *orders,
        scratch=(
            pltpu.VMEM((total, width), BF16),
            pltpu.VMEM((total, width), BF16),
            pltpu.VMEM((total, 2 * HD) if seq > BLOCK else (8, 2 * HD), F32),
        ),
    )
    back = swap(grads)

    def gathered(part):
        return call(kernel(gather_kernel, part=part), [((count, width), BF16)], back, gather)

    parts = [to_pair(gathered(1))] if sides == 2 else []
    parts.append(gathered(0))
    result = call(
        finish_kernel,
        [((count, width), BF16)],
        cosv,
        sinv,
        *parts,
        out_spec=HBM,
        scratch=(pltpu.VMEM((count, width), BF16), pltpu.SemaphoreType.DMA((PIECES,))),
    )
    return result.reshape(tokens, groups, width)


def solution(mesh):
    return jax.shard_map(
        body,
        mesh=mesh,
        in_specs=(
            P(("tile", "head"), None, None),
            P(None, ("tile", "head")),
            P(),
            P(("tile", "head"), None, None),
        ),
        out_specs=P(("tile", "head"), None, None),
        check_vma=False,
    )
```

```python
import functools
import math

import jax
import jax.numpy as jnp
from jax import lax
from jax.experimental import pallas as pl
from jax.experimental.pallas import tpu as pltpu
from jax.sharding import PartitionSpec as P

KV = 8
HD = 128
C = 2
QPK = 4
LANES = 128
BLOCK = 64
PIECES = 2
F32 = jnp.float32
BF16 = jnp.bfloat16
NEG = -1e30
VMEM = pl.BlockSpec(memory_space=pltpu.VMEM)
HBM = pl.BlockSpec(memory_space=pltpu.HBM)


def nt(a, b):
    return lax.dot_general(a, b, (((1,), (1,)), ((), ())), preferred_element_type=F32)


def iota(shape, dim):
    return lax.broadcasted_iota(jnp.int32, shape, dim)


def over(at, size):
    if size & (size - 1):
        return at // size
    return lax.shift_right_logical(at, jnp.int32(size.bit_length() - 1))


def rest(at, size):
    return at % size if size & (size - 1) else at & (size - 1)


def rope_tables(pos_ref):
    tokens = pos_ref.shape[1]
    half = HD // 2
    slots = rest(iota((tokens, HD), 1), half)
    first = half // 4
    second = (half - first) // 2
    eye = (iota((tokens, tokens), 0) == iota((tokens, tokens), 1)).astype(BF16)
    column = [
        nt(eye, jnp.broadcast_to(pos_ref[s : s + 1, :].astype(F32).astype(BF16), (HD, tokens)))
        for s in range(3)
    ]
    chosen = jnp.where(
        slots < first, column[0], jnp.where(slots < first + second, column[1], column[2])
    )
    freq = jnp.exp(-(2.0 * slots.astype(F32) / HD) * math.log(1000000.0))
    angle = chosen * freq
    sign = jnp.where(iota((tokens, HD), 1) < half, -1.0, 1.0)
    return jnp.cos(angle), jnp.sin(angle) * sign


def per_group(table):
    tokens = table.shape[0]
    return jnp.broadcast_to(table[:, None, :], (tokens, KV, HD)).reshape(tokens * KV, HD)


def token_slots(dest_ref, tokens, tile):
    start = (tile * lax.axis_size("head") + lax.axis_index("head")) * tokens
    count = tokens * KV
    off = start % LANES
    row = dest_ref[pl.ds(start // LANES, 1), :].astype(F32).astype(BF16)
    wide = (iota((count, LANES), 1) == off + over(iota((count, LANES), 0), KV)).astype(BF16)
    narrow = (iota((tokens, LANES), 1) == off + iota((tokens, LANES), 0)).astype(BF16)
    along = nt(jnp.broadcast_to(row, (8, LANES)), wide)[:1]
    down = nt(narrow, jnp.broadcast_to(row, (count, LANES)))
    lane = iota((tokens, count), 1)
    earlier = (down == along) & (iota((tokens, count), 0) < over(lane, KV))
    rank = jnp.sum(earlier.astype(F32), axis=0, keepdims=True)
    return (along * C + rank).astype(jnp.int32)


def row_parts(at, tiles, local, sides):
    rank, at = rest(at, C), over(at, C)
    side, at = rest(at, sides), over(at, sides)
    group, at = rest(at, local), over(at, local)
    units = tiles // sides
    order = unit_order(units, sides)
    place, head = rest(at, units), over(at, units)
    unit = place
    if order != list(range(units)):
        unit = sum(jnp.where(place == n, order[n], 0) for n in range(units))
    return head, unit, side, rank, group


def unit_order(units, sides):
    if sides == 2 and units == 8:
        return [z * 2 + y for y in (0, 1) for z in (2, 1, 0, 3)]
    return list(range(units))


def placement(dest_ref, tokens, tiles, local, sides, total):
    count = tokens * KV
    tile = lax.axis_index("tile")
    side = tile % sides
    head, unit, at_side, rank, group = row_parts(iota((total, LANES), 0), tiles, local, sides)
    target = unit * sides + side
    rows = (((target * C + rank) * sides + at_side) * KV + head * local + group)[:, :1]
    parts = []
    for other in range(sides):
        from_side = side + other - 2 * side * other
        slots = token_slots(dest_ref, tokens, tile - side + from_side)
        lanes = (slots * sides + from_side) * KV + rest(iota((1, count), 1), KV)
        parts.append((rows == lanes).astype(F32))
    return parts[0] if sides == 1 else jnp.concatenate(parts, 1)


def ready_kernel(
    vis_hbm, pos_hbm, dest_hbm, rows_ref, place_ref, vis_ref, pos_ref, dest_ref, sems, *, tiles, local, sides
):
    pairs = ((dest_hbm, dest_ref), (pos_hbm, pos_ref), (vis_hbm, vis_ref))
    loads = [pltpu.make_async_copy(a, b, sems.at[n]) for n, (a, b) in enumerate(pairs)]
    for load in loads:
        load.start()
    tokens = pos_ref.shape[1]
    loads[0].wait()
    place_ref[...] = placement(dest_ref, tokens, tiles, local, sides, place_ref.shape[0]).astype(BF16)
    loads[1].wait()
    cosv, sinv = rope_tables(pos_ref)
    loads[2].wait()
    turn(vis_ref, rows_ref, per_group(cosv), per_group(sinv))


def turn(from_ref, to_ref, cosv, sinv):
    for at in range(0, from_ref.shape[1], HD):
        x = from_ref[:, at : at + HD]
        if at < (QPK + 1) * HD:
            x = x.astype(F32)
            x = (x * cosv + pltpu.roll(x, HD // 2, 1) * sinv).astype(BF16)
        to_ref[:, at : at + HD] = x


def pack_kernel(rows_ref, place_ref, after_ref, *refs):
    del after_ref
    others, (out_hbm, both_ref, out_ref, out_sems) = refs[:-4], refs[-4:]
    count = rows_ref.shape[0]
    if others:
        vis_ref, pos_ref = others
        both_ref[:count, :] = rows_ref[...]
        cosv, sinv = rope_tables(pos_ref)
        turn(vis_ref, both_ref.at[count:, :], per_group(cosv), per_group(sinv))
    else:
        both_ref = rows_ref
    stores = Stores(out_ref, out_hbm, out_sems)
    for at in stores.pieces():
        out_ref[at, :] = jnp.dot(place_ref[at, :], both_ref[...], preferred_element_type=F32).astype(BF16)
        stores.start(at)
    stores.wait()


class Stores:
    def __init__(self, source, target, sems):
        self.source, self.target, self.sems, self.copies = source, target, sems, []

    def pieces(self):
        size = self.source.shape[0] // PIECES
        return [slice(n * size, (n + 1) * size) for n in range(PIECES)]

    def start(self, at):
        sem = self.sems.at[len(self.copies)]
        copy = pltpu.make_async_copy(self.source.at[at, :], self.target.at[at, :], sem)
        copy.start()
        self.copies.append(copy)

    def wait(self):
        for copy in self.copies:
            copy.wait()


def fill_tables(pos_ref, dest_ref, table_refs, tiles, heads, local, sides):
    cos_ref, sin_ref, gather_ref, pick_ref, bias_ref = table_refs
    tokens = pos_ref.shape[1]
    seq = heads * tiles * C
    cosv, sinv = rope_tables(pos_ref)
    cos_ref[...] = per_group(cosv)
    sin_ref[...] = per_group(sinv)
    place = placement(dest_ref, tokens, tiles, local, sides, seq * local)
    gather_ref[...] = jnp.transpose(place).astype(BF16)
    mine = lax.axis_index("tile")

    def slot_of(at):
        head, unit, side, rank, _ = row_parts(at, tiles, 1, sides)
        return (head * tiles + unit * sides + side) * C + rank

    slot = slot_of(iota((seq, LANES), 0))
    device = rest(over(slot, C), tiles) * heads + over(slot, tiles * C)

    def tally(block, sums):
        hit = (dest_ref[pl.ds(block, 1), :] == mine).astype(F32).astype(BF16)
        source = over(block * LANES + iota((seq, LANES), 1), tokens)
        return sums + nt((source == device).astype(F32).astype(BF16), jnp.broadcast_to(hit, (LANES, LANES)))

    counts = lax.fori_loop(0, dest_ref.shape[0], tally, jnp.zeros((seq, LANES), F32))
    taken = counts > rest(slot, C).astype(F32)
    pick_ref[...] = ((slot[:, :1] == iota((seq, seq), 1)) & taken[:, :1]).astype(F32).astype(BF16)
    key_ok = jnp.where(taken, 0.0, NEG)
    if bias_ref.shape[1] == LANES:
        bias_ref[...] = key_ok
    else:
        query = slot_of(rest(iota(bias_ref.shape, 1), seq))
        bias_ref[...] = jnp.where(slot[:, :1] <= query, key_ok[:, :1], NEG)


def split_cots(cot_ref, own_ref, other_ref, local):
    head = lax.axis_index("head")
    total, count = own_ref.shape[0], cot_ref.shape[0]
    slots = total // local
    row, lane = iota((total, count), 0), iota((total, count), 1)
    base = rest(row, slots) * KV + over(row, slots)
    cot = cot_ref[...]
    for ref, group in ((own_ref, head), (other_ref, 1 - head)):
        pick = (lane == base + group * local).astype(BF16)
        ref[...] = jnp.dot(pick, cot, preferred_element_type=F32).astype(BF16)


def is_late(sides):
    return lax.axis_index("tile") % sides == 0


def early_kernel(cot_hbm, pos_hbm, dest_hbm, *refs, tiles, heads, local, sides):
    *out_refs, cot_ref, pos_ref, dest_ref, sems = refs

    @pl.when(is_late(sides))
    def _():
        pairs = ((dest_hbm, dest_ref), (pos_hbm, pos_ref), (cot_hbm, cot_ref))
        loads = [pltpu.make_async_copy(a, b, sems.at[n]) for n, (a, b) in enumerate(pairs)]
        for load in loads:
            load.start()
        for load in loads:
            load.wait()
        split_cots(cot_ref, *out_refs[:2], local)
        fill_tables(pos_ref, dest_ref, out_refs[2:], tiles, heads, local, sides)


def table_kernel(pos_ref, dest_ref, after_ref, *refs, tiles, heads, local, sides):
    del after_ref
    if sides == 1:
        fill_tables(pos_ref, dest_ref, refs, tiles, heads, local, sides)
        return
    early_refs, out_refs = refs[: len(refs) // 2], refs[len(refs) // 2 :]

    @pl.when(is_late(sides))
    def _():
        for from_ref, to_ref in zip(early_refs, out_refs):
            to_ref[...] = from_ref[...]

    @pl.when(jnp.logical_not(is_late(sides)))
    def _():
        fill_tables(pos_ref, dest_ref, out_refs, tiles, heads, local, sides)


def split_kernel(cot_ref, own_early, other_early, own_ref, other_ref, *, local, sides):
    @pl.when(is_late(sides))
    def _():
        own_ref[...] = own_early[...]
        other_ref[...] = other_early[...]

    @pl.when(jnp.logical_not(is_late(sides)))
    def _():
        split_cots(cot_ref, own_ref, other_ref, local)


def join_kernel(pick_ref, *refs, local):
    cot_refs, (out_ref, whole) = refs[:-2], refs[-2:]
    seq = pick_ref.shape[0]
    block = min(BLOCK, seq)
    if len(cot_refs) == 2:
        half = seq // 2
        head = lax.axis_index("head")
        for ref, place in zip(cot_refs, (head, 1 - head)):
            for g in range(local):
                at = pl.multiple_of(g * seq + place * half, half)
                whole[pl.ds(at, half), :] = ref[g * half : (g + 1) * half, :]
    else:
        whole[...] = cot_refs[0][...]
    for first in range(0, seq, block):
        pick = pick_ref[first : first + block, :]
        for g in range(local):
            rows = whole[g * seq : (g + 1) * seq, :]
            part = jnp.dot(pick, rows, preferred_element_type=F32).astype(BF16)
            for q in range(QPK):
                at = (g * seq + first) * QPK + q * block
                out_ref[at : at + block, :] = part[:, q * HD : (q + 1) * HD]


def trade_halves(a, b):
    first = iota(a.shape, 1) < 4
    return jnp.where(first, a, pltpu.roll(b, 4, 1)), jnp.where(first, pltpu.roll(a, 4, 1), b)


def by_group(rows, local):
    if local == 1:
        return [rows]
    total, width = rows.shape
    tiles = rows.astype(F32).reshape(total // (8 * local), 2, local // 2, 8, width)
    parts = []
    for pair in range(local // 2):
        for x in trade_halves(tiles[:, 0, pair], tiles[:, 1, pair]):
            parts.append(x.reshape(total // local, width).astype(BF16))
    return parts


def by_place(parts):
    if len(parts) == 1:
        return parts[0]
    rows, width = parts[0].shape
    tiles = [x.reshape(rows // 8, 8, width) for x in parts]
    pairs = [trade_halves(tiles[n], tiles[n + 1]) for n in range(0, len(parts), 2)]
    whole = jnp.stack([jnp.stack([pair[side] for pair in pairs], 1) for side in range(2)], 1)
    return whole.reshape(rows * len(parts), width)


def attend_kernel(rows_ref, bias_ref, cot_ref, out_ref, sums_at, *, local):
    total, width = rows_ref.shape
    seq = total // local
    block = min(BLOCK, seq)
    wide = QPK * block
    qcols = QPK * HD
    scale = HD ** (-0.5)

    def step(first, arrived, bias):
        at = slice(0, block) if seq == block else pl.ds(first, block)
        keys = [x[:, qcols : qcols + HD] for x in arrived]
        values = [x[:, qcols + HD :] for x in arrived]
        asked = arrived if seq == block else [rows_ref[at, :]]
        queries = [jnp.concatenate([x[:, q * HD : (q + 1) * HD] for q in range(QPK)], 0) for x in asked]
        cots = [cot_ref[pl.ds((group * seq + first) * QPK, wide), :] for group in range(local)]
        scores = [nt(key, query) * (scale * math.log2(math.e)) + bias for key, query in zip(keys, queries)]
        dprobs = [nt(value, cot) for value, cot in zip(values, cots)]
        weights = [jnp.exp2(x - jnp.max(x, axis=0, keepdims=True)) for x in scores]
        probs = [(x * (1.0 / jnp.sum(x, axis=0, keepdims=True))).astype(BF16) for x in weights]
        broad = [x.astype(F32) for x in probs]
        deltas = [jnp.sum(x * y, axis=0, keepdims=True) for x, y in zip(broad, dprobs)]
        dscores = [(x * (y - z)).astype(BF16) for x, y, z in zip(broad, dprobs, deltas)]
        dqueries = [
            lax.dot_general(x, y, (((0,), (0,)), ((), ())), preferred_element_type=F32) * scale
            for x, y in zip(dscores, keys)
        ]
        dqueries = [
            jnp.concatenate([x[q * block : (q + 1) * block] for q in range(QPK)], 1) for x in dqueries
        ]
        dkeys = [jnp.dot(x, y, preferred_element_type=F32) for x, y in zip(dscores, queries)]
        dvalues = [jnp.dot(x, y, preferred_element_type=F32) for x, y in zip(probs, cots)]
        return dqueries, dkeys, dvalues

    if seq == block:
        arrived = by_group(rows_ref[...], local)
        terms = zip(*step(0, arrived, bias_ref[...]))
        parts = [jnp.concatenate([x, y * scale, z], 1) for x, y, z in terms]
        out_ref[...] = by_place(parts).astype(BF16)
        return
    sums_at[...] = jnp.zeros(sums_at.shape, F32)

    @pl.loop(0, seq // block)
    def _(index):
        first = pl.multiple_of(index * block, block)
        seen = iota((seq, wide), 0) <= first + rest(iota((seq, wide), 1), block)
        bias = jnp.where(seen, bias_ref[:, :1], NEG)
        (dquery,), (dkey,), (dvalue,) = step(first, [rows_ref[...]], bias)
        out_ref[pl.ds(first, block), :qcols] = dquery.astype(BF16)
        sums_at[:, :HD] += dkey
        sums_at[:, HD:] += dvalue

    out_ref[:, qcols : qcols + HD] = (sums_at[:, :HD] * scale).astype(BF16)
    out_ref[:, qcols + HD :] = sums_at[:, HD:].astype(BF16)


def gather_kernel(rows_ref, gather_ref, out_ref, *, part):
    count = out_ref.shape[0]
    pick = gather_ref[part * count : (part + 1) * count, :]
    out_ref[...] = jnp.dot(pick, rows_ref[...], preferred_element_type=F32).astype(BF16)


def finish_kernel(cos_ref, sin_ref, *refs):
    parts, (out_hbm, out_ref, out_sems) = refs[:-3], refs[-3:]
    stores = Stores(out_ref, out_hbm, out_sems)
    for at in stores.pieces():
        cosv, sinv = cos_ref[at, :], sin_ref[at, :]
        for first in range(0, out_ref.shape[1], HD):
            cols = slice(first, first + HD)
            x = sum(ref[at, cols].astype(F32) for ref in parts)
            if first < (QPK + 1) * HD:
                x = x * cosv - pltpu.roll(x, HD // 2, 1) * sinv
            out_ref[at, cols] = x.astype(BF16)
        stores.start(at)
    stores.wait()


def call(kernel, outs, *args, scratch=(), specs=None, out_spec=VMEM):
    shapes = [jax.ShapeDtypeStruct(s, d) for s, d in outs]
    single = len(shapes) == 1
    return pl.pallas_call(
        kernel,
        out_shape=shapes[0] if single else shapes,
        in_specs=specs or [VMEM] * len(args),
        out_specs=out_spec if single else [out_spec] * len(shapes),
        scratch_shapes=list(scratch),
        compiler_params=pltpu.CompilerParams(vmem_limit_bytes=48 * 2**20),
    )(*args)


def body(vision_rows, positions, destination, out_grad):
    tiles = lax.axis_size("tile")
    heads = lax.axis_size("head")
    tokens, groups, width = vision_rows.shape
    local = groups // heads
    count = tokens * groups
    seq = heads * tiles * C
    total = seq * local
    qcols = QPK * HD
    sides = 2 if heads == 2 and tiles % 2 == 0 else 1
    targets = destination.reshape(-1, LANES)
    rows = vision_rows.reshape(count, width)
    kernel = functools.partial

    def to_pair(x):
        return lax.ppermute(x, "tile", [(t, t ^ 1) for t in range(tiles)])

    others = [to_pair(rows), to_pair(positions)] if sides == 2 else []
    turned, place = call(
        kernel(ready_kernel, tiles=tiles, local=local, sides=sides),
        [((count, width), BF16), ((total, sides * count), BF16)],
        *(pltpu.with_memory_space_constraint(x, pltpu.HBM) for x in (rows, positions, targets)),
        specs=[HBM] * 3,
        scratch=(
            pltpu.VMEM(rows.shape, BF16),
            pltpu.VMEM(positions.shape, jnp.int32),
            pltpu.VMEM(targets.shape, jnp.int32),
            pltpu.SemaphoreType.DMA((3,)),
        ),
    )
    slots = out_grad.shape[0]
    cot_rows = out_grad.reshape(slots * groups, qcols)
    split_outs = [((slots * local, qcols), BF16)] * 2
    table_outs = [
        ((count, HD), F32),
        ((count, HD), F32),
        ((sides * count, total), BF16),
        ((seq, seq), BF16),
        ((seq, QPK * BLOCK if sides == 2 and seq == BLOCK else LANES), F32),
    ]
    early = []
    if sides == 2:
        early = call(
            kernel(early_kernel, tiles=tiles, heads=heads, local=local, sides=sides),
            split_outs + table_outs,
            *(pltpu.with_memory_space_constraint(x, pltpu.HBM) for x in (cot_rows, positions, targets)),
            specs=[HBM] * 3,
            scratch=(
                pltpu.VMEM(cot_rows.shape, BF16),
                pltpu.VMEM(positions.shape, jnp.int32),
                pltpu.VMEM(targets.shape, jnp.int32),
                pltpu.SemaphoreType.DMA((3,)),
            ),
        )
    outgoing = call(
        pack_kernel,
        [((total, width), BF16)],
        turned,
        place,
        early[0][:16, :LANES] if early else place[:16, :LANES],
        *others,
        out_spec=HBM,
        scratch=(
            pltpu.VMEM((sides * count, width), BF16),
            pltpu.VMEM((total, width), BF16),
            pltpu.SemaphoreType.DMA((PIECES,)),
        ),
    )

    def swap(rows):
        units = tiles // sides
        parts = rows.reshape(heads * units, -1, width)
        if sides == 1:
            axes, groups = ("head", "tile"), None
        else:
            axes, order = ("tile", "head"), unit_order(units, sides)
            groups = [
                [(unit * sides + side) * heads + head for head in range(heads) for unit in order]
                for side in range(sides)
            ]
        parts = lax.all_to_all(
            parts, axes, split_axis=0, concat_axis=0, tiled=True, axis_index_groups=groups
        )
        return parts.reshape(total, width)

    incoming = swap(outgoing)
    if sides == 2:
        own, other = call(kernel(split_kernel, local=local, sides=sides), split_outs, cot_rows, *early[:2])
        cots = [own, lax.ppermute(other, "head", [(0, 1), (1, 0)])]
    else:
        moved = lax.all_to_all(out_grad, "head", split_axis=1, concat_axis=0, tiled=True)
        cots = [jnp.swapaxes(moved, 0, 1).reshape(total, qcols)]
    cosv, sinv, gather, pick, bias = call(
        kernel(table_kernel, tiles=tiles, heads=heads, local=local, sides=sides),
        table_outs,
        positions,
        targets,
        outgoing[:16, :LANES],
        *early[2:],
    )
    cot = call(
        kernel(join_kernel, local=local),
        [((total * QPK, HD), BF16)],
        pick,
        *cots,
        scratch=(pltpu.VMEM((total, qcols), BF16),),
    )
    grads = call(
        kernel(attend_kernel, local=local),
        [((total, width), BF16)],
        incoming,
        bias,
        cot,
        scratch=(pltpu.VMEM((seq if seq > BLOCK else 8, 2 * HD), F32),),
    )
    back = swap(grads)

    def gathered(part):
        return call(kernel(gather_kernel, part=part), [((count, width), BF16)], back, gather)

    parts = [to_pair(gathered(1))] if sides == 2 else []
    parts.append(gathered(0))
    result = call(
        finish_kernel,
        [((count, width), BF16)],
        cosv,
        sinv,
        *parts,
        out_spec=HBM,
        scratch=(pltpu.VMEM((count, width), BF16), pltpu.SemaphoreType.DMA((PIECES,))),
    )
    return result.reshape(tokens, groups, width)


def solution(mesh):
    return jax.shard_map(
        body,
        mesh=mesh,
        in_specs=(
            P(("tile", "head"), None, None),
            P(None, ("tile", "head")),
            P(),
            P(("tile", "head"), None, None),
        ),
        out_specs=P(("tile", "head"), None, None),
        check_vma=False,
    )
```

```python
import functools
import math

import jax
import jax.numpy as jnp
from jax import lax
from jax.experimental import pallas as pl
from jax.experimental.pallas import tpu as pltpu
from jax.sharding import PartitionSpec as P

KV = 8
HD = 128
C = 2
QPK = 4
LANES = 128
BLOCK = 64
PIECES = 2
F32 = jnp.float32
BF16 = jnp.bfloat16
NEG = -1e30
VMEM = pl.BlockSpec(memory_space=pltpu.VMEM)
HBM = pl.BlockSpec(memory_space=pltpu.HBM)


def nt(a, b):
    return lax.dot_general(a, b, (((1,), (1,)), ((), ())), preferred_element_type=F32)


def iota(shape, dim):
    return lax.broadcasted_iota(jnp.int32, shape, dim)


def over(at, size):
    if size & (size - 1):
        return at // size
    return lax.shift_right_logical(at, jnp.int32(size.bit_length() - 1))


def rest(at, size):
    return at % size if size & (size - 1) else at & (size - 1)


def rope_tables(pos_ref):
    tokens = pos_ref.shape[1]
    half = HD // 2
    slots = rest(iota((tokens, HD), 1), half)
    first = half // 4
    second = (half - first) // 2
    eye = (iota((tokens, tokens), 0) == iota((tokens, tokens), 1)).astype(BF16)
    column = [
        nt(eye, jnp.broadcast_to(pos_ref[s : s + 1, :].astype(F32).astype(BF16), (HD, tokens)))
        for s in range(3)
    ]
    chosen = jnp.where(
        slots < first, column[0], jnp.where(slots < first + second, column[1], column[2])
    )
    freq = jnp.exp(-(2.0 * slots.astype(F32) / HD) * math.log(1000000.0))
    angle = chosen * freq
    sign = jnp.where(iota((tokens, HD), 1) < half, -1.0, 1.0)
    return jnp.cos(angle), jnp.sin(angle) * sign


def per_group(table):
    tokens = table.shape[0]
    return jnp.broadcast_to(table[:, None, :], (tokens, KV, HD)).reshape(tokens * KV, HD)


def token_slots(dest_ref, tokens, tile):
    start = (tile * lax.axis_size("head") + lax.axis_index("head")) * tokens
    count = tokens * KV
    off = start % LANES
    row = dest_ref[pl.ds(start // LANES, 1), :].astype(F32).astype(BF16)
    wide = (iota((count, LANES), 1) == off + over(iota((count, LANES), 0), KV)).astype(BF16)
    narrow = (iota((tokens, LANES), 1) == off + iota((tokens, LANES), 0)).astype(BF16)
    along = nt(jnp.broadcast_to(row, (8, LANES)), wide)[:1]
    down = nt(narrow, jnp.broadcast_to(row, (count, LANES)))
    lane = iota((tokens, count), 1)
    earlier = (down == along) & (iota((tokens, count), 0) < over(lane, KV))
    rank = jnp.sum(earlier.astype(F32), axis=0, keepdims=True)
    return (along * C + rank).astype(jnp.int32)


def row_parts(at, tiles, local, sides):
    rank, at = rest(at, C), over(at, C)
    side, at = rest(at, sides), over(at, sides)
    group, at = rest(at, local), over(at, local)
    units = tiles // sides
    order = unit_order(units, sides)
    place, head = rest(at, units), over(at, units)
    unit = place
    if order != list(range(units)):
        unit = sum(jnp.where(place == n, order[n], 0) for n in range(units))
    return head, unit, side, rank, group


def unit_order(units, sides):
    if sides == 2 and units == 8:
        return [z * 2 + y for y in (0, 1) for z in (2, 1, 0, 3)]
    return list(range(units))


def placement(dest_ref, tokens, tiles, local, sides, total):
    count = tokens * KV
    tile = lax.axis_index("tile")
    side = tile % sides
    head, unit, at_side, rank, group = row_parts(iota((total, LANES), 0), tiles, local, sides)
    target = unit * sides + side
    rows = (((target * C + rank) * sides + at_side) * KV + head * local + group)[:, :1]
    parts = []
    for other in range(sides):
        from_side = side + other - 2 * side * other
        slots = token_slots(dest_ref, tokens, tile - side + from_side)
        lanes = (slots * sides + from_side) * KV + rest(iota((1, count), 1), KV)
        parts.append((rows == lanes).astype(F32))
    return parts[0] if sides == 1 else jnp.concatenate(parts, 1)


def ready_kernel(pos_hbm, dest_hbm, cos_ref, sin_ref, place_ref, pos_ref, dest_ref, sems, *, tiles, local, sides):
    pairs = ((dest_hbm, dest_ref), (pos_hbm, pos_ref))
    loads = [pltpu.make_async_copy(a, b, sems.at[n]) for n, (a, b) in enumerate(pairs)]
    for load in loads:
        load.start()
    tokens = pos_ref.shape[1]
    loads[0].wait()
    place_ref[...] = placement(dest_ref, tokens, tiles, local, sides, place_ref.shape[0]).astype(BF16)
    loads[1].wait()
    cos_ref[...], sin_ref[...] = rope_tables(pos_ref)


def turn(from_ref, to_ref, cosv, sinv):
    for at in range(0, from_ref.shape[1], HD):
        x = from_ref[:, at : at + HD]
        if at < (QPK + 1) * HD:
            x = x.astype(F32)
            x = (x * cosv + pltpu.roll(x, HD // 2, 1) * sinv).astype(BF16)
        to_ref[:, at : at + HD] = x


def pack_kernel(vis_ref, cos_ref, sin_ref, place_ref, after_ref, *refs):
    del after_ref
    others, (out_hbm, both_ref, out_ref, out_sems) = refs[:-4], refs[-4:]
    count = vis_ref.shape[0]
    turn(vis_ref, both_ref.at[:count, :], per_group(cos_ref[...]), per_group(sin_ref[...]))
    if others:
        vis_ref, pos_ref = others
        cosv, sinv = rope_tables(pos_ref)
        turn(vis_ref, both_ref.at[count:, :], per_group(cosv), per_group(sinv))
    stores = Stores(out_ref, out_hbm, out_sems)
    for at in stores.pieces():
        out_ref[at, :] = jnp.dot(place_ref[at, :], both_ref[...], preferred_element_type=F32).astype(BF16)
        stores.start(at)
    stores.wait()


class Stores:
    def __init__(self, source, target, sems):
        self.source, self.target, self.sems, self.copies = source, target, sems, []

    def pieces(self):
        size = self.source.shape[0] // PIECES
        return [slice(n * size, (n + 1) * size) for n in range(PIECES)]

    def start(self, at):
        sem = self.sems.at[len(self.copies)]
        copy = pltpu.make_async_copy(self.source.at[at, :], self.target.at[at, :], sem)
        copy.start()
        self.copies.append(copy)

    def wait(self):
        for copy in self.copies:
            copy.wait()


def fill_tables(pos_ref, dest_ref, table_refs, tiles, heads, local, sides):
    cos_ref, sin_ref, gather_ref, pick_ref, bias_ref = table_refs
    tokens = pos_ref.shape[1]
    seq = heads * tiles * C
    cosv, sinv = rope_tables(pos_ref)
    cos_ref[...] = per_group(cosv)
    sin_ref[...] = per_group(sinv)
    place = placement(dest_ref, tokens, tiles, local, sides, seq * local)
    gather_ref[...] = jnp.transpose(place).astype(BF16)
    mine = lax.axis_index("tile")

    def slot_of(at):
        head, unit, side, rank, _ = row_parts(at, tiles, 1, sides)
        return (head * tiles + unit * sides + side) * C + rank

    slot = slot_of(iota((seq, LANES), 0))
    device = rest(over(slot, C), tiles) * heads + over(slot, tiles * C)

    def tally(block, sums):
        hit = (dest_ref[pl.ds(block, 1), :] == mine).astype(F32).astype(BF16)
        source = over(block * LANES + iota((seq, LANES), 1), tokens)
        return sums + nt((source == device).astype(F32).astype(BF16), jnp.broadcast_to(hit, (LANES, LANES)))

    counts = lax.fori_loop(0, dest_ref.shape[0], tally, jnp.zeros((seq, LANES), F32))
    taken = counts > rest(slot, C).astype(F32)
    pick_ref[...] = ((slot[:, :1] == iota((seq, seq), 1)) & taken[:, :1]).astype(F32).astype(BF16)
    key_ok = jnp.where(taken, 0.0, NEG)
    if seq > BLOCK:
        bias_ref[...] = key_ok
    else:
        query = slot_of(rest(iota(bias_ref.shape, 1), seq))
        bias_ref[...] = jnp.where(slot[:, :1] <= query, key_ok[:, :1], NEG)


def split_cots(cot_ref, own_ref, other_ref, local):
    head = lax.axis_index("head")
    total, count = own_ref.shape[0], cot_ref.shape[0]
    slots = total // local
    row, lane = iota((total, count), 0), iota((total, count), 1)
    base = rest(row, slots) * KV + over(row, slots)
    cot = cot_ref[...]
    for ref, group in ((own_ref, head), (other_ref, 1 - head)):
        pick = (lane == base + group * local).astype(BF16)
        ref[...] = jnp.dot(pick, cot, preferred_element_type=F32).astype(BF16)


def is_late(sides):
    return lax.axis_index("tile") % sides == 0


def early_kernel(cot_hbm, pos_hbm, dest_hbm, *refs, tiles, heads, local, sides):
    *out_refs, cot_ref, pos_ref, dest_ref, sems = refs

    @pl.when(is_late(sides))
    def _():
        pairs = ((dest_hbm, dest_ref), (pos_hbm, pos_ref), (cot_hbm, cot_ref))
        loads = [pltpu.make_async_copy(a, b, sems.at[n]) for n, (a, b) in enumerate(pairs)]
        for load in loads:
            load.start()
        for load in loads:
            load.wait()
        split_cots(cot_ref, *out_refs[:2], local)
        fill_tables(pos_ref, dest_ref, out_refs[2:], tiles, heads, local, sides)


def table_kernel(pos_ref, dest_ref, after_ref, *refs, tiles, heads, local, sides):
    del after_ref
    if sides == 1:
        fill_tables(pos_ref, dest_ref, refs, tiles, heads, local, sides)
        return
    early_refs, out_refs = refs[: len(refs) // 2], refs[len(refs) // 2 :]

    @pl.when(is_late(sides))
    def _():
        for from_ref, to_ref in zip(early_refs, out_refs):
            to_ref[...] = from_ref[...]

    @pl.when(jnp.logical_not(is_late(sides)))
    def _():
        fill_tables(pos_ref, dest_ref, out_refs, tiles, heads, local, sides)


def split_kernel(cot_ref, own_early, other_early, own_ref, other_ref, *, local, sides):
    @pl.when(is_late(sides))
    def _():
        own_ref[...] = own_early[...]
        other_ref[...] = other_early[...]

    @pl.when(jnp.logical_not(is_late(sides)))
    def _():
        split_cots(cot_ref, own_ref, other_ref, local)


def join_kernel(pick_ref, *refs, local):
    cot_refs, (out_ref, whole) = refs[:-2], refs[-2:]
    seq = pick_ref.shape[0]
    block = min(BLOCK, seq)
    if len(cot_refs) == 2:
        half = seq // 2
        head = lax.axis_index("head")
        for ref, place in zip(cot_refs, (head, 1 - head)):
            for g in range(local):
                at = pl.multiple_of(g * seq + place * half, half)
                whole[pl.ds(at, half), :] = ref[g * half : (g + 1) * half, :]
    else:
        whole[...] = cot_refs[0][...]
    for first in range(0, seq, block):
        pick = pick_ref[first : first + block, :]
        for g in range(local):
            rows = whole[g * seq : (g + 1) * seq, :]
            part = jnp.dot(pick, rows, preferred_element_type=F32).astype(BF16)
            for q in range(QPK):
                at = (g * seq + first) * QPK + q * block
                out_ref[at : at + block, :] = part[:, q * HD : (q + 1) * HD]


def trade_halves(a, b):
    first = iota(a.shape, 1) < 4
    return jnp.where(first, a, pltpu.roll(b, 4, 1)), jnp.where(first, pltpu.roll(a, 4, 1), b)


def by_group(rows, local):
    if local == 1:
        return [rows]
    total, width = rows.shape
    tiles = rows.astype(F32).reshape(total // (8 * local), 2, local // 2, 8, width)
    parts = []
    for pair in range(local // 2):
        for x in trade_halves(tiles[:, 0, pair], tiles[:, 1, pair]):
            parts.append(x.reshape(total // local, width).astype(BF16))
    return parts


def by_place(parts):
    if len(parts) == 1:
        return parts[0]
    rows, width = parts[0].shape
    tiles = [x.reshape(rows // 8, 8, width) for x in parts]
    pairs = [trade_halves(tiles[n], tiles[n + 1]) for n in range(0, len(parts), 2)]
    whole = jnp.stack([jnp.stack([pair[side] for pair in pairs], 1) for side in range(2)], 1)
    return whole.reshape(rows * len(parts), width)


def attend_kernel(rows_ref, bias_ref, cot_ref, out_ref, sums_at, *, local):
    total, width = rows_ref.shape
    seq = total // local
    block = min(BLOCK, seq)
    wide = QPK * block
    qcols = QPK * HD
    scale = HD ** (-0.5)

    def step(first, arrived, bias):
        at = slice(0, block) if seq == block else pl.ds(first, block)
        keys = [x[:, qcols : qcols + HD] for x in arrived]
        values = [x[:, qcols + HD :] for x in arrived]
        asked = arrived if seq == block else [rows_ref[at, :]]
        queries = [jnp.concatenate([x[:, q * HD : (q + 1) * HD] for q in range(QPK)], 0) for x in asked]
        cots = [cot_ref[pl.ds((group * seq + first) * QPK, wide), :] for group in range(local)]
        scores = [nt(key, query) * (scale * math.log2(math.e)) + bias for key, query in zip(keys, queries)]
        dprobs = [nt(value, cot) for value, cot in zip(values, cots)]
        weights = [jnp.exp2(x - jnp.max(x, axis=0, keepdims=True)) for x in scores]
        probs = [(x * (1.0 / jnp.sum(x, axis=0, keepdims=True))).astype(BF16) for x in weights]
        broad = [x.astype(F32) for x in probs]
        deltas = [jnp.sum(x * y, axis=0, keepdims=True) for x, y in zip(broad, dprobs)]
        dscores = [(x * (y - z)).astype(BF16) for x, y, z in zip(broad, dprobs, deltas)]
        dqueries = [
            lax.dot_general(x, y, (((0,), (0,)), ((), ())), preferred_element_type=F32) * scale
            for x, y in zip(dscores, keys)
        ]
        dqueries = [
            jnp.concatenate([x[q * block : (q + 1) * block] for q in range(QPK)], 1) for x in dqueries
        ]
        dkeys = [jnp.dot(x, y, preferred_element_type=F32) for x, y in zip(dscores, queries)]
        dvalues = [jnp.dot(x, y, preferred_element_type=F32) for x, y in zip(probs, cots)]
        return dqueries, dkeys, dvalues

    if seq == block:
        arrived = by_group(rows_ref[...], local)
        terms = zip(*step(0, arrived, bias_ref[...]))
        parts = [jnp.concatenate([x, y * scale, z], 1) for x, y, z in terms]
        out_ref[...] = by_place(parts).astype(BF16)
        return
    sums_at[...] = jnp.zeros(sums_at.shape, F32)

    @pl.loop(0, seq // block)
    def _(index):
        first = pl.multiple_of(index * block, block)
        seen = iota((seq, wide), 0) <= first + rest(iota((seq, wide), 1), block)
        bias = jnp.where(seen, bias_ref[:, :1], NEG)
        (dquery,), (dkey,), (dvalue,) = step(first, [rows_ref[...]], bias)
        out_ref[pl.ds(first, block), :qcols] = dquery.astype(BF16)
        sums_at[:, :HD] += dkey
        sums_at[:, HD:] += dvalue

    out_ref[:, qcols : qcols + HD] = (sums_at[:, :HD] * scale).astype(BF16)
    out_ref[:, qcols + HD :] = sums_at[:, HD:].astype(BF16)


def gather_kernel(rows_ref, gather_ref, out_ref, *, part):
    count = out_ref.shape[0]
    pick = gather_ref[part * count : (part + 1) * count, :]
    out_ref[...] = jnp.dot(pick, rows_ref[...], preferred_element_type=F32).astype(BF16)


def finish_kernel(cos_ref, sin_ref, *refs):
    parts, (out_hbm, out_ref, out_sems) = refs[:-3], refs[-3:]
    stores = Stores(out_ref, out_hbm, out_sems)
    for at in stores.pieces():
        cosv, sinv = cos_ref[at, :], sin_ref[at, :]
        for first in range(0, out_ref.shape[1], HD):
            cols = slice(first, first + HD)
            x = sum(ref[at, cols].astype(F32) for ref in parts)
            if first < (QPK + 1) * HD:
                x = x * cosv - pltpu.roll(x, HD // 2, 1) * sinv
            out_ref[at, cols] = x.astype(BF16)
        stores.start(at)
    stores.wait()


def call(kernel, outs, *args, scratch=(), specs=None, out_spec=VMEM):
    shapes = [jax.ShapeDtypeStruct(s, d) for s, d in outs]
    single = len(shapes) == 1
    return pl.pallas_call(
        kernel,
        out_shape=shapes[0] if single else shapes,
        in_specs=specs or [VMEM] * len(args),
        out_specs=out_spec if single else [out_spec] * len(shapes),
        scratch_shapes=list(scratch),
        compiler_params=pltpu.CompilerParams(vmem_limit_bytes=48 * 2**20),
    )(*args)


def body(vision_rows, positions, destination, out_grad):
    tiles = lax.axis_size("tile")
    heads = lax.axis_size("head")
    tokens, groups, width = vision_rows.shape
    local = groups // heads
    count = tokens * groups
    seq = heads * tiles * C
    total = seq * local
    qcols = QPK * HD
    sides = 2 if heads == 2 and tiles % 2 == 0 else 1
    if local > 1 and sides * C != 4:
        raise ValueError("unsupported mesh")
    targets = destination.reshape(-1, LANES)
    rows = vision_rows.reshape(count, width)
    kernel = functools.partial

    def to_pair(x):
        return lax.ppermute(x, "tile", [(t, t ^ 1) for t in range(tiles)])

    others = [to_pair(rows), to_pair(positions)] if sides == 2 else []
    cos_own, sin_own, place = call(
        kernel(ready_kernel, tiles=tiles, local=local, sides=sides),
        [((tokens, HD), F32), ((tokens, HD), F32), ((total, sides * count), BF16)],
        *(pltpu.with_memory_space_constraint(x, pltpu.HBM) for x in (positions, targets)),
        specs=[HBM] * 2,
        scratch=(
            pltpu.VMEM(positions.shape, jnp.int32),
            pltpu.VMEM(targets.shape, jnp.int32),
            pltpu.SemaphoreType.DMA((2,)),
        ),
    )
    slots = out_grad.shape[0]
    cot_rows = out_grad.reshape(slots * groups, qcols)
    split_outs = [((slots * local, qcols), BF16)] * 2
    table_outs = [
        ((count, HD), F32),
        ((count, HD), F32),
        ((sides * count, total), BF16),
        ((seq, seq), BF16),
        ((seq, LANES if seq > BLOCK else QPK * seq), F32),
    ]
    early = []
    if sides == 2:
        early = call(
            kernel(early_kernel, tiles=tiles, heads=heads, local=local, sides=sides),
            split_outs + table_outs,
            *(pltpu.with_memory_space_constraint(x, pltpu.HBM) for x in (cot_rows, positions, targets)),
            specs=[HBM] * 3,
            scratch=(
                pltpu.VMEM(cot_rows.shape, BF16),
                pltpu.VMEM(positions.shape, jnp.int32),
                pltpu.VMEM(targets.shape, jnp.int32),
                pltpu.SemaphoreType.DMA((3,)),
            ),
        )
    outgoing = call(
        pack_kernel,
        [((total, width), BF16)],
        rows,
        cos_own,
        sin_own,
        place,
        early[0][:16, :LANES] if early else place[:16, :LANES],
        *others,
        out_spec=HBM,
        scratch=(
            pltpu.VMEM((sides * count, width), BF16),
            pltpu.VMEM((total, width), BF16),
            pltpu.SemaphoreType.DMA((PIECES,)),
        ),
    )

    def swap(rows):
        units = tiles // sides
        parts = rows.reshape(heads * units, -1, width)
        if sides == 1:
            axes, groups = ("head", "tile"), None
        else:
            axes, order = ("tile", "head"), unit_order(units, sides)
            groups = [
                [(unit * sides + side) * heads + head for head in range(heads) for unit in order]
                for side in range(sides)
            ]
        parts = lax.all_to_all(
            parts, axes, split_axis=0, concat_axis=0, tiled=True, axis_index_groups=groups
        )
        return parts.reshape(total, width)

    incoming = swap(outgoing)
    if sides == 2:
        own, other = call(kernel(split_kernel, local=local, sides=sides), split_outs, cot_rows, *early[:2])
        cots = [own, lax.ppermute(other, "head", [(0, 1), (1, 0)])]
    else:
        moved = lax.all_to_all(out_grad, "head", split_axis=1, concat_axis=0, tiled=True)
        cots = [jnp.swapaxes(moved, 0, 1).reshape(total, qcols)]
    cosv, sinv, gather, pick, bias = call(
        kernel(table_kernel, tiles=tiles, heads=heads, local=local, sides=sides),
        table_outs,
        positions,
        targets,
        outgoing[:16, :LANES],
        *early[2:],
    )
    cot = call(
        kernel(join_kernel, local=local),
        [((total * QPK, HD), BF16)],
        pick,
        *cots,
        scratch=(pltpu.VMEM((total, qcols), BF16),),
    )
    grads = call(
        kernel(attend_kernel, local=local),
        [((total, width), BF16)],
        incoming,
        bias,
        cot,
        scratch=(pltpu.VMEM((seq if seq > BLOCK else 8, 2 * HD), F32),),
    )
    back = swap(grads)

    def gathered(part):
        return call(kernel(gather_kernel, part=part), [((count, width), BF16)], back, gather)

    parts = [to_pair(gathered(1))] if sides == 2 else []
    parts.append(gathered(0))
    result = call(
        finish_kernel,
        [((count, width), BF16)],
        cosv,
        sinv,
        *parts,
        out_spec=HBM,
        scratch=(pltpu.VMEM((count, width), BF16), pltpu.SemaphoreType.DMA((PIECES,))),
    )
    return result.reshape(tokens, groups, width)


def solution(mesh):
    return jax.shard_map(
        body,
        mesh=mesh,
        in_specs=(
            P(("tile", "head"), None, None),
            P(None, ("tile", "head")),
            P(),
            P(("tile", "head"), None, None),
        ),
        out_specs=P(("tile", "head"), None, None),
        check_vma=False,
    )
```

```python
import functools
import math

import jax
import jax.numpy as jnp
from jax import lax
from jax.experimental import pallas as pl
from jax.experimental.pallas import tpu as pltpu
from jax.sharding import PartitionSpec as P

KV = 8
HD = 128
C = 2
QPK = 4
LANES = 128
BLOCK = 64
PIECES = 2
F32 = jnp.float32
BF16 = jnp.bfloat16
NEG = -1e30
VMEM = pl.BlockSpec(memory_space=pltpu.VMEM)
HBM = pl.BlockSpec(memory_space=pltpu.HBM)


def nt(a, b):
    return lax.dot_general(a, b, (((1,), (1,)), ((), ())), preferred_element_type=F32)


def iota(shape, dim):
    return lax.broadcasted_iota(jnp.int32, shape, dim)


def over(at, size):
    if size & (size - 1):
        return at // size
    return lax.shift_right_logical(at, jnp.int32(size.bit_length() - 1))


def rest(at, size):
    return at % size if size & (size - 1) else at & (size - 1)


def rope_parts(tokens):
    half = HD // 2
    slots = rest(iota((tokens, HD), 1), half)
    freq = jnp.exp(-(2.0 * slots.astype(F32) / HD) * math.log(1000000.0))
    sign = jnp.where(iota((tokens, HD), 1) < half, -1.0, 1.0)
    eye = (iota((tokens, tokens), 0) == iota((tokens, tokens), 1)).astype(BF16)
    return slots, freq, sign, eye


def rope_tables(pos_ref, parts=None):
    tokens = pos_ref.shape[1]
    slots, freq, sign, eye = parts or rope_parts(tokens)
    first = HD // 2 // 4
    second = (HD // 2 - first) // 2
    column = [
        nt(eye, jnp.broadcast_to(pos_ref[s : s + 1, :].astype(F32).astype(BF16), (HD, tokens)))
        for s in range(3)
    ]
    chosen = jnp.where(
        slots < first, column[0], jnp.where(slots < first + second, column[1], column[2])
    )
    angle = chosen * freq
    return jnp.cos(angle), jnp.sin(angle) * sign


def per_group(table):
    tokens = table.shape[0]
    return jnp.broadcast_to(table[:, None, :], (tokens, KV, HD)).reshape(tokens * KV, HD)


def token_finders(tokens, tile):
    start = (tile * lax.axis_size("head") + lax.axis_index("head")) * tokens
    count = tokens * KV
    off = start % LANES
    wide = (iota((count, LANES), 1) == off + over(iota((count, LANES), 0), KV)).astype(BF16)
    narrow = (iota((tokens, LANES), 1) == off + iota((tokens, LANES), 0)).astype(BF16)
    return start // LANES, wide, narrow


def token_slots(dest_ref, finders):
    at, wide, narrow = finders
    count, tokens = wide.shape[0], narrow.shape[0]
    row = dest_ref[pl.ds(at, 1), :].astype(F32).astype(BF16)
    along = nt(jnp.broadcast_to(row, (8, LANES)), wide)[:1]
    down = nt(narrow, jnp.broadcast_to(row, (count, LANES)))
    lane = iota((tokens, count), 1)
    earlier = (down == along) & (iota((tokens, count), 0) < over(lane, KV))
    rank = jnp.sum(earlier.astype(F32), axis=0, keepdims=True)
    return (along * C + rank).astype(jnp.int32)


def row_parts(at, tiles, local, sides):
    rank, at = rest(at, C), over(at, C)
    side, at = rest(at, sides), over(at, sides)
    group, at = rest(at, local), over(at, local)
    units = tiles // sides
    order = unit_order(units, sides)
    place, head = rest(at, units), over(at, units)
    unit = place
    if order != list(range(units)):
        unit = sum(jnp.where(place == n, order[n], 0) for n in range(units))
    return head, unit, side, rank, group


def unit_order(units, sides):
    if sides == 2 and units == 8:
        return [z * 2 + y for y in (0, 1) for z in (2, 1, 0, 3)]
    return list(range(units))


def placement_parts(tokens, tiles, local, sides, total):
    tile = lax.axis_index("tile")
    side = tile % sides
    head, unit, at_side, rank, group = row_parts(iota((total, LANES), 0), tiles, local, sides)
    target = unit * sides + side
    rows = (((target * C + rank) * sides + at_side) * KV + head * local + group)[:, :1]
    from_sides = [side + other - 2 * side * other for other in range(sides)]
    return rows, [(n, token_finders(tokens, tile - side + n)) for n in from_sides]


def placement(dest_ref, parts):
    rows, devices = parts
    places = []
    for from_side, finders in devices:
        count = finders[1].shape[0]
        slots = token_slots(dest_ref, finders)
        lanes = (slots * len(devices) + from_side) * KV + rest(iota((1, count), 1), KV)
        places.append((rows == lanes).astype(F32))
    return places[0] if len(places) == 1 else jnp.concatenate(places, 1)


def ready_kernel(pos_hbm, dest_hbm, cos_ref, sin_ref, place_ref, pos_ref, dest_ref, sems, *, tiles, local, sides):
    pairs = ((dest_hbm, dest_ref), (pos_hbm, pos_ref))
    loads = [pltpu.make_async_copy(a, b, sems.at[n]) for n, (a, b) in enumerate(pairs)]
    for load in loads:
        load.start()
    tokens = pos_ref.shape[1]
    place_parts = placement_parts(tokens, tiles, local, sides, place_ref.shape[0])
    angle_parts = rope_parts(tokens)
    for load in loads:
        load.wait()
    place_ref[...] = placement(dest_ref, place_parts).astype(BF16)
    cos_ref[...], sin_ref[...] = rope_tables(pos_ref, angle_parts)


def turn(from_ref, to_ref, cosv, sinv):
    for at in range(0, from_ref.shape[1], HD):
        x = from_ref[:, at : at + HD]
        if at < (QPK + 1) * HD:
            x = x.astype(F32)
            x = (x * cosv + pltpu.roll(x, HD // 2, 1) * sinv).astype(BF16)
        to_ref[:, at : at + HD] = x


def pack_kernel(vis_ref, cos_ref, sin_ref, place_ref, after_ref, *refs):
    del after_ref
    others, (out_hbm, both_ref, out_ref, out_sems) = refs[:-4], refs[-4:]
    count = vis_ref.shape[0]
    turn(vis_ref, both_ref.at[:count, :], per_group(cos_ref[...]), per_group(sin_ref[...]))
    if others:
        vis_ref, pos_ref = others
        cosv, sinv = rope_tables(pos_ref)
        turn(vis_ref, both_ref.at[count:, :], per_group(cosv), per_group(sinv))
    stores = Stores(out_ref, out_hbm, out_sems)
    for at in stores.pieces():
        out_ref[at, :] = jnp.dot(place_ref[at, :], both_ref[...], preferred_element_type=F32).astype(BF16)
        stores.start(at)
    stores.wait()


class Stores:
    def __init__(self, source, target, sems):
        self.source, self.target, self.sems, self.copies = source, target, sems, []

    def pieces(self):
        size = self.source.shape[0] // PIECES
        return [slice(n * size, (n + 1) * size) for n in range(PIECES)]

    def start(self, at):
        sem = self.sems.at[len(self.copies)]
        copy = pltpu.make_async_copy(self.source.at[at, :], self.target.at[at, :], sem)
        copy.start()
        self.copies.append(copy)

    def wait(self):
        for copy in self.copies:
            copy.wait()


def fill_tables(pos_ref, dest_ref, table_refs, tiles, heads, local, sides):
    cos_ref, sin_ref, gather_ref, pick_ref, bias_ref = table_refs
    tokens = pos_ref.shape[1]
    seq = heads * tiles * C
    cosv, sinv = rope_tables(pos_ref)
    cos_ref[...] = per_group(cosv)
    sin_ref[...] = per_group(sinv)
    place = placement(dest_ref, placement_parts(tokens, tiles, local, sides, seq * local))
    gather_ref[...] = jnp.transpose(place).astype(BF16)
    mine = lax.axis_index("tile")

    def slot_of(at):
        head, unit, side, rank, _ = row_parts(at, tiles, 1, sides)
        return (head * tiles + unit * sides + side) * C + rank

    slot = slot_of(iota((seq, LANES), 0))
    device = rest(over(slot, C), tiles) * heads + over(slot, tiles * C)

    def tally(block, sums):
        hit = (dest_ref[pl.ds(block, 1), :] == mine).astype(F32).astype(BF16)
        source = over(block * LANES + iota((seq, LANES), 1), tokens)
        return sums + nt((source == device).astype(F32).astype(BF16), jnp.broadcast_to(hit, (LANES, LANES)))

    counts = lax.fori_loop(0, dest_ref.shape[0], tally, jnp.zeros((seq, LANES), F32))
    taken = counts > rest(slot, C).astype(F32)
    pick_ref[...] = ((slot[:, :1] == iota((seq, seq), 1)) & taken[:, :1]).astype(F32).astype(BF16)
    key_ok = jnp.where(taken, 0.0, NEG)
    if seq > BLOCK:
        bias_ref[...] = key_ok
    else:
        query = slot_of(rest(iota(bias_ref.shape, 1), seq))
        bias_ref[...] = jnp.where(slot[:, :1] <= query, key_ok[:, :1], NEG)


def split_cots(cot_ref, own_ref, other_ref, local):
    head = lax.axis_index("head")
    total, count = own_ref.shape[0], cot_ref.shape[0]
    slots = total // local
    row, lane = iota((total, count), 0), iota((total, count), 1)
    base = rest(row, slots) * KV + over(row, slots)
    cot = cot_ref[...]
    for ref, group in ((own_ref, head), (other_ref, 1 - head)):
        pick = (lane == base + group * local).astype(BF16)
        ref[...] = jnp.dot(pick, cot, preferred_element_type=F32).astype(BF16)


def is_late(sides):
    return lax.axis_index("tile") % sides == 0


def early_kernel(cot_hbm, pos_hbm, dest_hbm, *refs, tiles, heads, local, sides):
    *out_refs, cot_ref, pos_ref, dest_ref, sems = refs

    @pl.when(is_late(sides))
    def _():
        pairs = ((dest_hbm, dest_ref), (pos_hbm, pos_ref), (cot_hbm, cot_ref))
        loads = [pltpu.make_async_copy(a, b, sems.at[n]) for n, (a, b) in enumerate(pairs)]
        for load in loads[:2]:
            load.start()
        for load in loads[:2]:
            load.wait()
        fill_tables(pos_ref, dest_ref, out_refs[2:], tiles, heads, local, sides)
        loads[2].start()
        loads[2].wait()
        split_cots(cot_ref, *out_refs[:2], local)


def table_kernel(pos_ref, dest_ref, after_ref, *refs, tiles, heads, local, sides):
    del after_ref
    if sides == 1:
        fill_tables(pos_ref, dest_ref, refs, tiles, heads, local, sides)
        return
    early_refs, out_refs = refs[: len(refs) // 2], refs[len(refs) // 2 :]

    @pl.when(is_late(sides))
    def _():
        for from_ref, to_ref in zip(early_refs, out_refs):
            to_ref[...] = from_ref[...]

    @pl.when(jnp.logical_not(is_late(sides)))
    def _():
        fill_tables(pos_ref, dest_ref, out_refs, tiles, heads, local, sides)


def split_kernel(cot_ref, own_early, other_early, own_ref, other_ref, *, local, sides):
    @pl.when(is_late(sides))
    def _():
        own_ref[...] = own_early[...]
        other_ref[...] = other_early[...]

    @pl.when(jnp.logical_not(is_late(sides)))
    def _():
        split_cots(cot_ref, own_ref, other_ref, local)


def join_kernel(pick_ref, *refs, local):
    cot_refs, (out_ref, whole) = refs[:-2], refs[-2:]
    seq = pick_ref.shape[0]
    block = min(BLOCK, seq)
    if len(cot_refs) == 2:
        half = seq // 2
        head = lax.axis_index("head")
        for ref, place in zip(cot_refs, (head, 1 - head)):
            for g in range(local):
                at = pl.multiple_of(g * seq + place * half, half)
                whole[pl.ds(at, half), :] = ref[g * half : (g + 1) * half, :]
    else:
        whole[...] = cot_refs[0][...]
    for first in range(0, seq, block):
        pick = pick_ref[first : first + block, :]
        for g in range(local):
            rows = whole[g * seq : (g + 1) * seq, :]
            part = jnp.dot(pick, rows, preferred_element_type=F32).astype(BF16)
            for q in range(QPK):
                at = (g * seq + first) * QPK + q * block
                out_ref[at : at + block, :] = part[:, q * HD : (q + 1) * HD]


def trade_halves(a, b):
    first = iota(a.shape, 1) < 4
    return jnp.where(first, a, pltpu.roll(b, 4, 1)), jnp.where(first, pltpu.roll(a, 4, 1), b)


def by_group(rows, local):
    if local == 1:
        return [rows]
    total, width = rows.shape
    tiles = rows.astype(F32).reshape(total // (8 * local), 2, local // 2, 8, width)
    parts = []
    for pair in range(local // 2):
        for x in trade_halves(tiles[:, 0, pair], tiles[:, 1, pair]):
            parts.append(x.reshape(total // local, width).astype(BF16))
    return parts


def by_place(parts):
    if len(parts) == 1:
        return parts[0]
    rows, width = parts[0].shape
    tiles = [x.reshape(rows // 8, 8, width) for x in parts]
    pairs = [trade_halves(tiles[n], tiles[n + 1]) for n in range(0, len(parts), 2)]
    whole = jnp.stack([jnp.stack([pair[side] for pair in pairs], 1) for side in range(2)], 1)
    return whole.reshape(rows * len(parts), width)


def attend_kernel(rows_ref, bias_ref, cot_ref, out_ref, sums_at, *, local):
    total, width = rows_ref.shape
    seq = total // local
    block = min(BLOCK, seq)
    wide = QPK * block
    qcols = QPK * HD
    scale = HD ** (-0.5)

    def step(first, arrived, bias):
        at = slice(0, block) if seq == block else pl.ds(first, block)
        keys = [x[:, qcols : qcols + HD] for x in arrived]
        values = [x[:, qcols + HD :] for x in arrived]
        asked = arrived if seq == block else [rows_ref[at, :]]
        queries = [jnp.concatenate([x[:, q * HD : (q + 1) * HD] for q in range(QPK)], 0) for x in asked]
        cots = [cot_ref[pl.ds((group * seq + first) * QPK, wide), :] for group in range(local)]
        scores = [nt(key, query) * (scale * math.log2(math.e)) + bias for key, query in zip(keys, queries)]
        dprobs = [nt(value, cot) for value, cot in zip(values, cots)]
        weights = [jnp.exp2(x - jnp.max(x, axis=0, keepdims=True)) for x in scores]
        probs = [(x * (1.0 / jnp.sum(x, axis=0, keepdims=True))).astype(BF16) for x in weights]
        broad = [x.astype(F32) for x in probs]
        deltas = [jnp.sum(x * y, axis=0, keepdims=True) for x, y in zip(broad, dprobs)]
        dscores = [(x * (y - z)).astype(BF16) for x, y, z in zip(broad, dprobs, deltas)]
        dqueries = [
            lax.dot_general(x, y, (((0,), (0,)), ((), ())), preferred_element_type=F32) * scale
            for x, y in zip(dscores, keys)
        ]
        dqueries = [
            jnp.concatenate([x[q * block : (q + 1) * block] for q in range(QPK)], 1) for x in dqueries
        ]
        dkeys = [jnp.dot(x, y, preferred_element_type=F32) for x, y in zip(dscores, queries)]
        dvalues = [jnp.dot(x, y, preferred_element_type=F32) for x, y in zip(probs, cots)]
        return dqueries, dkeys, dvalues

    if seq == block:
        arrived = by_group(rows_ref[...], local)
        terms = zip(*step(0, arrived, bias_ref[...]))
        parts = [jnp.concatenate([x, y * scale, z], 1) for x, y, z in terms]
        out_ref[...] = by_place(parts).astype(BF16)
        return
    sums_at[...] = jnp.zeros(sums_at.shape, F32)

    @pl.loop(0, seq // block)
    def _(index):
        first = pl.multiple_of(index * block, block)
        seen = iota((seq, wide), 0) <= first + rest(iota((seq, wide), 1), block)
        bias = jnp.where(seen, bias_ref[:, :1], NEG)
        (dquery,), (dkey,), (dvalue,) = step(first, [rows_ref[...]], bias)
        out_ref[pl.ds(first, block), :qcols] = dquery.astype(BF16)
        sums_at[:, :HD] += dkey
        sums_at[:, HD:] += dvalue

    out_ref[:, qcols : qcols + HD] = (sums_at[:, :HD] * scale).astype(BF16)
    out_ref[:, qcols + HD :] = sums_at[:, HD:].astype(BF16)


def gather_kernel(rows_ref, gather_ref, out_ref, *, part):
    count = out_ref.shape[0]
    pick = gather_ref[part * count : (part + 1) * count, :]
    out_ref[...] = jnp.dot(pick, rows_ref[...], preferred_element_type=F32).astype(BF16)


def finish_kernel(cos_ref, sin_ref, *refs):
    parts, (out_hbm, out_ref, out_sems) = refs[:-3], refs[-3:]
    stores = Stores(out_ref, out_hbm, out_sems)
    for at in stores.pieces():
        cosv, sinv = cos_ref[at, :], sin_ref[at, :]
        for first in range(0, out_ref.shape[1], HD):
            cols = slice(first, first + HD)
            x = sum(ref[at, cols].astype(F32) for ref in parts)
            if first < (QPK + 1) * HD:
                x = x * cosv - pltpu.roll(x, HD // 2, 1) * sinv
            out_ref[at, cols] = x.astype(BF16)
        stores.start(at)
    stores.wait()


def call(kernel, outs, *args, scratch=(), specs=None, out_spec=VMEM):
    shapes = [jax.ShapeDtypeStruct(s, d) for s, d in outs]
    single = len(shapes) == 1
    return pl.pallas_call(
        kernel,
        out_shape=shapes[0] if single else shapes,
        in_specs=specs or [VMEM] * len(args),
        out_specs=out_spec if single else [out_spec] * len(shapes),
        scratch_shapes=list(scratch),
        compiler_params=pltpu.CompilerParams(vmem_limit_bytes=48 * 2**20),
    )(*args)


def body(vision_rows, positions, destination, out_grad):
    tiles = lax.axis_size("tile")
    heads = lax.axis_size("head")
    tokens, groups, width = vision_rows.shape
    local = groups // heads
    count = tokens * groups
    seq = heads * tiles * C
    total = seq * local
    qcols = QPK * HD
    sides = 2 if heads == 2 and tiles % 2 == 0 else 1
    if local > 1 and sides * C != 4:
        raise ValueError("unsupported mesh")
    targets = destination.reshape(-1, LANES)
    rows = vision_rows.reshape(count, width)
    kernel = functools.partial

    def to_pair(x):
        return lax.ppermute(x, "tile", [(t, t ^ 1) for t in range(tiles)])

    others = [to_pair(rows), to_pair(positions)] if sides == 2 else []
    cos_own, sin_own, place = call(
        kernel(ready_kernel, tiles=tiles, local=local, sides=sides),
        [((tokens, HD), F32), ((tokens, HD), F32), ((total, sides * count), BF16)],
        *(pltpu.with_memory_space_constraint(x, pltpu.HBM) for x in (positions, targets)),
        specs=[HBM] * 2,
        scratch=(
            pltpu.VMEM(positions.shape, jnp.int32),
            pltpu.VMEM(targets.shape, jnp.int32),
            pltpu.SemaphoreType.DMA((2,)),
        ),
    )
    slots = out_grad.shape[0]
    cot_rows = out_grad.reshape(slots * groups, qcols)
    split_outs = [((slots * local, qcols), BF16)] * 2
    table_outs = [
        ((count, HD), F32),
        ((count, HD), F32),
        ((sides * count, total), BF16),
        ((seq, seq), BF16),
        ((seq, LANES if seq > BLOCK else QPK * seq), F32),
    ]
    early = []
    if sides == 2:
        early = call(
            kernel(early_kernel, tiles=tiles, heads=heads, local=local, sides=sides),
            split_outs + table_outs,
            *(pltpu.with_memory_space_constraint(x, pltpu.HBM) for x in (cot_rows, positions, targets)),
            specs=[HBM] * 3,
            scratch=(
                pltpu.VMEM(cot_rows.shape, BF16),
                pltpu.VMEM(positions.shape, jnp.int32),
                pltpu.VMEM(targets.shape, jnp.int32),
                pltpu.SemaphoreType.DMA((3,)),
            ),
        )
    outgoing = call(
        pack_kernel,
        [((total, width), BF16)],
        rows,
        cos_own,
        sin_own,
        place,
        early[0][:16, :LANES] if early else place[:16, :LANES],
        *others,
        out_spec=HBM,
        scratch=(
            pltpu.VMEM((sides * count, width), BF16),
            pltpu.VMEM((total, width), BF16),
            pltpu.SemaphoreType.DMA((PIECES,)),
        ),
    )

    def swap(rows):
        units = tiles // sides
        parts = rows.reshape(heads * units, -1, width)
        if sides == 1:
            axes, groups = ("head", "tile"), None
        else:
            axes, order = ("tile", "head"), unit_order(units, sides)
            groups = [
                [(unit * sides + side) * heads + head for head in range(heads) for unit in order]
                for side in range(sides)
            ]
        parts = lax.all_to_all(
            parts, axes, split_axis=0, concat_axis=0, tiled=True, axis_index_groups=groups
        )
        return parts.reshape(total, width)

    incoming = swap(outgoing)
    if sides == 2:
        own, other = call(kernel(split_kernel, local=local, sides=sides), split_outs, cot_rows, *early[:2])
        cots = [own, lax.ppermute(other, "head", [(0, 1), (1, 0)])]
    else:
        moved = lax.all_to_all(out_grad, "head", split_axis=1, concat_axis=0, tiled=True)
        cots = [jnp.swapaxes(moved, 0, 1).reshape(total, qcols)]
    cosv, sinv, gather, pick, bias = call(
        kernel(table_kernel, tiles=tiles, heads=heads, local=local, sides=sides),
        table_outs,
        positions,
        targets,
        outgoing[:16, :LANES],
        *early[2:],
    )
    cot = call(
        kernel(join_kernel, local=local),
        [((total * QPK, HD), BF16)],
        pick,
        *cots,
        scratch=(pltpu.VMEM((total, qcols), BF16),),
    )
    grads = call(
        kernel(attend_kernel, local=local),
        [((total, width), BF16)],
        incoming,
        bias,
        cot,
        scratch=(pltpu.VMEM((seq if seq > BLOCK else 8, 2 * HD), F32),),
    )
    back = swap(grads)

    def gathered(part):
        return call(kernel(gather_kernel, part=part), [((count, width), BF16)], back, gather)

    parts = [to_pair(gathered(1))] if sides == 2 else []
    parts.append(gathered(0))
    result = call(
        finish_kernel,
        [((count, width), BF16)],
        cosv,
        sinv,
        *parts,
        out_spec=HBM,
        scratch=(pltpu.VMEM((count, width), BF16), pltpu.SemaphoreType.DMA((PIECES,))),
    )
    return result.reshape(tokens, groups, width)


def solution(mesh):
    return jax.shard_map(
        body,
        mesh=mesh,
        in_specs=(
            P(("tile", "head"), None, None),
            P(None, ("tile", "head")),
            P(),
            P(("tile", "head"), None, None),
        ),
        out_specs=P(("tile", "head"), None, None),
        check_vma=False,
    )
```

```python
import functools
import math

import jax
import jax.numpy as jnp
from jax import lax
from jax.experimental import pallas as pl
from jax.experimental.pallas import tpu as pltpu
from jax.sharding import PartitionSpec as P

KV = 8
HD = 128
C = 2
QPK = 4
LANES = 128
BLOCK = 64
PIECES = 2
F32 = jnp.float32
BF16 = jnp.bfloat16
NEG = -1e30
VMEM = pl.BlockSpec(memory_space=pltpu.VMEM)
HBM = pl.BlockSpec(memory_space=pltpu.HBM)


def nt(a, b):
    return lax.dot_general(a, b, (((1,), (1,)), ((), ())), preferred_element_type=F32)


def iota(shape, dim):
    return lax.broadcasted_iota(jnp.int32, shape, dim)


def over(at, size):
    if size & (size - 1):
        return at // size
    return lax.shift_right_logical(at, jnp.int32(size.bit_length() - 1))


def rest(at, size):
    return at % size if size & (size - 1) else at & (size - 1)


def rope_parts(tokens):
    half = HD // 2
    slots = rest(iota((tokens, HD), 1), half)
    freq = jnp.exp(-(2.0 * slots.astype(F32) / HD) * math.log(1000000.0))
    sign = jnp.where(iota((tokens, HD), 1) < half, -1.0, 1.0)
    eye = (iota((tokens, tokens), 0) == iota((tokens, tokens), 1)).astype(BF16)
    return slots, freq, sign, eye


def rope_tables(pos_ref, parts=None):
    tokens = pos_ref.shape[1]
    slots, freq, sign, eye = parts or rope_parts(tokens)
    first = HD // 2 // 4
    second = (HD // 2 - first) // 2
    column = [
        nt(eye, jnp.broadcast_to(pos_ref[s : s + 1, :].astype(F32).astype(BF16), (HD, tokens)))
        for s in range(3)
    ]
    chosen = jnp.where(
        slots < first, column[0], jnp.where(slots < first + second, column[1], column[2])
    )
    angle = chosen * freq
    return jnp.cos(angle), jnp.sin(angle) * sign


def per_group(table):
    tokens = table.shape[0]
    return jnp.broadcast_to(table[:, None, :], (tokens, KV, HD)).reshape(tokens * KV, HD)


def token_finders(tokens, tile):
    start = (tile * lax.axis_size("head") + lax.axis_index("head")) * tokens
    count = tokens * KV
    off = start % LANES
    wide = (iota((count, LANES), 1) == off + over(iota((count, LANES), 0), KV)).astype(BF16)
    narrow = (iota((tokens, LANES), 1) == off + iota((tokens, LANES), 0)).astype(BF16)
    return start // LANES, wide, narrow


def token_slots(dest_ref, finders):
    at, wide, narrow = finders
    count, tokens = wide.shape[0], narrow.shape[0]
    row = dest_ref[pl.ds(at, 1), :].astype(F32).astype(BF16)
    along = nt(jnp.broadcast_to(row, (8, LANES)), wide)[:1]
    down = nt(narrow, jnp.broadcast_to(row, (count, LANES)))
    lane = iota((tokens, count), 1)
    earlier = (down == along) & (iota((tokens, count), 0) < over(lane, KV))
    rank = jnp.sum(earlier.astype(F32), axis=0, keepdims=True)
    return (along * C + rank).astype(jnp.int32)


def row_parts(at, tiles, local, sides, back=False):
    rank, at = rest(at, C), over(at, C)
    side, at = rest(at, sides), over(at, sides)
    group, at = rest(at, local), over(at, local)
    units = tiles // sides
    order = unit_order(units, sides, back)
    place, head = rest(at, units), over(at, units)
    if order == [(n + order[0]) % units for n in range(units)]:
        unit = rest(place + order[0], units)
    else:
        unit = sum(jnp.where(place == n, order[n], 0) for n in range(units))
    return head, unit, side, rank, group


def unit_order(units, sides, back):
    if sides == 1:
        return list(range(units))
    if back and units == 8:
        return [z * 2 + y for y in (0, 1) for z in (2, 1, 0, 3)]
    return [(n + units // 2) % units for n in range(units)]


def placement_parts(tokens, tiles, local, sides, total, back=False):
    tile = lax.axis_index("tile")
    side = tile % sides
    head, unit, at_side, rank, group = row_parts(iota((total, LANES), 0), tiles, local, sides, back)
    target = unit * sides + side
    rows = (((target * C + rank) * sides + at_side) * KV + head * local + group)[:, :1]
    from_sides = [side + other - 2 * side * other for other in range(sides)]
    return rows, [(n, token_finders(tokens, tile - side + n)) for n in from_sides]


def placement(dest_ref, parts):
    rows, devices = parts
    places = []
    for from_side, finders in devices:
        count = finders[1].shape[0]
        slots = token_slots(dest_ref, finders)
        lanes = (slots * len(devices) + from_side) * KV + rest(iota((1, count), 1), KV)
        places.append((rows == lanes).astype(F32))
    return places[0] if len(places) == 1 else jnp.concatenate(places, 1)


def ready_kernel(pos_hbm, dest_hbm, cos_ref, sin_ref, place_ref, pos_ref, dest_ref, sems, *, tiles, local, sides):
    pairs = ((dest_hbm, dest_ref), (pos_hbm, pos_ref))
    loads = [pltpu.make_async_copy(a, b, sems.at[n]) for n, (a, b) in enumerate(pairs)]
    for load in loads:
        load.start()
    tokens = pos_ref.shape[1]
    place_parts = placement_parts(tokens, tiles, local, sides, place_ref.shape[0])
    angle_parts = rope_parts(tokens)
    for load in loads:
        load.wait()
    place_ref[...] = placement(dest_ref, place_parts).astype(BF16)
    cos_ref[...], sin_ref[...] = rope_tables(pos_ref, angle_parts)


def turn(from_ref, to_ref, cosv, sinv):
    for at in range(0, from_ref.shape[1], HD):
        x = from_ref[:, at : at + HD]
        if at < (QPK + 1) * HD:
            x = x.astype(F32)
            x = (x * cosv + pltpu.roll(x, HD // 2, 1) * sinv).astype(BF16)
        to_ref[:, at : at + HD] = x


def pack_kernel(vis_ref, cos_ref, sin_ref, place_ref, after_ref, *refs):
    del after_ref
    others, (out_hbm, both_ref, out_ref, out_sems) = refs[:-4], refs[-4:]
    count = vis_ref.shape[0]
    turn(vis_ref, both_ref.at[:count, :], per_group(cos_ref[...]), per_group(sin_ref[...]))
    if others:
        vis_ref, pos_ref = others
        cosv, sinv = rope_tables(pos_ref)
        turn(vis_ref, both_ref.at[count:, :], per_group(cosv), per_group(sinv))
    stores = Stores(out_ref, out_hbm, out_sems)
    for at in stores.pieces():
        out_ref[at, :] = jnp.dot(place_ref[at, :], both_ref[...], preferred_element_type=F32).astype(BF16)
        stores.start(at)
    stores.wait()


class Stores:
    def __init__(self, source, target, sems):
        self.source, self.target, self.sems, self.copies = source, target, sems, []

    def pieces(self):
        size = self.source.shape[0] // PIECES
        return [slice(n * size, (n + 1) * size) for n in range(PIECES)]

    def start(self, at):
        sem = self.sems.at[len(self.copies)]
        copy = pltpu.make_async_copy(self.source.at[at, :], self.target.at[at, :], sem)
        copy.start()
        self.copies.append(copy)

    def wait(self):
        for copy in self.copies:
            copy.wait()


def fill_tables(pos_ref, dest_ref, table_refs, tiles, heads, local, sides):
    cos_ref, sin_ref, gather_ref, pick_ref, bias_ref = table_refs
    tokens = pos_ref.shape[1]
    seq = heads * tiles * C
    cosv, sinv = rope_tables(pos_ref)
    cos_ref[...] = per_group(cosv)
    sin_ref[...] = per_group(sinv)
    place = placement(dest_ref, placement_parts(tokens, tiles, local, sides, seq * local, True))
    gather_ref[...] = jnp.transpose(place).astype(BF16)
    mine = lax.axis_index("tile")

    def slot_of(at):
        head, unit, side, rank, _ = row_parts(at, tiles, 1, sides)
        return (head * tiles + unit * sides + side) * C + rank

    slot = slot_of(iota((seq, LANES), 0))
    device = rest(over(slot, C), tiles) * heads + over(slot, tiles * C)

    def tally(block, sums):
        hit = (dest_ref[pl.ds(block, 1), :] == mine).astype(F32).astype(BF16)
        source = over(block * LANES + iota((seq, LANES), 1), tokens)
        return sums + nt((source == device).astype(F32).astype(BF16), jnp.broadcast_to(hit, (LANES, LANES)))

    counts = lax.fori_loop(0, dest_ref.shape[0], tally, jnp.zeros((seq, LANES), F32))
    taken = counts > rest(slot, C).astype(F32)
    pick_ref[...] = ((slot[:, :1] == iota((seq, seq), 1)) & taken[:, :1]).astype(F32).astype(BF16)
    key_ok = jnp.where(taken, 0.0, NEG)
    if seq > BLOCK:
        bias_ref[...] = key_ok
    else:
        query = slot_of(rest(iota(bias_ref.shape, 1), seq))
        bias_ref[...] = jnp.where(slot[:, :1] <= query, key_ok[:, :1], NEG)


def split_cots(cot_ref, own_ref, other_ref, local):
    head = lax.axis_index("head")
    total, count = own_ref.shape[0], cot_ref.shape[0]
    slots = total // local
    row, lane = iota((total, count), 0), iota((total, count), 1)
    base = rest(row, slots) * KV + over(row, slots)
    cot = cot_ref[...]
    for ref, group in ((own_ref, head), (other_ref, 1 - head)):
        pick = (lane == base + group * local).astype(BF16)
        ref[...] = jnp.dot(pick, cot, preferred_element_type=F32).astype(BF16)


def is_late(sides):
    return lax.axis_index("tile") % sides == 0


def early_kernel(cot_hbm, pos_hbm, dest_hbm, *refs, tiles, heads, local, sides):
    *out_refs, cot_ref, pos_ref, dest_ref, sems = refs

    @pl.when(is_late(sides))
    def _():
        pairs = ((dest_hbm, dest_ref), (pos_hbm, pos_ref), (cot_hbm, cot_ref))
        loads = [pltpu.make_async_copy(a, b, sems.at[n]) for n, (a, b) in enumerate(pairs)]
        for load in loads[:2]:
            load.start()
        for load in loads[:2]:
            load.wait()
        fill_tables(pos_ref, dest_ref, out_refs[2:], tiles, heads, local, sides)
        loads[2].start()
        loads[2].wait()
        split_cots(cot_ref, *out_refs[:2], local)


def table_kernel(pos_ref, dest_ref, after_ref, *refs, tiles, heads, local, sides):
    del after_ref
    if sides == 1:
        fill_tables(pos_ref, dest_ref, refs, tiles, heads, local, sides)
        return
    early_refs, out_refs = refs[: len(refs) // 2], refs[len(refs) // 2 :]

    @pl.when(is_late(sides))
    def _():
        for from_ref, to_ref in zip(early_refs, out_refs):
            to_ref[...] = from_ref[...]

    @pl.when(jnp.logical_not(is_late(sides)))
    def _():
        fill_tables(pos_ref, dest_ref, out_refs, tiles, heads, local, sides)


def split_kernel(cot_ref, own_early, other_early, own_ref, other_ref, *, local, sides):
    @pl.when(is_late(sides))
    def _():
        own_ref[...] = own_early[...]
        other_ref[...] = other_early[...]

    @pl.when(jnp.logical_not(is_late(sides)))
    def _():
        split_cots(cot_ref, own_ref, other_ref, local)


def join_kernel(pick_ref, *refs, local):
    cot_refs, (out_ref, whole) = refs[:-2], refs[-2:]
    seq = pick_ref.shape[0]
    block = min(BLOCK, seq)
    if len(cot_refs) == 2:
        half = seq // 2
        head = lax.axis_index("head")
        for ref, place in zip(cot_refs, (head, 1 - head)):
            for g in range(local):
                at = pl.multiple_of(g * seq + place * half, half)
                whole[pl.ds(at, half), :] = ref[g * half : (g + 1) * half, :]
    else:
        whole[...] = cot_refs[0][...]
    for first in range(0, seq, block):
        pick = pick_ref[first : first + block, :]
        for g in range(local):
            rows = whole[g * seq : (g + 1) * seq, :]
            part = jnp.dot(pick, rows, preferred_element_type=F32).astype(BF16)
            for q in range(QPK):
                at = (g * seq + first) * QPK + q * block
                out_ref[at : at + block, :] = part[:, q * HD : (q + 1) * HD]


def trade_halves(a, b):
    first = iota(a.shape, 1) < 4
    return jnp.where(first, a, pltpu.roll(b, 4, 1)), jnp.where(first, pltpu.roll(a, 4, 1), b)


def by_group(rows, local):
    if local == 1:
        return [rows]
    total, width = rows.shape
    tiles = rows.astype(F32).reshape(total // (8 * local), 2, local // 2, 8, width)
    parts = []
    for pair in range(local // 2):
        for x in trade_halves(tiles[:, 0, pair], tiles[:, 1, pair]):
            parts.append(x.reshape(total // local, width).astype(BF16))
    return parts


def by_place(parts):
    if len(parts) == 1:
        return parts[0]
    rows, width = parts[0].shape
    tiles = [x.reshape(rows // 8, 8, width) for x in parts]
    pairs = [trade_halves(tiles[n], tiles[n + 1]) for n in range(0, len(parts), 2)]
    whole = jnp.stack([jnp.stack([pair[side] for pair in pairs], 1) for side in range(2)], 1)
    return whole.reshape(rows * len(parts), width)


def attend_kernel(rows_ref, bias_ref, cot_ref, out_ref, sums_at, *, local, places):
    total, width = rows_ref.shape
    seq = total // local
    block = min(BLOCK, seq)
    wide = QPK * block
    qcols = QPK * HD
    scale = HD ** (-0.5)

    def step(first, arrived, bias):
        at = slice(0, block) if seq == block else pl.ds(first, block)
        keys = [x[:, qcols : qcols + HD] for x in arrived]
        values = [x[:, qcols + HD :] for x in arrived]
        asked = arrived if seq == block else [rows_ref[at, :]]
        queries = [jnp.concatenate([x[:, q * HD : (q + 1) * HD] for q in range(QPK)], 0) for x in asked]
        cots = [cot_ref[pl.ds((group * seq + first) * QPK, wide), :] for group in range(local)]
        scores = [nt(key, query) * (scale * math.log2(math.e)) + bias for key, query in zip(keys, queries)]
        dprobs = [nt(value, cot) for value, cot in zip(values, cots)]
        weights = [jnp.exp2(x - jnp.max(x, axis=0, keepdims=True)) for x in scores]
        probs = [(x * (1.0 / jnp.sum(x, axis=0, keepdims=True))).astype(BF16) for x in weights]
        broad = [x.astype(F32) for x in probs]
        deltas = [jnp.sum(x * y, axis=0, keepdims=True) for x, y in zip(broad, dprobs)]
        dscores = [(x * (y - z)).astype(BF16) for x, y, z in zip(broad, dprobs, deltas)]
        dqueries = [
            lax.dot_general(x, y, (((0,), (0,)), ((), ())), preferred_element_type=F32) * scale
            for x, y in zip(dscores, keys)
        ]
        dqueries = [
            jnp.concatenate([x[q * block : (q + 1) * block] for q in range(QPK)], 1) for x in dqueries
        ]
        dkeys = [jnp.dot(x, y, preferred_element_type=F32) for x, y in zip(dscores, queries)]
        dvalues = [jnp.dot(x, y, preferred_element_type=F32) for x, y in zip(probs, cots)]
        return dqueries, dkeys, dvalues

    if seq == block:
        arrived = by_group(rows_ref[...], local)
        terms = zip(*step(0, arrived, bias_ref[...]))
        parts = [jnp.concatenate([x, y * scale, z], 1) for x, y, z in terms]
        grads = by_place(parts).astype(BF16)
        if places != sorted(places):
            size = total // len(places)
            grads = jnp.concatenate([grads[n * size : (n + 1) * size] for n in places], 0)
        out_ref[...] = grads
        return
    sums_at[...] = jnp.zeros(sums_at.shape, F32)

    @pl.loop(0, seq // block)
    def _(index):
        first = pl.multiple_of(index * block, block)
        seen = iota((seq, wide), 0) <= first + rest(iota((seq, wide), 1), block)
        bias = jnp.where(seen, bias_ref[:, :1], NEG)
        (dquery,), (dkey,), (dvalue,) = step(first, [rows_ref[...]], bias)
        out_ref[pl.ds(first, block), :qcols] = dquery.astype(BF16)
        sums_at[:, :HD] += dkey
        sums_at[:, HD:] += dvalue

    out_ref[:, qcols : qcols + HD] = (sums_at[:, :HD] * scale).astype(BF16)
    out_ref[:, qcols + HD :] = sums_at[:, HD:].astype(BF16)


def gather_kernel(rows_ref, gather_ref, out_ref, *, part):
    count = out_ref.shape[0]
    pick = gather_ref[part * count : (part + 1) * count, :]
    out_ref[...] = jnp.dot(pick, rows_ref[...], preferred_element_type=F32).astype(BF16)


def finish_kernel(cos_ref, sin_ref, *refs):
    parts, (out_hbm, out_ref, out_sems) = refs[:-3], refs[-3:]
    stores = Stores(out_ref, out_hbm, out_sems)
    for at in stores.pieces():
        cosv, sinv = cos_ref[at, :], sin_ref[at, :]
        for first in range(0, out_ref.shape[1], HD):
            cols = slice(first, first + HD)
            x = sum(ref[at, cols].astype(F32) for ref in parts)
            if first < (QPK + 1) * HD:
                x = x * cosv - pltpu.roll(x, HD // 2, 1) * sinv
            out_ref[at, cols] = x.astype(BF16)
        stores.start(at)
    stores.wait()


def call(kernel, outs, *args, scratch=(), specs=None, out_spec=VMEM):
    shapes = [jax.ShapeDtypeStruct(s, d) for s, d in outs]
    single = len(shapes) == 1
    return pl.pallas_call(
        kernel,
        out_shape=shapes[0] if single else shapes,
        in_specs=specs or [VMEM] * len(args),
        out_specs=out_spec if single else [out_spec] * len(shapes),
        scratch_shapes=list(scratch),
        compiler_params=pltpu.CompilerParams(vmem_limit_bytes=48 * 2**20),
    )(*args)


def body(vision_rows, positions, destination, out_grad):
    tiles = lax.axis_size("tile")
    heads = lax.axis_size("head")
    tokens, groups, width = vision_rows.shape
    local = groups // heads
    count = tokens * groups
    seq = heads * tiles * C
    total = seq * local
    qcols = QPK * HD
    sides = 2 if heads == 2 and tiles % 2 == 0 else 1
    if local > 1 and sides * C != 4:
        raise ValueError("unsupported mesh")
    targets = destination.reshape(-1, LANES)
    rows = vision_rows.reshape(count, width)
    kernel = functools.partial

    def to_pair(x):
        return lax.ppermute(x, "tile", [(t, t ^ 1) for t in range(tiles)])

    others = [to_pair(rows), to_pair(positions)] if sides == 2 else []
    cos_own, sin_own, place = call(
        kernel(ready_kernel, tiles=tiles, local=local, sides=sides),
        [((tokens, HD), F32), ((tokens, HD), F32), ((total, sides * count), BF16)],
        *(pltpu.with_memory_space_constraint(x, pltpu.HBM) for x in (positions, targets)),
        specs=[HBM] * 2,
        scratch=(
            pltpu.VMEM(positions.shape, jnp.int32),
            pltpu.VMEM(targets.shape, jnp.int32),
            pltpu.SemaphoreType.DMA((2,)),
        ),
    )
    slots = out_grad.shape[0]
    cot_rows = out_grad.reshape(slots * groups, qcols)
    split_outs = [((slots * local, qcols), BF16)] * 2
    table_outs = [
        ((count, HD), F32),
        ((count, HD), F32),
        ((sides * count, total), BF16),
        ((seq, seq), BF16),
        ((seq, LANES if seq > BLOCK else QPK * seq), F32),
    ]
    early = []
    if sides == 2:
        early = call(
            kernel(early_kernel, tiles=tiles, heads=heads, local=local, sides=sides),
            split_outs + table_outs,
            *(pltpu.with_memory_space_constraint(x, pltpu.HBM) for x in (cot_rows, positions, targets)),
            specs=[HBM] * 3,
            scratch=(
                pltpu.VMEM(cot_rows.shape, BF16),
                pltpu.VMEM(positions.shape, jnp.int32),
                pltpu.VMEM(targets.shape, jnp.int32),
                pltpu.SemaphoreType.DMA((3,)),
            ),
        )
    outgoing = call(
        pack_kernel,
        [((total, width), BF16)],
        rows,
        cos_own,
        sin_own,
        place,
        early[0][:16, :LANES] if early else place[:16, :LANES],
        *others,
        out_spec=HBM,
        scratch=(
            pltpu.VMEM((sides * count, width), BF16),
            pltpu.VMEM((total, width), BF16),
            pltpu.SemaphoreType.DMA((PIECES,)),
        ),
    )

    def swap(rows, back=False):
        units = tiles // sides
        parts = rows.reshape(heads * units, -1, width)
        if sides == 1:
            axes, groups = ("head", "tile"), None
        else:
            axes, order = ("tile", "head"), unit_order(units, sides, back)
            groups = [
                [(unit * sides + side) * heads + head for head in range(heads) for unit in order]
                for side in range(sides)
            ]
        parts = lax.all_to_all(
            parts, axes, split_axis=0, concat_axis=0, tiled=True, axis_index_groups=groups
        )
        return parts.reshape(total, width)

    incoming = swap(outgoing)
    if sides == 2:
        own, other = call(kernel(split_kernel, local=local, sides=sides), split_outs, cot_rows, *early[:2])
        cots = [own, lax.ppermute(other, "head", [(0, 1), (1, 0)])]
    else:
        moved = lax.all_to_all(out_grad, "head", split_axis=1, concat_axis=0, tiled=True)
        cots = [jnp.swapaxes(moved, 0, 1).reshape(total, qcols)]
    cosv, sinv, gather, pick, bias = call(
        kernel(table_kernel, tiles=tiles, heads=heads, local=local, sides=sides),
        table_outs,
        positions,
        targets,
        outgoing[:16, :LANES],
        *early[2:],
    )
    cot = call(
        kernel(join_kernel, local=local),
        [((total * QPK, HD), BF16)],
        pick,
        *cots,
        scratch=(pltpu.VMEM((total, qcols), BF16),),
    )
    units = tiles // sides
    there, back = (unit_order(units, sides, way) for way in (False, True))
    places = [head * units + there.index(unit) for head in range(heads) for unit in back]
    grads = call(
        kernel(attend_kernel, local=local, places=places),
        [((total, width), BF16)],
        incoming,
        bias,
        cot,
        scratch=(pltpu.VMEM((seq if seq > BLOCK else 8, 2 * HD), F32),),
    )
    returned = swap(grads, True)

    def gathered(part):
        return call(kernel(gather_kernel, part=part), [((count, width), BF16)], returned, gather)

    parts = [to_pair(gathered(1))] if sides == 2 else []
    parts.append(gathered(0))
    result = call(
        finish_kernel,
        [((count, width), BF16)],
        cosv,
        sinv,
        *parts,
        out_spec=HBM,
        scratch=(pltpu.VMEM((count, width), BF16), pltpu.SemaphoreType.DMA((PIECES,))),
    )
    return result.reshape(tokens, groups, width)


def solution(mesh):
    return jax.shard_map(
        body,
        mesh=mesh,
        in_specs=(
            P(("tile", "head"), None, None),
            P(None, ("tile", "head")),
            P(),
            P(("tile", "head"), None, None),
        ),
        out_specs=P(("tile", "head"), None, None),
        check_vma=False,
    )
```

```python
import functools
import math

import jax
import jax.numpy as jnp
from jax import lax
from jax.experimental import pallas as pl
from jax.experimental.pallas import tpu as pltpu
from jax.sharding import PartitionSpec as P

KV = 8
HD = 128
C = 2
QPK = 4
LANES = 128
BLOCK = 64
PIECES = 2
F32 = jnp.float32
BF16 = jnp.bfloat16
NEG = -1e30
VMEM = pl.BlockSpec(memory_space=pltpu.VMEM)
HBM = pl.BlockSpec(memory_space=pltpu.HBM)


def nt(a, b):
    return lax.dot_general(a, b, (((1,), (1,)), ((), ())), preferred_element_type=F32)


def iota(shape, dim):
    return lax.broadcasted_iota(jnp.int32, shape, dim)


def over(at, size):
    if size & (size - 1):
        return at // size
    return lax.shift_right_logical(at, jnp.int32(size.bit_length() - 1))


def rest(at, size):
    return at % size if size & (size - 1) else at & (size - 1)


def rope_parts(tokens):
    half = HD // 2
    slots = rest(iota((tokens, HD), 1), half)
    freq = jnp.exp(-(2.0 * slots.astype(F32) / HD) * math.log(1000000.0))
    sign = jnp.where(iota((tokens, HD), 1) < half, -1.0, 1.0)
    eye = (iota((tokens, tokens), 0) == iota((tokens, tokens), 1)).astype(BF16)
    return slots, freq, sign, eye


def rope_tables(pos_ref, parts=None):
    tokens = pos_ref.shape[1]
    slots, freq, sign, eye = parts or rope_parts(tokens)
    first = HD // 2 // 4
    second = (HD // 2 - first) // 2
    column = [
        nt(eye, jnp.broadcast_to(pos_ref[s : s + 1, :].astype(F32).astype(BF16), (HD, tokens)))
        for s in range(3)
    ]
    chosen = jnp.where(
        slots < first, column[0], jnp.where(slots < first + second, column[1], column[2])
    )
    angle = chosen * freq
    return jnp.cos(angle), jnp.sin(angle) * sign


def per_group(table):
    tokens = table.shape[0]
    return jnp.broadcast_to(table[:, None, :], (tokens, KV, HD)).reshape(tokens * KV, HD)


def token_finders(tokens, tile):
    start = (tile * lax.axis_size("head") + lax.axis_index("head")) * tokens
    count = tokens * KV
    off = start % LANES
    wide = (iota((count, LANES), 1) == off + over(iota((count, LANES), 0), KV)).astype(BF16)
    narrow = (iota((tokens, LANES), 1) == off + iota((tokens, LANES), 0)).astype(BF16)
    return start // LANES, wide, narrow


def token_slots(dest_ref, finders):
    at, wide, narrow = finders
    count, tokens = wide.shape[0], narrow.shape[0]
    row = dest_ref[pl.ds(at, 1), :].astype(F32).astype(BF16)
    along = nt(jnp.broadcast_to(row, (8, LANES)), wide)[:1]
    down = nt(narrow, jnp.broadcast_to(row, (count, LANES)))
    lane = iota((tokens, count), 1)
    earlier = (down == along) & (iota((tokens, count), 0) < over(lane, KV))
    rank = jnp.sum(earlier.astype(F32), axis=0, keepdims=True)
    return (along * C + rank).astype(jnp.int32)


def row_parts(at, tiles, local, sides, back=False):
    rank, at = rest(at, C), over(at, C)
    side, at = rest(at, sides), over(at, sides)
    group, at = rest(at, local), over(at, local)
    units = tiles // sides
    order = unit_order(units, sides, back)
    place, head = rest(at, units), over(at, units)
    if order == [(n + order[0]) % units for n in range(units)]:
        unit = rest(place + order[0], units)
    else:
        unit = sum(jnp.where(place == n, order[n], 0) for n in range(units))
    return head, unit, side, rank, group


def unit_order(units, sides, back):
    if sides == 1:
        return list(range(units))
    if back and units == 8:
        return [z * 2 for z in (2, 1, 0, 3)] + [z * 2 + 1 for z in (3, 2, 1, 0)]
    return [(n + units // 2) % units for n in range(units)]


def placement_parts(tokens, tiles, local, sides, total, back=False):
    tile = lax.axis_index("tile")
    side = tile % sides
    head, unit, at_side, rank, group = row_parts(iota((total, LANES), 0), tiles, local, sides, back)
    target = unit * sides + side
    rows = (((target * C + rank) * sides + at_side) * KV + head * local + group)[:, :1]
    from_sides = [side + other - 2 * side * other for other in range(sides)]
    return rows, [(n, token_finders(tokens, tile - side + n)) for n in from_sides]


def placement(dest_ref, parts):
    rows, devices = parts
    places = []
    for from_side, finders in devices:
        count = finders[1].shape[0]
        slots = token_slots(dest_ref, finders)
        lanes = (slots * len(devices) + from_side) * KV + rest(iota((1, count), 1), KV)
        places.append((rows == lanes).astype(F32))
    return places[0] if len(places) == 1 else jnp.concatenate(places, 1)


def ready_kernel(pos_hbm, dest_hbm, cos_ref, sin_ref, place_ref, pos_ref, dest_ref, sems, *, tiles, local, sides):
    pairs = ((dest_hbm, dest_ref), (pos_hbm, pos_ref))
    loads = [pltpu.make_async_copy(a, b, sems.at[n]) for n, (a, b) in enumerate(pairs)]
    for load in loads:
        load.start()
    tokens = pos_ref.shape[1]
    place_parts = placement_parts(tokens, tiles, local, sides, place_ref.shape[0])
    angle_parts = rope_parts(tokens)
    for load in loads:
        load.wait()
    place_ref[...] = placement(dest_ref, place_parts).astype(BF16)
    cos_ref[...], sin_ref[...] = rope_tables(pos_ref, angle_parts)


def turn(from_ref, to_ref, cosv, sinv):
    for at in range(0, from_ref.shape[1], HD):
        x = from_ref[:, at : at + HD]
        if at < (QPK + 1) * HD:
            x = x.astype(F32)
            x = (x * cosv + pltpu.roll(x, HD // 2, 1) * sinv).astype(BF16)
        to_ref[:, at : at + HD] = x


def pack_kernel(vis_ref, cos_ref, sin_ref, place_ref, after_ref, *refs):
    del after_ref
    others, (out_hbm, both_ref, out_ref, out_sems) = refs[:-4], refs[-4:]
    count = vis_ref.shape[0]
    turn(vis_ref, both_ref.at[:count, :], per_group(cos_ref[...]), per_group(sin_ref[...]))
    if others:
        vis_ref, pos_ref = others
        cosv, sinv = rope_tables(pos_ref)
        turn(vis_ref, both_ref.at[count:, :], per_group(cosv), per_group(sinv))
    stores = Stores(out_ref, out_hbm, out_sems)
    for at in stores.pieces():
        out_ref[at, :] = jnp.dot(place_ref[at, :], both_ref[...], preferred_element_type=F32).astype(BF16)
        stores.start(at)
    stores.wait()


class Stores:
    def __init__(self, source, target, sems):
        self.source, self.target, self.sems, self.copies = source, target, sems, []

    def pieces(self):
        size = self.source.shape[0] // PIECES
        return [slice(n * size, (n + 1) * size) for n in range(PIECES)]

    def start(self, at):
        sem = self.sems.at[len(self.copies)]
        copy = pltpu.make_async_copy(self.source.at[at, :], self.target.at[at, :], sem)
        copy.start()
        self.copies.append(copy)

    def wait(self):
        for copy in self.copies:
            copy.wait()


def fill_tables(pos_ref, dest_ref, table_refs, tiles, heads, local, sides):
    cos_ref, sin_ref, gather_ref, pick_ref, bias_ref = table_refs
    tokens = pos_ref.shape[1]
    seq = heads * tiles * C
    cosv, sinv = rope_tables(pos_ref)
    cos_ref[...] = per_group(cosv)
    sin_ref[...] = per_group(sinv)
    place = placement(dest_ref, placement_parts(tokens, tiles, local, sides, seq * local, True))
    gather_ref[...] = jnp.transpose(place).astype(BF16)
    mine = lax.axis_index("tile")

    def slot_of(at):
        head, unit, side, rank, _ = row_parts(at, tiles, 1, sides)
        return (head * tiles + unit * sides + side) * C + rank

    slot = slot_of(iota((seq, LANES), 0))
    device = rest(over(slot, C), tiles) * heads + over(slot, tiles * C)

    def tally(block, sums):
        hit = (dest_ref[pl.ds(block, 1), :] == mine).astype(F32).astype(BF16)
        source = over(block * LANES + iota((seq, LANES), 1), tokens)
        return sums + nt((source == device).astype(F32).astype(BF16), jnp.broadcast_to(hit, (LANES, LANES)))

    counts = lax.fori_loop(0, dest_ref.shape[0], tally, jnp.zeros((seq, LANES), F32))
    taken = counts > rest(slot, C).astype(F32)
    pick_ref[...] = ((slot[:, :1] == iota((seq, seq), 1)) & taken[:, :1]).astype(F32).astype(BF16)
    key_ok = jnp.where(taken, 0.0, NEG)
    if seq > BLOCK:
        bias_ref[...] = key_ok
    else:
        query = slot_of(rest(iota(bias_ref.shape, 1), seq))
        bias_ref[...] = jnp.where(slot[:, :1] <= query, key_ok[:, :1], NEG)


def split_cots(cot_ref, own_ref, other_ref, local):
    head = lax.axis_index("head")
    total, count = own_ref.shape[0], cot_ref.shape[0]
    slots = total // local
    row, lane = iota((total, count), 0), iota((total, count), 1)
    base = rest(row, slots) * KV + over(row, slots)
    cot = cot_ref[...]
    for ref, group in ((own_ref, head), (other_ref, 1 - head)):
        pick = (lane == base + group * local).astype(BF16)
        ref[...] = jnp.dot(pick, cot, preferred_element_type=F32).astype(BF16)


def is_late(sides):
    return lax.axis_index("tile") % sides == 0


def early_kernel(cot_hbm, pos_hbm, dest_hbm, *refs, tiles, heads, local, sides):
    *out_refs, cot_ref, pos_ref, dest_ref, sems = refs

    @pl.when(is_late(sides))
    def _():
        pairs = ((dest_hbm, dest_ref), (pos_hbm, pos_ref), (cot_hbm, cot_ref))
        loads = [pltpu.make_async_copy(a, b, sems.at[n]) for n, (a, b) in enumerate(pairs)]
        for load in loads[:2]:
            load.start()
        for load in loads[:2]:
            load.wait()
        fill_tables(pos_ref, dest_ref, out_refs[2:], tiles, heads, local, sides)
        loads[2].start()
        loads[2].wait()
        split_cots(cot_ref, *out_refs[:2], local)


def table_kernel(pos_ref, dest_ref, after_ref, *refs, tiles, heads, local, sides):
    del after_ref
    if sides == 1:
        fill_tables(pos_ref, dest_ref, refs, tiles, heads, local, sides)
        return
    early_refs, out_refs = refs[: len(refs) // 2], refs[len(refs) // 2 :]

    @pl.when(is_late(sides))
    def _():
        for from_ref, to_ref in zip(early_refs, out_refs):
            to_ref[...] = from_ref[...]

    @pl.when(jnp.logical_not(is_late(sides)))
    def _():
        fill_tables(pos_ref, dest_ref, out_refs, tiles, heads, local, sides)


def split_kernel(cot_ref, own_early, other_early, own_ref, other_ref, *, local, sides):
    @pl.when(is_late(sides))
    def _():
        own_ref[...] = own_early[...]
        other_ref[...] = other_early[...]

    @pl.when(jnp.logical_not(is_late(sides)))
    def _():
        split_cots(cot_ref, own_ref, other_ref, local)


def join_kernel(pick_ref, *refs, local):
    cot_refs, (out_ref, whole) = refs[:-2], refs[-2:]
    seq = pick_ref.shape[0]
    block = min(BLOCK, seq)
    if len(cot_refs) == 2:
        half = seq // 2
        head = lax.axis_index("head")
        for ref, place in zip(cot_refs, (head, 1 - head)):
            for g in range(local):
                at = pl.multiple_of(g * seq + place * half, half)
                whole[pl.ds(at, half), :] = ref[g * half : (g + 1) * half, :]
    else:
        whole[...] = cot_refs[0][...]
    for first in range(0, seq, block):
        pick = pick_ref[first : first + block, :]
        for g in range(local):
            rows = whole[g * seq : (g + 1) * seq, :]
            part = jnp.dot(pick, rows, preferred_element_type=F32).astype(BF16)
            for q in range(QPK):
                at = (g * seq + first) * QPK + q * block
                out_ref[at : at + block, :] = part[:, q * HD : (q + 1) * HD]


def trade_halves(a, b):
    first = iota(a.shape, 1) < 4
    return jnp.where(first, a, pltpu.roll(b, 4, 1)), jnp.where(first, pltpu.roll(a, 4, 1), b)


def by_group(rows, local):
    if local == 1:
        return [rows]
    total, width = rows.shape
    tiles = rows.astype(F32).reshape(total // (8 * local), 2, local // 2, 8, width)
    parts = []
    for pair in range(local // 2):
        for x in trade_halves(tiles[:, 0, pair], tiles[:, 1, pair]):
            parts.append(x.reshape(total // local, width).astype(BF16))
    return parts


def by_place(parts):
    if len(parts) == 1:
        return parts[0]
    rows, width = parts[0].shape
    tiles = [x.reshape(rows // 8, 8, width) for x in parts]
    pairs = [trade_halves(tiles[n], tiles[n + 1]) for n in range(0, len(parts), 2)]
    whole = jnp.stack([jnp.stack([pair[side] for pair in pairs], 1) for side in range(2)], 1)
    return whole.reshape(rows * len(parts), width)


def attend_kernel(rows_ref, bias_ref, cot_ref, out_ref, sums_at, *, local, places):
    total, width = rows_ref.shape
    seq = total // local
    block = min(BLOCK, seq)
    wide = QPK * block
    qcols = QPK * HD
    scale = HD ** (-0.5)

    def step(first, arrived, bias):
        at = slice(0, block) if seq == block else pl.ds(first, block)
        keys = [x[:, qcols : qcols + HD] for x in arrived]
        values = [x[:, qcols + HD :] for x in arrived]
        asked = arrived if seq == block else [rows_ref[at, :]]
        queries = [jnp.concatenate([x[:, q * HD : (q + 1) * HD] for q in range(QPK)], 0) for x in asked]
        cots = [cot_ref[pl.ds((group * seq + first) * QPK, wide), :] for group in range(local)]
        scores = [nt(key, query) * (scale * math.log2(math.e)) + bias for key, query in zip(keys, queries)]
        dprobs = [nt(value, cot) for value, cot in zip(values, cots)]
        weights = [jnp.exp2(x - jnp.max(x, axis=0, keepdims=True)) for x in scores]
        probs = [(x * (1.0 / jnp.sum(x, axis=0, keepdims=True))).astype(BF16) for x in weights]
        broad = [x.astype(F32) for x in probs]
        deltas = [jnp.sum(x * y, axis=0, keepdims=True) for x, y in zip(broad, dprobs)]
        dscores = [(x * (y - z)).astype(BF16) for x, y, z in zip(broad, dprobs, deltas)]
        dqueries = [
            lax.dot_general(x, y, (((0,), (0,)), ((), ())), preferred_element_type=F32) * scale
            for x, y in zip(dscores, keys)
        ]
        dqueries = [
            jnp.concatenate([x[q * block : (q + 1) * block] for q in range(QPK)], 1) for x in dqueries
        ]
        dkeys = [jnp.dot(x, y, preferred_element_type=F32) for x, y in zip(dscores, queries)]
        dvalues = [jnp.dot(x, y, preferred_element_type=F32) for x, y in zip(probs, cots)]
        return dqueries, dkeys, dvalues

    if seq == block:
        arrived = by_group(rows_ref[...], local)
        terms = zip(*step(0, arrived, bias_ref[...]))
        parts = [jnp.concatenate([x, y * scale, z], 1) for x, y, z in terms]
        grads = by_place(parts).astype(BF16)
        if places != sorted(places):
            size = total // len(places)
            grads = jnp.concatenate([grads[n * size : (n + 1) * size] for n in places], 0)
        out_ref[...] = grads
        return
    sums_at[...] = jnp.zeros(sums_at.shape, F32)

    @pl.loop(0, seq // block)
    def _(index):
        first = pl.multiple_of(index * block, block)
        seen = iota((seq, wide), 0) <= first + rest(iota((seq, wide), 1), block)
        bias = jnp.where(seen, bias_ref[:, :1], NEG)
        (dquery,), (dkey,), (dvalue,) = step(first, [rows_ref[...]], bias)
        out_ref[pl.ds(first, block), :qcols] = dquery.astype(BF16)
        sums_at[:, :HD] += dkey
        sums_at[:, HD:] += dvalue

    out_ref[:, qcols : qcols + HD] = (sums_at[:, :HD] * scale).astype(BF16)
    out_ref[:, qcols + HD :] = sums_at[:, HD:].astype(BF16)


def gather_kernel(rows_ref, gather_ref, out_ref, *, part):
    count = out_ref.shape[0]
    pick = gather_ref[part * count : (part + 1) * count, :]
    out_ref[...] = jnp.dot(pick, rows_ref[...], preferred_element_type=F32).astype(BF16)


def finish_kernel(cos_ref, sin_ref, *refs):
    parts, (out_hbm, out_ref, out_sems) = refs[:-3], refs[-3:]
    stores = Stores(out_ref, out_hbm, out_sems)
    for at in stores.pieces():
        cosv, sinv = cos_ref[at, :], sin_ref[at, :]
        for first in range(0, out_ref.shape[1], HD):
            cols = slice(first, first + HD)
            x = sum(ref[at, cols].astype(F32) for ref in parts)
            if first < (QPK + 1) * HD:
                x = x * cosv - pltpu.roll(x, HD // 2, 1) * sinv
            out_ref[at, cols] = x.astype(BF16)
        stores.start(at)
    stores.wait()


def call(kernel, outs, *args, scratch=(), specs=None, out_spec=VMEM):
    shapes = [jax.ShapeDtypeStruct(s, d) for s, d in outs]
    single = len(shapes) == 1
    return pl.pallas_call(
        kernel,
        out_shape=shapes[0] if single else shapes,
        in_specs=specs or [VMEM] * len(args),
        out_specs=out_spec if single else [out_spec] * len(shapes),
        scratch_shapes=list(scratch),
        compiler_params=pltpu.CompilerParams(vmem_limit_bytes=48 * 2**20),
    )(*args)


def body(vision_rows, positions, destination, out_grad):
    tiles = lax.axis_size("tile")
    heads = lax.axis_size("head")
    tokens, groups, width = vision_rows.shape
    local = groups // heads
    count = tokens * groups
    seq = heads * tiles * C
    total = seq * local
    qcols = QPK * HD
    sides = 2 if heads == 2 and tiles % 2 == 0 else 1
    if local > 1 and sides * C != 4:
        raise ValueError("unsupported mesh")
    targets = destination.reshape(-1, LANES)
    rows = vision_rows.reshape(count, width)
    kernel = functools.partial

    def to_pair(x):
        return lax.ppermute(x, "tile", [(t, t ^ 1) for t in range(tiles)])

    others = [to_pair(rows), to_pair(positions)] if sides == 2 else []
    cos_own, sin_own, place = call(
        kernel(ready_kernel, tiles=tiles, local=local, sides=sides),
        [((tokens, HD), F32), ((tokens, HD), F32), ((total, sides * count), BF16)],
        *(pltpu.with_memory_space_constraint(x, pltpu.HBM) for x in (positions, targets)),
        specs=[HBM] * 2,
        scratch=(
            pltpu.VMEM(positions.shape, jnp.int32),
            pltpu.VMEM(targets.shape, jnp.int32),
            pltpu.SemaphoreType.DMA((2,)),
        ),
    )
    slots = out_grad.shape[0]
    cot_rows = out_grad.reshape(slots * groups, qcols)
    split_outs = [((slots * local, qcols), BF16)] * 2
    table_outs = [
        ((count, HD), F32),
        ((count, HD), F32),
        ((sides * count, total), BF16),
        ((seq, seq), BF16),
        ((seq, LANES if seq > BLOCK else QPK * seq), F32),
    ]
    early = []
    if sides == 2:
        early = call(
            kernel(early_kernel, tiles=tiles, heads=heads, local=local, sides=sides),
            split_outs + table_outs,
            *(pltpu.with_memory_space_constraint(x, pltpu.HBM) for x in (cot_rows, positions, targets)),
            specs=[HBM] * 3,
            scratch=(
                pltpu.VMEM(cot_rows.shape, BF16),
                pltpu.VMEM(positions.shape, jnp.int32),
                pltpu.VMEM(targets.shape, jnp.int32),
                pltpu.SemaphoreType.DMA((3,)),
            ),
        )
    outgoing = call(
        pack_kernel,
        [((total, width), BF16)],
        rows,
        cos_own,
        sin_own,
        place,
        early[0][:16, :LANES] if early else place[:16, :LANES],
        *others,
        out_spec=HBM,
        scratch=(
            pltpu.VMEM((sides * count, width), BF16),
            pltpu.VMEM((total, width), BF16),
            pltpu.SemaphoreType.DMA((PIECES,)),
        ),
    )

    def swap(rows, back=False):
        units = tiles // sides
        parts = rows.reshape(heads * units, -1, width)
        if sides == 1:
            axes, groups = ("head", "tile"), None
        else:
            axes, order = ("tile", "head"), unit_order(units, sides, back)
            groups = [
                [(unit * sides + side) * heads + head for head in range(heads) for unit in order]
                for side in range(sides)
            ]
        parts = lax.all_to_all(
            parts, axes, split_axis=0, concat_axis=0, tiled=True, axis_index_groups=groups
        )
        return parts.reshape(total, width)

    incoming = swap(outgoing)
    if sides == 2:
        own, other = call(kernel(split_kernel, local=local, sides=sides), split_outs, cot_rows, *early[:2])
        cots = [own, lax.ppermute(other, "head", [(0, 1), (1, 0)])]
    else:
        moved = lax.all_to_all(out_grad, "head", split_axis=1, concat_axis=0, tiled=True)
        cots = [jnp.swapaxes(moved, 0, 1).reshape(total, qcols)]
    cosv, sinv, gather, pick, bias = call(
        kernel(table_kernel, tiles=tiles, heads=heads, local=local, sides=sides),
        table_outs,
        positions,
        targets,
        outgoing[:16, :LANES],
        *early[2:],
    )
    cot = call(
        kernel(join_kernel, local=local),
        [((total * QPK, HD), BF16)],
        pick,
        *cots,
        scratch=(pltpu.VMEM((total, qcols), BF16),),
    )
    units = tiles // sides
    there, back = (unit_order(units, sides, way) for way in (False, True))
    places = [head * units + there.index(unit) for head in range(heads) for unit in back]
    grads = call(
        kernel(attend_kernel, local=local, places=places),
        [((total, width), BF16)],
        incoming,
        bias,
        cot,
        scratch=(pltpu.VMEM((seq if seq > BLOCK else 8, 2 * HD), F32),),
    )
    returned = swap(grads, True)

    def gathered(part):
        return call(kernel(gather_kernel, part=part), [((count, width), BF16)], returned, gather)

    parts = [to_pair(gathered(1))] if sides == 2 else []
    parts.append(gathered(0))
    result = call(
        finish_kernel,
        [((count, width), BF16)],
        cosv,
        sinv,
        *parts,
        out_spec=HBM,
        scratch=(pltpu.VMEM((count, width), BF16), pltpu.SemaphoreType.DMA((PIECES,))),
    )
    return result.reshape(tokens, groups, width)


def solution(mesh):
    return jax.shard_map(
        body,
        mesh=mesh,
        in_specs=(
            P(("tile", "head"), None, None),
            P(None, ("tile", "head")),
            P(),
            P(("tile", "head"), None, None),
        ),
        out_specs=P(("tile", "head"), None, None),
        check_vma=False,
    )
```

```python
import functools
import math

import jax
import jax.numpy as jnp
from jax import lax
from jax.experimental import pallas as pl
from jax.experimental.pallas import tpu as pltpu
from jax.sharding import PartitionSpec as P

KV = 8
HD = 128
C = 2
QPK = 4
LANES = 128
BLOCK = 64
PIECES = 2
F32 = jnp.float32
BF16 = jnp.bfloat16
NEG = -1e30
VMEM = pl.BlockSpec(memory_space=pltpu.VMEM)
HBM = pl.BlockSpec(memory_space=pltpu.HBM)


def nt(a, b):
    return lax.dot_general(a, b, (((1,), (1,)), ((), ())), preferred_element_type=F32)


def iota(shape, dim):
    return lax.broadcasted_iota(jnp.int32, shape, dim)


def over(at, size):
    if size & (size - 1):
        return at // size
    return lax.shift_right_logical(at, jnp.int32(size.bit_length() - 1))


def rest(at, size):
    return at % size if size & (size - 1) else at & (size - 1)


def rope_parts(tokens):
    half = HD // 2
    slots = rest(iota((tokens, HD), 1), half)
    freq = jnp.exp(-(2.0 * slots.astype(F32) / HD) * math.log(1000000.0))
    sign = jnp.where(iota((tokens, HD), 1) < half, -1.0, 1.0)
    eye = (iota((tokens, tokens), 0) == iota((tokens, tokens), 1)).astype(BF16)
    return slots, freq, sign, eye


def rope_tables(pos_ref, parts=None):
    tokens = pos_ref.shape[1]
    slots, freq, sign, eye = parts or rope_parts(tokens)
    first = HD // 2 // 4
    second = (HD // 2 - first) // 2
    column = [
        nt(eye, jnp.broadcast_to(pos_ref[s : s + 1, :].astype(F32).astype(BF16), (HD, tokens)))
        for s in range(3)
    ]
    chosen = jnp.where(
        slots < first, column[0], jnp.where(slots < first + second, column[1], column[2])
    )
    angle = chosen * freq
    return jnp.cos(angle), jnp.sin(angle) * sign


def per_group(table):
    tokens = table.shape[0]
    return jnp.broadcast_to(table[:, None, :], (tokens, KV, HD)).reshape(tokens * KV, HD)


def token_finders(tokens, tile):
    start = (tile * lax.axis_size("head") + lax.axis_index("head")) * tokens
    count = tokens * KV
    off = start % LANES
    wide = (iota((count, LANES), 1) == off + over(iota((count, LANES), 0), KV)).astype(BF16)
    narrow = (iota((tokens, LANES), 1) == off + iota((tokens, LANES), 0)).astype(BF16)
    return start // LANES, wide, narrow


def token_slots(dest_ref, finders):
    at, wide, narrow = finders
    count, tokens = wide.shape[0], narrow.shape[0]
    row = dest_ref[pl.ds(at, 1), :].astype(F32).astype(BF16)
    along = nt(jnp.broadcast_to(row, (8, LANES)), wide)[:1]
    down = nt(narrow, jnp.broadcast_to(row, (count, LANES)))
    lane = iota((tokens, count), 1)
    earlier = (down == along) & (iota((tokens, count), 0) < over(lane, KV))
    rank = jnp.sum(earlier.astype(F32), axis=0, keepdims=True)
    return (along * C + rank).astype(jnp.int32)


def row_parts(at, tiles, local, sides, back=False):
    rank, at = rest(at, C), over(at, C)
    side, at = rest(at, sides), over(at, sides)
    group, at = rest(at, local), over(at, local)
    units = tiles // sides
    order = unit_order(units, sides, back)
    place, head = rest(at, units), over(at, units)
    if order == [(n + order[0]) % units for n in range(units)]:
        unit = rest(place + order[0], units)
    else:
        unit = sum(jnp.where(place == n, order[n], 0) for n in range(units))
    return head, unit, side, rank, group


def unit_order(units, sides, back):
    if sides == 1:
        return list(range(units))
    if back and units == 8:
        return [z * 2 for z in (2, 1, 0, 3)] + [z * 2 + 1 for z in (3, 2, 1, 0)]
    return [(n + units // 2) % units for n in range(units)]


def placement_parts(tokens, tiles, local, sides, total, back=False):
    tile = lax.axis_index("tile")
    side = tile % sides
    head, unit, at_side, rank, group = row_parts(iota((total, LANES), 0), tiles, local, sides, back)
    target = unit * sides + side
    rows = (((target * C + rank) * sides + at_side) * KV + head * local + group)[:, :1]
    from_sides = [side + other - 2 * side * other for other in range(sides)]
    return rows, [(n, token_finders(tokens, tile - side + n)) for n in from_sides]


def placement(dest_ref, parts):
    rows, devices = parts
    places = []
    for from_side, finders in devices:
        count = finders[1].shape[0]
        slots = token_slots(dest_ref, finders)
        lanes = (slots * len(devices) + from_side) * KV + rest(iota((1, count), 1), KV)
        places.append((rows == lanes).astype(F32))
    return places[0] if len(places) == 1 else jnp.concatenate(places, 1)


def ready_kernel(pos_hbm, dest_hbm, cos_ref, sin_ref, place_ref, pos_ref, dest_ref, sems, *, tiles, local, sides):
    pairs = ((dest_hbm, dest_ref), (pos_hbm, pos_ref))
    loads = [pltpu.make_async_copy(a, b, sems.at[n]) for n, (a, b) in enumerate(pairs)]
    for load in loads:
        load.start()
    tokens = pos_ref.shape[1]
    place_parts = placement_parts(tokens, tiles, local, sides, place_ref.shape[0])
    angle_parts = rope_parts(tokens)
    for load in loads:
        load.wait()
    place_ref[...] = placement(dest_ref, place_parts).astype(BF16)
    cos_ref[...], sin_ref[...] = rope_tables(pos_ref, angle_parts)


def turn(from_ref, to_ref, cosv, sinv):
    for at in range(0, from_ref.shape[1], HD):
        x = from_ref[:, at : at + HD]
        if at < (QPK + 1) * HD:
            x = x.astype(F32)
            x = (x * cosv + pltpu.roll(x, HD // 2, 1) * sinv).astype(BF16)
        to_ref[:, at : at + HD] = x


def pack_kernel(vis_ref, cos_ref, sin_ref, place_ref, after_ref, *refs):
    del after_ref
    others, (out_hbm, both_ref, out_ref, out_sems) = refs[:-4], refs[-4:]
    count = vis_ref.shape[0]
    turn(vis_ref, both_ref.at[:count, :], per_group(cos_ref[...]), per_group(sin_ref[...]))
    if others:
        vis_ref, pos_ref = others
        cosv, sinv = rope_tables(pos_ref)
        turn(vis_ref, both_ref.at[count:, :], per_group(cosv), per_group(sinv))
    stores = Stores(out_ref, out_hbm, out_sems)
    for at in stores.pieces():
        out_ref[at, :] = jnp.dot(place_ref[at, :], both_ref[...], preferred_element_type=F32).astype(BF16)
        stores.start(at)
    stores.wait()


class Stores:
    def __init__(self, source, target, sems):
        self.source, self.target, self.sems, self.copies = source, target, sems, []

    def pieces(self):
        size = self.source.shape[0] // PIECES
        return [slice(n * size, (n + 1) * size) for n in range(PIECES)]

    def start(self, at):
        sem = self.sems.at[len(self.copies)]
        copy = pltpu.make_async_copy(self.source.at[at, :], self.target.at[at, :], sem)
        copy.start()
        self.copies.append(copy)

    def wait(self):
        for copy in self.copies:
            copy.wait()


def fill_tables(pos_ref, dest_ref, table_refs, tiles, heads, local, sides):
    cos_ref, sin_ref, gather_ref, pick_ref, bias_ref = table_refs
    tokens = pos_ref.shape[1]
    seq = heads * tiles * C
    cosv, sinv = rope_tables(pos_ref)
    cos_ref[...] = per_group(cosv)
    sin_ref[...] = per_group(sinv)
    place = placement(dest_ref, placement_parts(tokens, tiles, local, sides, seq * local, True))
    gather_ref[...] = jnp.transpose(place).astype(BF16)
    mine = lax.axis_index("tile")

    def slot_of(at):
        head, unit, side, rank, _ = row_parts(at, tiles, 1, sides)
        return (head * tiles + unit * sides + side) * C + rank

    slot = slot_of(iota((seq, LANES), 0))
    device = rest(over(slot, C), tiles) * heads + over(slot, tiles * C)

    def tally(block, sums):
        hit = (dest_ref[pl.ds(block, 1), :] == mine).astype(F32).astype(BF16)
        source = over(block * LANES + iota((seq, LANES), 1), tokens)
        return sums + nt((source == device).astype(F32).astype(BF16), jnp.broadcast_to(hit, (LANES, LANES)))

    counts = lax.fori_loop(0, dest_ref.shape[0], tally, jnp.zeros((seq, LANES), F32))
    taken = counts > rest(slot, C).astype(F32)
    pick_ref[...] = ((slot[:, :1] == iota((seq, seq), 1)) & taken[:, :1]).astype(F32).astype(BF16)
    key_ok = jnp.where(taken, 0.0, NEG)
    if seq > BLOCK:
        bias_ref[...] = key_ok
    else:
        query = slot_of(rest(iota(bias_ref.shape, 1), seq))
        bias_ref[...] = jnp.where(slot[:, :1] <= query, key_ok[:, :1], NEG)


def split_cots(cot_ref, own_ref, other_ref, local):
    head = lax.axis_index("head")
    total, count = own_ref.shape[0], cot_ref.shape[0]
    slots = total // local
    row, lane = iota((total, count), 0), iota((total, count), 1)
    base = rest(row, slots) * KV + over(row, slots)
    cot = cot_ref[...]
    for ref, group in ((own_ref, head), (other_ref, 1 - head)):
        pick = (lane == base + group * local).astype(BF16)
        ref[...] = jnp.dot(pick, cot, preferred_element_type=F32).astype(BF16)


def is_late(sides):
    return lax.axis_index("tile") % sides == 0


def early_kernel(cot_hbm, pos_hbm, dest_hbm, *refs, tiles, heads, local, sides):
    *out_refs, cot_ref, pos_ref, dest_ref, sems = refs

    @pl.when(is_late(sides))
    def _():
        pairs = ((dest_hbm, dest_ref), (pos_hbm, pos_ref), (cot_hbm, cot_ref))
        loads = [pltpu.make_async_copy(a, b, sems.at[n]) for n, (a, b) in enumerate(pairs)]
        for load in loads:
            load.start()
        for load in loads:
            load.wait()
        split_cots(cot_ref, *out_refs[:2], local)
        fill_tables(pos_ref, dest_ref, out_refs[2:], tiles, heads, local, sides)


def table_kernel(pos_ref, dest_ref, after_ref, *refs, tiles, heads, local, sides):
    del after_ref
    if sides == 1:
        fill_tables(pos_ref, dest_ref, refs, tiles, heads, local, sides)
        return
    early_refs, out_refs = refs[: len(refs) // 2], refs[len(refs) // 2 :]

    @pl.when(is_late(sides))
    def _():
        for from_ref, to_ref in zip(early_refs, out_refs):
            to_ref[...] = from_ref[...]

    @pl.when(jnp.logical_not(is_late(sides)))
    def _():
        fill_tables(pos_ref, dest_ref, out_refs, tiles, heads, local, sides)


def split_kernel(cot_ref, own_early, other_early, own_ref, other_ref, *, local, sides):
    @pl.when(is_late(sides))
    def _():
        own_ref[...] = own_early[...]
        other_ref[...] = other_early[...]

    @pl.when(jnp.logical_not(is_late(sides)))
    def _():
        split_cots(cot_ref, own_ref, other_ref, local)


def join_kernel(pick_ref, *refs, local):
    cot_refs, (out_ref, whole) = refs[:-2], refs[-2:]
    seq = pick_ref.shape[0]
    block = min(BLOCK, seq)
    if len(cot_refs) == 2:
        half = seq // 2
        head = lax.axis_index("head")
        for ref, place in zip(cot_refs, (head, 1 - head)):
            for g in range(local):
                at = pl.multiple_of(g * seq + place * half, half)
                whole[pl.ds(at, half), :] = ref[g * half : (g + 1) * half, :]
    else:
        whole[...] = cot_refs[0][...]
    for first in range(0, seq, block):
        pick = pick_ref[first : first + block, :]
        for g in range(local):
            rows = whole[g * seq : (g + 1) * seq, :]
            part = jnp.dot(pick, rows, preferred_element_type=F32).astype(BF16)
            for q in range(QPK):
                at = (g * seq + first) * QPK + q * block
                out_ref[at : at + block, :] = part[:, q * HD : (q + 1) * HD]


def trade_halves(a, b):
    first = iota(a.shape, 1) < 4
    return jnp.where(first, a, pltpu.roll(b, 4, 1)), jnp.where(first, pltpu.roll(a, 4, 1), b)


def by_group(rows, local):
    if local == 1:
        return [rows]
    total, width = rows.shape
    tiles = rows.astype(F32).reshape(total // (8 * local), 2, local // 2, 8, width)
    parts = []
    for pair in range(local // 2):
        for x in trade_halves(tiles[:, 0, pair], tiles[:, 1, pair]):
            parts.append(x.reshape(total // local, width).astype(BF16))
    return parts


def by_place(parts):
    if len(parts) == 1:
        return parts[0]
    rows, width = parts[0].shape
    tiles = [x.reshape(rows // 8, 8, width) for x in parts]
    pairs = [trade_halves(tiles[n], tiles[n + 1]) for n in range(0, len(parts), 2)]
    whole = jnp.stack([jnp.stack([pair[side] for pair in pairs], 1) for side in range(2)], 1)
    return whole.reshape(rows * len(parts), width)


def attend_kernel(rows_ref, bias_ref, cot_ref, out_ref, sums_at, *, local, places):
    total, width = rows_ref.shape
    seq = total // local
    block = min(BLOCK, seq)
    wide = QPK * block
    qcols = QPK * HD
    scale = HD ** (-0.5)

    def step(first, arrived, bias):
        at = slice(0, block) if seq == block else pl.ds(first, block)
        keys = [x[:, qcols : qcols + HD] for x in arrived]
        values = [x[:, qcols + HD :] for x in arrived]
        asked = arrived if seq == block else [rows_ref[at, :]]
        queries = [jnp.concatenate([x[:, q * HD : (q + 1) * HD] for q in range(QPK)], 0) for x in asked]
        cots = [cot_ref[pl.ds((group * seq + first) * QPK, wide), :] for group in range(local)]
        scores = [nt(key, query) * (scale * math.log2(math.e)) + bias for key, query in zip(keys, queries)]
        dprobs = [nt(value, cot) for value, cot in zip(values, cots)]
        weights = [jnp.exp2(x - jnp.max(x, axis=0, keepdims=True)) for x in scores]
        probs = [(x * (1.0 / jnp.sum(x, axis=0, keepdims=True))).astype(BF16) for x in weights]
        broad = [x.astype(F32) for x in probs]
        deltas = [jnp.sum(x * y, axis=0, keepdims=True) for x, y in zip(broad, dprobs)]
        dscores = [(x * (y - z)).astype(BF16) for x, y, z in zip(broad, dprobs, deltas)]
        dqueries = [
            lax.dot_general(x, y, (((0,), (0,)), ((), ())), preferred_element_type=F32) * scale
            for x, y in zip(dscores, keys)
        ]
        dqueries = [
            jnp.concatenate([x[q * block : (q + 1) * block] for q in range(QPK)], 1) for x in dqueries
        ]
        dkeys = [jnp.dot(x, y, preferred_element_type=F32) for x, y in zip(dscores, queries)]
        dvalues = [jnp.dot(x, y, preferred_element_type=F32) for x, y in zip(probs, cots)]
        return dqueries, dkeys, dvalues

    if seq == block:
        arrived = by_group(rows_ref[...], local)
        terms = zip(*step(0, arrived, bias_ref[...]))
        parts = [jnp.concatenate([x, y * scale, z], 1) for x, y, z in terms]
        grads = by_place(parts).astype(BF16)
        if places != sorted(places):
            size = total // len(places)
            grads = jnp.concatenate([grads[n * size : (n + 1) * size] for n in places], 0)
        out_ref[...] = grads
        return
    sums_at[...] = jnp.zeros(sums_at.shape, F32)

    @pl.loop(0, seq // block)
    def _(index):
        first = pl.multiple_of(index * block, block)
        seen = iota((seq, wide), 0) <= first + rest(iota((seq, wide), 1), block)
        bias = jnp.where(seen, bias_ref[:, :1], NEG)
        (dquery,), (dkey,), (dvalue,) = step(first, [rows_ref[...]], bias)
        out_ref[pl.ds(first, block), :qcols] = dquery.astype(BF16)
        sums_at[:, :HD] += dkey
        sums_at[:, HD:] += dvalue

    out_ref[:, qcols : qcols + HD] = (sums_at[:, :HD] * scale).astype(BF16)
    out_ref[:, qcols + HD :] = sums_at[:, HD:].astype(BF16)


def gather_kernel(rows_ref, gather_ref, out_ref, *, part):
    count = out_ref.shape[0]
    pick = gather_ref[part * count : (part + 1) * count, :]
    out_ref[...] = jnp.dot(pick, rows_ref[...], preferred_element_type=F32).astype(BF16)


def finish_kernel(cos_ref, sin_ref, *refs):
    parts, (out_hbm, out_ref, out_sems) = refs[:-3], refs[-3:]
    stores = Stores(out_ref, out_hbm, out_sems)
    for at in stores.pieces():
        cosv, sinv = cos_ref[at, :], sin_ref[at, :]
        for first in range(0, out_ref.shape[1], HD):
            cols = slice(first, first + HD)
            x = sum(ref[at, cols].astype(F32) for ref in parts)
            if first < (QPK + 1) * HD:
                x = x * cosv - pltpu.roll(x, HD // 2, 1) * sinv
            out_ref[at, cols] = x.astype(BF16)
        stores.start(at)
    stores.wait()


def call(kernel, outs, *args, scratch=(), specs=None, out_spec=VMEM):
    shapes = [jax.ShapeDtypeStruct(s, d) for s, d in outs]
    single = len(shapes) == 1
    return pl.pallas_call(
        kernel,
        out_shape=shapes[0] if single else shapes,
        in_specs=specs or [VMEM] * len(args),
        out_specs=out_spec if single else [out_spec] * len(shapes),
        scratch_shapes=list(scratch),
        compiler_params=pltpu.CompilerParams(vmem_limit_bytes=48 * 2**20),
    )(*args)


def body(vision_rows, positions, destination, out_grad):
    tiles = lax.axis_size("tile")
    heads = lax.axis_size("head")
    tokens, groups, width = vision_rows.shape
    local = groups // heads
    count = tokens * groups
    seq = heads * tiles * C
    total = seq * local
    qcols = QPK * HD
    sides = 2 if heads == 2 and tiles % 2 == 0 else 1
    if local > 1 and sides * C != 4:
        raise ValueError("unsupported mesh")
    targets = destination.reshape(-1, LANES)
    rows = vision_rows.reshape(count, width)
    kernel = functools.partial

    def to_pair(x):
        return lax.ppermute(x, "tile", [(t, t ^ 1) for t in range(tiles)])

    others = [to_pair(rows), to_pair(positions)] if sides == 2 else []
    cos_own, sin_own, place = call(
        kernel(ready_kernel, tiles=tiles, local=local, sides=sides),
        [((tokens, HD), F32), ((tokens, HD), F32), ((total, sides * count), BF16)],
        *(pltpu.with_memory_space_constraint(x, pltpu.HBM) for x in (positions, targets)),
        specs=[HBM] * 2,
        scratch=(
            pltpu.VMEM(positions.shape, jnp.int32),
            pltpu.VMEM(targets.shape, jnp.int32),
            pltpu.SemaphoreType.DMA((2,)),
        ),
    )
    slots = out_grad.shape[0]
    cot_rows = out_grad.reshape(slots * groups, qcols)
    split_outs = [((slots * local, qcols), BF16)] * 2
    table_outs = [
        ((count, HD), F32),
        ((count, HD), F32),
        ((sides * count, total), BF16),
        ((seq, seq), BF16),
        ((seq, LANES if seq > BLOCK else QPK * seq), F32),
    ]
    early = []
    if sides == 2:
        early = call(
            kernel(early_kernel, tiles=tiles, heads=heads, local=local, sides=sides),
            split_outs + table_outs,
            *(pltpu.with_memory_space_constraint(x, pltpu.HBM) for x in (cot_rows, positions, targets)),
            specs=[HBM] * 3,
            scratch=(
                pltpu.VMEM(cot_rows.shape, BF16),
                pltpu.VMEM(positions.shape, jnp.int32),
                pltpu.VMEM(targets.shape, jnp.int32),
                pltpu.SemaphoreType.DMA((3,)),
            ),
        )
    outgoing = call(
        pack_kernel,
        [((total, width), BF16)],
        rows,
        cos_own,
        sin_own,
        place,
        early[0][:16, :LANES] if early else place[:16, :LANES],
        *others,
        out_spec=HBM,
        scratch=(
            pltpu.VMEM((sides * count, width), BF16),
            pltpu.VMEM((total, width), BF16),
            pltpu.SemaphoreType.DMA((PIECES,)),
        ),
    )

    def swap(rows, back=False):
        units = tiles // sides
        parts = rows.reshape(heads * units, -1, width)
        if sides == 1:
            axes, groups = ("head", "tile"), None
        else:
            axes, order = ("tile", "head"), unit_order(units, sides, back)
            groups = [
                [(unit * sides + side) * heads + head for head in range(heads) for unit in order]
                for side in range(sides)
            ]
        parts = lax.all_to_all(
            parts, axes, split_axis=0, concat_axis=0, tiled=True, axis_index_groups=groups
        )
        return parts.reshape(total, width)

    incoming = swap(outgoing)
    if sides == 2:
        own, other = call(kernel(split_kernel, local=local, sides=sides), split_outs, cot_rows, *early[:2])
        cots = [own, lax.ppermute(other, "head", [(0, 1), (1, 0)])]
    else:
        moved = lax.all_to_all(out_grad, "head", split_axis=1, concat_axis=0, tiled=True)
        cots = [jnp.swapaxes(moved, 0, 1).reshape(total, qcols)]
    cosv, sinv, gather, pick, bias = call(
        kernel(table_kernel, tiles=tiles, heads=heads, local=local, sides=sides),
        table_outs,
        positions,
        targets,
        outgoing[:16, :LANES],
        *early[2:],
    )
    cot = call(
        kernel(join_kernel, local=local),
        [((total * QPK, HD), BF16)],
        pick,
        *cots,
        scratch=(pltpu.VMEM((total, qcols), BF16),),
    )
    units = tiles // sides
    there, back = (unit_order(units, sides, way) for way in (False, True))
    places = [head * units + there.index(unit) for head in range(heads) for unit in back]
    grads = call(
        kernel(attend_kernel, local=local, places=places),
        [((total, width), BF16)],
        incoming,
        bias,
        cot,
        scratch=(pltpu.VMEM((seq if seq > BLOCK else 8, 2 * HD), F32),),
    )
    returned = swap(grads, True)

    def gathered(part):
        return call(kernel(gather_kernel, part=part), [((count, width), BF16)], returned, gather)

    parts = [to_pair(gathered(1))] if sides == 2 else []
    parts.append(gathered(0))
    result = call(
        finish_kernel,
        [((count, width), BF16)],
        cosv,
        sinv,
        *parts,
        out_spec=HBM,
        scratch=(pltpu.VMEM((count, width), BF16), pltpu.SemaphoreType.DMA((PIECES,))),
    )
    return result.reshape(tokens, groups, width)


def solution(mesh):
    return jax.shard_map(
        body,
        mesh=mesh,
        in_specs=(
            P(("tile", "head"), None, None),
            P(None, ("tile", "head")),
            P(),
            P(("tile", "head"), None, None),
        ),
        out_specs=P(("tile", "head"), None, None),
        check_vma=False,
    )
```

```python
import functools
import math

import jax
import jax.numpy as jnp
from jax import lax
from jax.experimental import pallas as pl
from jax.experimental.pallas import tpu as pltpu
from jax.sharding import PartitionSpec as P

KV = 8
HD = 128
C = 2
QPK = 4
LANES = 128
BLOCK = 64
PIECES = 2
F32 = jnp.float32
BF16 = jnp.bfloat16
NEG = -1e30
VMEM = pl.BlockSpec(memory_space=pltpu.VMEM)
HBM = pl.BlockSpec(memory_space=pltpu.HBM)


def nt(a, b):
    return lax.dot_general(a, b, (((1,), (1,)), ((), ())), preferred_element_type=F32)


def iota(shape, dim):
    return lax.broadcasted_iota(jnp.int32, shape, dim)


def over(at, size):
    if size & (size - 1):
        return at // size
    return lax.shift_right_logical(at, jnp.int32(size.bit_length() - 1))


def rest(at, size):
    return at % size if size & (size - 1) else at & (size - 1)


def rope_parts(tokens):
    half = HD // 2
    slots = rest(iota((tokens, HD), 1), half)
    freq = jnp.exp(-(2.0 * slots.astype(F32) / HD) * math.log(1000000.0))
    sign = jnp.where(iota((tokens, HD), 1) < half, -1.0, 1.0)
    eye = (iota((tokens, tokens), 0) == iota((tokens, tokens), 1)).astype(BF16)
    return slots, freq, sign, eye


def rope_tables(pos_ref, parts=None):
    tokens = pos_ref.shape[1]
    slots, freq, sign, eye = parts or rope_parts(tokens)
    first = HD // 2 // 4
    second = (HD // 2 - first) // 2
    column = [
        nt(eye, jnp.broadcast_to(pos_ref[s : s + 1, :].astype(F32).astype(BF16), (HD, tokens)))
        for s in range(3)
    ]
    chosen = jnp.where(
        slots < first, column[0], jnp.where(slots < first + second, column[1], column[2])
    )
    angle = chosen * freq
    return jnp.cos(angle), jnp.sin(angle) * sign


def per_group(table):
    tokens = table.shape[0]
    return jnp.broadcast_to(table[:, None, :], (tokens, KV, HD)).reshape(tokens * KV, HD)


def token_finders(tokens, tile):
    start = (tile * lax.axis_size("head") + lax.axis_index("head")) * tokens
    count = tokens * KV
    off = start % LANES
    wide = (iota((count, LANES), 1) == off + over(iota((count, LANES), 0), KV)).astype(BF16)
    narrow = (iota((tokens, LANES), 1) == off + iota((tokens, LANES), 0)).astype(BF16)
    return start // LANES, wide, narrow


def token_slots(dest_ref, finders):
    at, wide, narrow = finders
    count, tokens = wide.shape[0], narrow.shape[0]
    row = dest_ref[pl.ds(at, 1), :].astype(F32).astype(BF16)
    along = nt(jnp.broadcast_to(row, (8, LANES)), wide)[:1]
    down = nt(narrow, jnp.broadcast_to(row, (count, LANES)))
    lane = iota((tokens, count), 1)
    earlier = (down == along) & (iota((tokens, count), 0) < over(lane, KV))
    rank = jnp.sum(earlier.astype(F32), axis=0, keepdims=True)
    return (along * C + rank).astype(jnp.int32)


def row_parts(at, tiles, local, sides, back=False):
    rank, at = rest(at, C), over(at, C)
    side, at = rest(at, sides), over(at, sides)
    group, at = rest(at, local), over(at, local)
    units = tiles // sides
    order = unit_order(units, sides, back)
    place, head = rest(at, units), over(at, units)
    if order == [(n + order[0]) % units for n in range(units)]:
        unit = rest(place + order[0], units)
    else:
        unit = sum(jnp.where(place == n, order[n], 0) for n in range(units))
    return head, unit, side, rank, group


def unit_order(units, sides, back):
    if sides == 1:
        return list(range(units))
    if back and units == 8:
        return [z * 2 for z in (2, 1, 0, 3)] + [z * 2 + 1 for z in (3, 2, 1, 0)]
    return [(n + units // 2) % units for n in range(units)]


def placement_parts(tokens, tiles, local, sides, total, back=False):
    tile = lax.axis_index("tile")
    side = tile % sides
    head, unit, at_side, rank, group = row_parts(iota((total, LANES), 0), tiles, local, sides, back)
    target = unit * sides + side
    rows = (((target * C + rank) * sides + at_side) * KV + head * local + group)[:, :1]
    from_sides = [side + other - 2 * side * other for other in range(sides)]
    return rows, [(n, token_finders(tokens, tile - side + n)) for n in from_sides]


def placement(dest_ref, parts):
    rows, devices = parts
    places = []
    for from_side, finders in devices:
        count = finders[1].shape[0]
        slots = token_slots(dest_ref, finders)
        lanes = (slots * len(devices) + from_side) * KV + rest(iota((1, count), 1), KV)
        places.append((rows == lanes).astype(F32))
    return places[0] if len(places) == 1 else jnp.concatenate(places, 1)


def ready_kernel(pos_hbm, dest_hbm, cos_ref, sin_ref, place_ref, pos_ref, dest_ref, sems, *, tiles, local, sides):
    pairs = ((dest_hbm, dest_ref), (pos_hbm, pos_ref))
    loads = [pltpu.make_async_copy(a, b, sems.at[n]) for n, (a, b) in enumerate(pairs)]
    for load in loads:
        load.start()
    tokens = pos_ref.shape[1]
    place_parts = placement_parts(tokens, tiles, local, sides, place_ref.shape[0])
    angle_parts = rope_parts(tokens)
    for load in loads:
        load.wait()
    place_ref[...] = placement(dest_ref, place_parts).astype(BF16)
    cos_ref[...], sin_ref[...] = rope_tables(pos_ref, angle_parts)


def turn(from_ref, to_ref, cosv, sinv):
    for at in range(0, from_ref.shape[1], HD):
        x = from_ref[:, at : at + HD]
        if at < (QPK + 1) * HD:
            x = x.astype(F32)
            x = (x * cosv + pltpu.roll(x, HD // 2, 1) * sinv).astype(BF16)
        to_ref[:, at : at + HD] = x


def pack_kernel(vis_ref, cos_ref, sin_ref, place_ref, after_ref, *refs):
    del after_ref
    others, (out_hbm, both_ref, out_ref, out_sems) = refs[:-4], refs[-4:]
    count = vis_ref.shape[0]
    turn(vis_ref, both_ref.at[:count, :], per_group(cos_ref[...]), per_group(sin_ref[...]))
    if others:
        vis_ref, pos_ref = others
        cosv, sinv = rope_tables(pos_ref)
        turn(vis_ref, both_ref.at[count:, :], per_group(cosv), per_group(sinv))
    stores = Stores(out_ref, out_hbm, out_sems)
    for at in stores.pieces():
        out_ref[at, :] = jnp.dot(place_ref[at, :], both_ref[...], preferred_element_type=F32).astype(BF16)
        stores.start(at)
    stores.wait()


class Stores:
    def __init__(self, source, target, sems):
        self.source, self.target, self.sems, self.copies = source, target, sems, []

    def pieces(self):
        size = self.source.shape[0] // PIECES
        return [slice(n * size, (n + 1) * size) for n in range(PIECES)]

    def start(self, at):
        sem = self.sems.at[len(self.copies)]
        copy = pltpu.make_async_copy(self.source.at[at, :], self.target.at[at, :], sem)
        copy.start()
        self.copies.append(copy)

    def wait(self):
        for copy in self.copies:
            copy.wait()


def fill_tables(pos_ref, dest_ref, table_refs, tiles, heads, local, sides):
    cos_ref, sin_ref, gather_ref, pick_ref, bias_ref = table_refs
    tokens = pos_ref.shape[1]
    seq = heads * tiles * C
    cosv, sinv = rope_tables(pos_ref)
    cos_ref[...] = per_group(cosv)
    sin_ref[...] = per_group(sinv)
    place = placement(dest_ref, placement_parts(tokens, tiles, local, sides, seq * local, True))
    gather_ref[...] = jnp.transpose(place).astype(BF16)
    mine = lax.axis_index("tile")

    def slot_of(at):
        head, unit, side, rank, _ = row_parts(at, tiles, 1, sides)
        return (head * tiles + unit * sides + side) * C + rank

    slot = slot_of(iota((seq, LANES), 0))
    device = rest(over(slot, C), tiles) * heads + over(slot, tiles * C)

    def tally(block, sums):
        hit = (dest_ref[pl.ds(block, 1), :] == mine).astype(F32).astype(BF16)
        source = over(block * LANES + iota((seq, LANES), 1), tokens)
        return sums + nt((source == device).astype(F32).astype(BF16), jnp.broadcast_to(hit, (LANES, LANES)))

    counts = lax.fori_loop(0, dest_ref.shape[0], tally, jnp.zeros((seq, LANES), F32))
    taken = counts > rest(slot, C).astype(F32)
    pick_ref[...] = ((slot[:, :1] == iota((seq, seq), 1)) & taken[:, :1]).astype(F32).astype(BF16)
    key_ok = jnp.where(taken, 0.0, NEG)
    if seq > BLOCK:
        bias_ref[...] = key_ok
    else:
        query = slot_of(rest(iota(bias_ref.shape, 1), seq))
        bias_ref[...] = jnp.where(slot[:, :1] <= query, key_ok[:, :1], NEG)


def split_cots(cot_ref, own_ref, other_ref, local):
    head = lax.axis_index("head")
    total, count = own_ref.shape[0], cot_ref.shape[0]
    slots = total // local
    row, lane = iota((total, count), 0), iota((total, count), 1)
    base = rest(row, slots) * KV + over(row, slots)
    cot = cot_ref[...]
    for ref, group in ((own_ref, head), (other_ref, 1 - head)):
        pick = (lane == base + group * local).astype(BF16)
        ref[...] = jnp.dot(pick, cot, preferred_element_type=F32).astype(BF16)


def is_late(sides):
    return lax.axis_index("tile") % sides == 0


def early_kernel(cot_hbm, pos_hbm, dest_hbm, *refs, tiles, heads, local, sides):
    *out_refs, cot_ref, pos_ref, dest_ref, sems = refs

    @pl.when(is_late(sides))
    def _():
        pairs = ((dest_hbm, dest_ref), (pos_hbm, pos_ref), (cot_hbm, cot_ref))
        loads = [pltpu.make_async_copy(a, b, sems.at[n]) for n, (a, b) in enumerate(pairs)]
        for load in loads:
            load.start()
        for load in loads[:2]:
            load.wait()
        fill_tables(pos_ref, dest_ref, out_refs[2:], tiles, heads, local, sides)
        loads[2].wait()
        split_cots(cot_ref, *out_refs[:2], local)


def table_kernel(pos_ref, dest_ref, after_ref, *refs, tiles, heads, local, sides):
    del after_ref
    if sides == 1:
        fill_tables(pos_ref, dest_ref, refs, tiles, heads, local, sides)
        return
    early_refs, out_refs = refs[: len(refs) // 2], refs[len(refs) // 2 :]

    @pl.when(is_late(sides))
    def _():
        for from_ref, to_ref in zip(early_refs, out_refs):
            to_ref[...] = from_ref[...]

    @pl.when(jnp.logical_not(is_late(sides)))
    def _():
        fill_tables(pos_ref, dest_ref, out_refs, tiles, heads, local, sides)


def split_kernel(cot_ref, own_early, other_early, own_ref, other_ref, *, local, sides):
    @pl.when(is_late(sides))
    def _():
        own_ref[...] = own_early[...]
        other_ref[...] = other_early[...]

    @pl.when(jnp.logical_not(is_late(sides)))
    def _():
        split_cots(cot_ref, own_ref, other_ref, local)


def join_kernel(pick_ref, *refs, local):
    cot_refs, (out_ref, whole) = refs[:-2], refs[-2:]
    seq = pick_ref.shape[0]
    block = min(BLOCK, seq)
    if len(cot_refs) == 2:
        half = seq // 2
        head = lax.axis_index("head")
        for ref, place in zip(cot_refs, (head, 1 - head)):
            for g in range(local):
                at = pl.multiple_of(g * seq + place * half, half)
                whole[pl.ds(at, half), :] = ref[g * half : (g + 1) * half, :]
    else:
        whole[...] = cot_refs[0][...]
    for first in range(0, seq, block):
        pick = pick_ref[first : first + block, :]
        for g in range(local):
            rows = whole[g * seq : (g + 1) * seq, :]
            part = jnp.dot(pick, rows, preferred_element_type=F32).astype(BF16)
            for q in range(QPK):
                at = (g * seq + first) * QPK + q * block
                out_ref[at : at + block, :] = part[:, q * HD : (q + 1) * HD]


def trade_halves(a, b):
    first = iota(a.shape, 1) < 4
    return jnp.where(first, a, pltpu.roll(b, 4, 1)), jnp.where(first, pltpu.roll(a, 4, 1), b)


def by_group(rows, local):
    if local == 1:
        return [rows]
    total, width = rows.shape
    tiles = rows.astype(F32).reshape(total // (8 * local), 2, local // 2, 8, width)
    parts = []
    for pair in range(local // 2):
        for x in trade_halves(tiles[:, 0, pair], tiles[:, 1, pair]):
            parts.append(x.reshape(total // local, width).astype(BF16))
    return parts


def by_place(parts):
    if len(parts) == 1:
        return parts[0]
    rows, width = parts[0].shape
    tiles = [x.reshape(rows // 8, 8, width) for x in parts]
    pairs = [trade_halves(tiles[n], tiles[n + 1]) for n in range(0, len(parts), 2)]
    whole = jnp.stack([jnp.stack([pair[side] for pair in pairs], 1) for side in range(2)], 1)
    return whole.reshape(rows * len(parts), width)


def attend_kernel(rows_ref, bias_ref, cot_ref, out_ref, sums_at, *, local, places):
    total, width = rows_ref.shape
    seq = total // local
    block = min(BLOCK, seq)
    wide = QPK * block
    qcols = QPK * HD
    scale = HD ** (-0.5)

    def step(first, arrived, bias):
        at = slice(0, block) if seq == block else pl.ds(first, block)
        keys = [x[:, qcols : qcols + HD] for x in arrived]
        values = [x[:, qcols + HD :] for x in arrived]
        asked = arrived if seq == block else [rows_ref[at, :]]
        queries = [jnp.concatenate([x[:, q * HD : (q + 1) * HD] for q in range(QPK)], 0) for x in asked]
        cots = [cot_ref[pl.ds((group * seq + first) * QPK, wide), :] for group in range(local)]
        scores = [nt(key, query) * (scale * math.log2(math.e)) + bias for key, query in zip(keys, queries)]
        dprobs = [nt(value, cot) for value, cot in zip(values, cots)]
        weights = [jnp.exp2(x - jnp.max(x, axis=0, keepdims=True)) for x in scores]
        probs = [(x * (1.0 / jnp.sum(x, axis=0, keepdims=True))).astype(BF16) for x in weights]
        broad = [x.astype(F32) for x in probs]
        deltas = [jnp.sum(x * y, axis=0, keepdims=True) for x, y in zip(broad, dprobs)]
        dscores = [(x * (y - z)).astype(BF16) for x, y, z in zip(broad, dprobs, deltas)]
        dqueries = [
            lax.dot_general(x, y, (((0,), (0,)), ((), ())), preferred_element_type=F32) * scale
            for x, y in zip(dscores, keys)
        ]
        dqueries = [
            jnp.concatenate([x[q * block : (q + 1) * block] for q in range(QPK)], 1) for x in dqueries
        ]
        dkeys = [jnp.dot(x, y, preferred_element_type=F32) for x, y in zip(dscores, queries)]
        dvalues = [jnp.dot(x, y, preferred_element_type=F32) for x, y in zip(probs, cots)]
        return dqueries, dkeys, dvalues

    if seq == block:
        arrived = by_group(rows_ref[...], local)
        terms = zip(*step(0, arrived, bias_ref[...]))
        parts = [jnp.concatenate([x, y * scale, z], 1) for x, y, z in terms]
        grads = by_place(parts).astype(BF16)
        if places != sorted(places):
            size = total // len(places)
            grads = jnp.concatenate([grads[n * size : (n + 1) * size] for n in places], 0)
        out_ref[...] = grads
        return
    sums_at[...] = jnp.zeros(sums_at.shape, F32)

    @pl.loop(0, seq // block)
    def _(index):
        first = pl.multiple_of(index * block, block)
        seen = iota((seq, wide), 0) <= first + rest(iota((seq, wide), 1), block)
        bias = jnp.where(seen, bias_ref[:, :1], NEG)
        (dquery,), (dkey,), (dvalue,) = step(first, [rows_ref[...]], bias)
        out_ref[pl.ds(first, block), :qcols] = dquery.astype(BF16)
        sums_at[:, :HD] += dkey
        sums_at[:, HD:] += dvalue

    out_ref[:, qcols : qcols + HD] = (sums_at[:, :HD] * scale).astype(BF16)
    out_ref[:, qcols + HD :] = sums_at[:, HD:].astype(BF16)


def gather_kernel(rows_ref, gather_ref, out_ref, *, part):
    count = out_ref.shape[0]
    pick = gather_ref[part * count : (part + 1) * count, :]
    out_ref[...] = jnp.dot(pick, rows_ref[...], preferred_element_type=F32).astype(BF16)


def finish_kernel(cos_ref, sin_ref, *refs):
    parts, (out_hbm, out_ref, out_sems) = refs[:-3], refs[-3:]
    stores = Stores(out_ref, out_hbm, out_sems)
    for at in stores.pieces():
        cosv, sinv = cos_ref[at, :], sin_ref[at, :]
        for first in range(0, out_ref.shape[1], HD):
            cols = slice(first, first + HD)
            x = sum(ref[at, cols].astype(F32) for ref in parts)
            if first < (QPK + 1) * HD:
                x = x * cosv - pltpu.roll(x, HD // 2, 1) * sinv
            out_ref[at, cols] = x.astype(BF16)
        stores.start(at)
    stores.wait()


def call(kernel, outs, *args, scratch=(), specs=None, out_spec=VMEM):
    shapes = [jax.ShapeDtypeStruct(s, d) for s, d in outs]
    single = len(shapes) == 1
    return pl.pallas_call(
        kernel,
        out_shape=shapes[0] if single else shapes,
        in_specs=specs or [VMEM] * len(args),
        out_specs=out_spec if single else [out_spec] * len(shapes),
        scratch_shapes=list(scratch),
        compiler_params=pltpu.CompilerParams(vmem_limit_bytes=48 * 2**20),
    )(*args)


def body(vision_rows, positions, destination, out_grad):
    tiles = lax.axis_size("tile")
    heads = lax.axis_size("head")
    tokens, groups, width = vision_rows.shape
    local = groups // heads
    count = tokens * groups
    seq = heads * tiles * C
    total = seq * local
    qcols = QPK * HD
    sides = 2 if heads == 2 and tiles % 2 == 0 else 1
    if local > 1 and sides * C != 4:
        raise ValueError("unsupported mesh")
    targets = destination.reshape(-1, LANES)
    rows = vision_rows.reshape(count, width)
    kernel = functools.partial

    def to_pair(x):
        return lax.ppermute(x, "tile", [(t, t ^ 1) for t in range(tiles)])

    others = [to_pair(rows), to_pair(positions)] if sides == 2 else []
    cos_own, sin_own, place = call(
        kernel(ready_kernel, tiles=tiles, local=local, sides=sides),
        [((tokens, HD), F32), ((tokens, HD), F32), ((total, sides * count), BF16)],
        *(pltpu.with_memory_space_constraint(x, pltpu.HBM) for x in (positions, targets)),
        specs=[HBM] * 2,
        scratch=(
            pltpu.VMEM(positions.shape, jnp.int32),
            pltpu.VMEM(targets.shape, jnp.int32),
            pltpu.SemaphoreType.DMA((2,)),
        ),
    )
    slots = out_grad.shape[0]
    cot_rows = out_grad.reshape(slots * groups, qcols)
    split_outs = [((slots * local, qcols), BF16)] * 2
    table_outs = [
        ((count, HD), F32),
        ((count, HD), F32),
        ((sides * count, total), BF16),
        ((seq, seq), BF16),
        ((seq, LANES if seq > BLOCK else QPK * seq), F32),
    ]
    early = []
    if sides == 2:
        early = call(
            kernel(early_kernel, tiles=tiles, heads=heads, local=local, sides=sides),
            split_outs + table_outs,
            *(pltpu.with_memory_space_constraint(x, pltpu.HBM) for x in (cot_rows, positions, targets)),
            specs=[HBM] * 3,
            scratch=(
                pltpu.VMEM(cot_rows.shape, BF16),
                pltpu.VMEM(positions.shape, jnp.int32),
                pltpu.VMEM(targets.shape, jnp.int32),
                pltpu.SemaphoreType.DMA((3,)),
            ),
        )
    outgoing = call(
        pack_kernel,
        [((total, width), BF16)],
        rows,
        cos_own,
        sin_own,
        place,
        early[0][:16, :LANES] if early else place[:16, :LANES],
        *others,
        out_spec=HBM,
        scratch=(
            pltpu.VMEM((sides * count, width), BF16),
            pltpu.VMEM((total, width), BF16),
            pltpu.SemaphoreType.DMA((PIECES,)),
        ),
    )

    def swap(rows, back=False):
        units = tiles // sides
        parts = rows.reshape(heads * units, -1, width)
        if sides == 1:
            axes, groups = ("head", "tile"), None
        else:
            axes, order = ("tile", "head"), unit_order(units, sides, back)
            groups = [
                [(unit * sides + side) * heads + head for head in range(heads) for unit in order]
                for side in range(sides)
            ]
        parts = lax.all_to_all(
            parts, axes, split_axis=0, concat_axis=0, tiled=True, axis_index_groups=groups
        )
        return parts.reshape(total, width)

    incoming = swap(outgoing)
    if sides == 2:
        own, other = call(kernel(split_kernel, local=local, sides=sides), split_outs, cot_rows, *early[:2])
        cots = [own, lax.ppermute(other, "head", [(0, 1), (1, 0)])]
    else:
        moved = lax.all_to_all(out_grad, "head", split_axis=1, concat_axis=0, tiled=True)
        cots = [jnp.swapaxes(moved, 0, 1).reshape(total, qcols)]
    cosv, sinv, gather, pick, bias = call(
        kernel(table_kernel, tiles=tiles, heads=heads, local=local, sides=sides),
        table_outs,
        positions,
        targets,
        outgoing[:16, :LANES],
        *early[2:],
    )
    cot = call(
        kernel(join_kernel, local=local),
        [((total * QPK, HD), BF16)],
        pick,
        *cots,
        scratch=(pltpu.VMEM((total, qcols), BF16),),
    )
    units = tiles // sides
    there, back = (unit_order(units, sides, way) for way in (False, True))
    places = [head * units + there.index(unit) for head in range(heads) for unit in back]
    grads = call(
        kernel(attend_kernel, local=local, places=places),
        [((total, width), BF16)],
        incoming,
        bias,
        cot,
        scratch=(pltpu.VMEM((seq if seq > BLOCK else 8, 2 * HD), F32),),
    )
    returned = swap(grads, True)

    def gathered(part):
        return call(kernel(gather_kernel, part=part), [((count, width), BF16)], returned, gather)

    parts = [to_pair(gathered(1))] if sides == 2 else []
    parts.append(gathered(0))
    result = call(
        finish_kernel,
        [((count, width), BF16)],
        cosv,
        sinv,
        *parts,
        out_spec=HBM,
        scratch=(pltpu.VMEM((count, width), BF16), pltpu.SemaphoreType.DMA((PIECES,))),
    )
    return result.reshape(tokens, groups, width)


def solution(mesh):
    return jax.shard_map(
        body,
        mesh=mesh,
        in_specs=(
            P(("tile", "head"), None, None),
            P(None, ("tile", "head")),
            P(),
            P(("tile", "head"), None, None),
        ),
        out_specs=P(("tile", "head"), None, None),
        check_vma=False,
    )
```
